32 devices in a mesh: rep: 4 (over y, x), wide: 8 (over z, core).
Axes of the slice: x: 2, y: 2, z: 4, core: 2. Of those that a mesh axis runs over, the one named last changes fastest.
Arguments:
- token_ids: int32 [4, 1, 2, 1, 2048], P('rep'), may hold values from 0 to 50303, as said below
- prompt_mask: int32 [4, 1, 2, 1, 2048], P('rep'), may hold values from 0 to 1, as said below
- loss_pos: int32 [4, 1, 2, 8, 16], P('rep'), may hold values from 0 to 254
- tables: float32 [2, 50304, 512], P(None, 'wide', 'rep'), may hold values from -12 to 12
- attention: float32 [2, 2, 512, 512], P(None, None, 'wide', 'rep')
- feedforward: float32 [2, 2, 512, 2048], P(None, None, 'wide', 'rep')
- key_value: float32 [512, 128], P('wide', 'rep'), may hold values from -0.25 to 0.25
- gains_biases: float32 [12416], P('rep')
- first_tables: float32 [4, 2, 50304, 512], P('rep', None, 'wide'), may hold values from -5.8365434e-06 to 5.8365434e-06
- first_attention: float32 [4, 2, 2, 512, 512], P('rep', None, None, 'wide'), may hold values from -2.2888184e-05 to 2.2888184e-05
- first_feedforward: float32 [4, 2, 2, 512, 2048], P('rep', None, None, 'wide'), may hold values from -2.2888184e-05 to 2.2888184e-05
- first_key_value: float32 [4, 512, 128], P('rep', 'wide'), may hold values from -2.2888184e-05 to 2.2888184e-05
- first_gains: float32 [4, 12416], P('rep'), may hold values from -9.1552734e-05 to 9.1552734e-05
- second_tables: float32 [4, 2, 50304, 512], P('rep', None, 'wide'), may hold values from 9.2553283e-14 to 3.69509303e-11
- second_attention: float32 [4, 2, 2, 512, 512], P('rep', None, None, 'wide'), may hold values from 9.255328e-12 to 3.6950932e-11
- second_feedforward: float32 [4, 2, 2, 512, 2048], P('rep', None, None, 'wide'), may hold values from 9.255328e-12 to 3.6950932e-11
- second_key_value: float32 [4, 512, 128], P('rep', 'wide'), may hold values from 9.255328e-12 to 3.6950932e-11
- second_gains: float32 [4, 12416], P('rep'), may hold values from 1.759568e-10 to 7.038272e-10
- outer_tables: float32 [2, 50304, 512], P(None, 'wide', 'rep'), may hold values from -0.3125 to 0.3125
- outer_attention: float32 [2, 2, 512, 512], P(None, None, 'wide', 'rep'), may hold values from -0.3125 to 0.3125
- outer_feedforward: float32 [2, 2, 512, 2048], P(None, None, 'wide', 'rep'), may hold values from -0.3125 to 0.3125
- outer_key_value: float32 [512, 128], P('wide', 'rep'), may hold values from -0.3125 to 0.3125
- outer_gains: float32 [12416], P('rep'), may hold values from -0.3125 to 0.3125
Outputs:
- loss_sum: float32 [4], P('rep')
- loss_count: float32 [4], P('rep')
- new_tables: float32 [2, 50304, 512], P(None, 'wide', 'rep')
- new_attention: float32 [2, 2, 512, 512], P(None, None, 'wide', 'rep')
- new_feedforward: float32 [2, 2, 512, 2048], P(None, None, 'wide', 'rep')
- new_key_value: float32 [512, 128], P('wide', 'rep')
- new_gains: float32 [12416], P('rep')
- next_first_tables: float32 [4, 2, 50304, 512], P('rep', None, 'wide')
- next_first_attention: float32 [4, 2, 2, 512, 512], P('rep', None, None, 'wide')
- next_first_feedforward: float32 [4, 2, 2, 512, 2048], P('rep', None, None, 'wide')
- next_first_key_value: float32 [4, 512, 128], P('rep', 'wide')
- next_first_gains: float32 [4, 12416], P('rep')
- next_second_tables: float32 [4, 2, 50304, 512], P('rep', None, 'wide')
- next_second_attention: float32 [4, 2, 2, 512, 512], P('rep', None, None, 'wide')
- next_second_feedforward: float32 [4, 2, 2, 512, 2048], P('rep', None, None, 'wide')
- next_second_key_value: float32 [4, 512, 128], P('rep', 'wide')
- next_second_gains: float32 [4, 12416], P('rep')
- next_outer_tables: float32 [2, 50304, 512], P(None, 'wide', 'rep')
- next_outer_attention: float32 [2, 2, 512, 512], P(None, None, 'wide', 'rep')
- next_outer_feedforward: float32 [2, 2, 512, 2048], P(None, None, 'wide', 'rep')
- next_outer_key_value: float32 [512, 128], P('wide', 'rep')
- next_outer_gains: float32 [12416], P('rep')
The draws below stay inside these ranges and needn't reach their ends.
Inputs may be any that keep to these rules, and one draw needn't show every extreme that they name: In each sequence prompt_mask is 0 before a prompt length under 2 * 2048 / 3 and 1 from there on. `token_ids`: vocabulary shard q holds the ids q * 6288 to (q + 1) * 6288 - 1. The 256 tokens of one device of wide in a micro-batch (places w * 256 to (w + 1) * 256 - 1 of every sequence) hold at most 64 ids of one shard, and in every micro-batch of a group some shard holds exactly 64 ids of every device's tokens.
All inputs are finite; a program needn't handle non-finite values.
Results may differ from the reference program's by a relative error of at most 0.012.
The reference program's roundings to bfloat16 on the way (of `normed`, `queries`, `pairs` and `context`) count: a program that leaves them out, or rounds other values in their place, can miss the bound.
Values may be sent and summed in bfloat16 or wider, within the bound.
No kernel may reach another device: no remote copies, remote signals or barrier semaphores. Data moves between devices by JAX's collectives and lax.ppermute only.
A program may use at most 448 MiB of HBM per device.

```python
import math
import jax
import jax.numpy as jnp
from jax import lax

D = 512
HEADS = 8
HD = 64
ROT = 16
FF = 2048
VOCAB = 50304
L = 2
LEN = 2048
MICRO = 2
INNER = 1
STEP = 5
TOK_DEV = 256
LROWS = 16
SEQS = 1
ROWS_SEQ = 256
SMALL = 12416
NPARAMS = 56832128
N_REP = 4
N_WIDE = 8


def draw_token_ids(key, part):
    key = jax.random.fold_in(key, 16)
    keys = jax.random.split(key, 5)
    shard_rows = VOCAB // N_WIDE
    blocks = (N_REP, INNER, MICRO, N_WIDE)
    hot = jax.random.randint(keys[0], (N_REP, INNER, MICRO, 1, 1), 0, N_WIDE)
    cold = jax.random.randint(keys[1], blocks + (1,), 0, N_WIDE - 1)
    cold = cold + (cold >= hot).astype(jnp.int32)
    labels = jnp.arange(TOK_DEV, dtype=jnp.int32) % N_WIDE
    labels = jnp.where(labels == cold, hot, labels)
    scores = jax.random.randint(keys[2], blocks + (TOK_DEV,), 0, 65536) * TOK_DEV + jnp.arange(TOK_DEV, dtype=jnp.int32)
    order = jnp.argsort(scores, axis=-1, stable=True)
    labels = jnp.take_along_axis(labels, order, axis=-1)
    depth = jax.random.randint(keys[3], blocks + (TOK_DEV,), 0, 9)
    limit = jnp.maximum(jnp.right_shift(jnp.full(depth.shape, shard_rows, jnp.int32), depth), 1)
    within = jax.random.randint(keys[4], blocks + (TOK_DEV,), 0, limit)
    ids = labels * shard_rows + within
    ids = ids.reshape(N_REP, INNER, MICRO, N_WIDE, SEQS, ROWS_SEQ).transpose(0, 1, 2, 4, 3, 5)
    return ids.reshape(N_REP, INNER, MICRO, SEQS, LEN)


def draw_prompt_mask(key, part):
    key = jax.random.fold_in(key, 11)
    lengths = jax.random.randint(key, (N_REP, INNER, MICRO, SEQS, 1), 0, 2 * LEN // 3)
    places = jnp.arange(LEN, dtype=jnp.int32)
    return (places >= lengths).astype(jnp.int32)


def draw_tables(key, part):
    key = jax.random.fold_in(key, 12)
    noise = jax.random.normal(key, (2, VOCAB, D), jnp.float32)
    upper = 3.0
    rising = 1.0 + (upper - 1.0) * jnp.arange(VOCAB, dtype=jnp.float32) / VOCAB
    return jnp.stack([0.02 * noise[0], noise[1] * rising[:, None] / math.sqrt(D)])


def draw_attention(key, part):
    key = jax.random.fold_in(key, 13)
    noise = jax.random.normal(key, (L, 2, D, D), jnp.float32)
    scales = jnp.array([1.0 / math.sqrt(D), math.sqrt(LEN / (4.0 * D))], jnp.float32)
    return noise * scales[None, :, None, None]


def draw_feedforward(key, part):
    key = jax.random.fold_in(key, 14)
    noise = jax.random.normal(key, (L, 2, D, FF), jnp.float32)
    scales = jnp.array([1.0 / math.sqrt(D), 1.0 / math.sqrt(FF)], jnp.float32)
    return noise * scales[None, :, None, None]


def draw_gains_biases(key, part):
    key = jax.random.fold_in(key, 15)
    noise = jax.random.normal(key, (SMALL,), jnp.float32)
    ramp = 0.5 + jnp.arange(D, dtype=jnp.float32) / D
    span = 7 * D + FF
    pieces = []
    for layer_number in range(L):
        segment = noise[layer_number * span:(layer_number + 1) * span]
        pieces.append(ramp * (1.0 + 0.1 * segment[0:D]))
        pieces.append(0.2 * segment[D:2 * D])
        pieces.append(ramp * (1.0 + 0.1 * segment[2 * D:3 * D]))
        pieces.append(0.2 * segment[3 * D:])
    remain = noise[L * span:]
    pieces.append(0.2 * remain[:2 * HD])
    pieces.append(ramp * (1.0 + 0.1 * remain[2 * HD:2 * HD + D]))
    pieces.append(0.2 * remain[2 * HD + D:])
    return jnp.concatenate(pieces)


def draw_first_tables(key, part):
    key = jax.random.fold_in(key, 17)
    noise = jnp.clip(jax.random.normal(key, (N_REP, 2, VOCAB, D), jnp.float32), -4.0, 4.0)
    factor = jnp.array([0.1, 1.0], jnp.float32)
    return noise * factor[None, :, None, None] * (0.011 / math.sqrt(NPARAMS))


def draw_second_tables(key, part):
    key = jax.random.fold_in(key, 18)
    spread = jax.random.uniform(key, (N_REP, 2, VOCAB, D), jnp.float32, math.log(0.000526), math.log(0.0021))
    factor = jnp.array([0.01, 1.0], jnp.float32)
    return jnp.exp(spread) * factor[None, :, None, None] / NPARAMS


def touch_ends(result, key, least, high):
    index_at = [jax.random.randint(jax.random.fold_in(key, axis), (), 0, length) for axis, length in enumerate(result.shape)]
    widest = result.shape.index(max(result.shape))
    neighbour = index_at[:widest] + [(index_at[widest] + 1) % result.shape[widest]] + index_at[widest + 1:]
    return result.at[tuple(index_at)].set(least).at[tuple(neighbour)].set(high)


def block_levels(rng, dims, cuts, low, largest):
    def one(dim, blocks):
        heights = jax.random.uniform(jax.random.fold_in(jax.random.fold_in(rng, 6), dim), (blocks,), jnp.float32, low / len(cuts), largest / len(cuts))
        return jnp.repeat(jnp.exp(heights), dims[dim] // blocks).reshape((-1,) + (1,) * (len(dims) - dim - 1))

    level = one(*cuts[0])
    for cut in cuts[1:]:
        level = level * one(*cut)
    return level


def normal_values(own_key, dims, scale, most, cuts=(), kind=jnp.bfloat16):
    entries = jax.random.normal(own_key, dims, jnp.float32) * scale
    if len(cuts) > 0:
        entries = block_levels(own_key, dims, cuts, -0.22, 0.18) * entries
    return jnp.clip(entries, min=-most, max=most).astype(kind)


def setup_inputs(seed: int = 0) -> dict:
    streams_of = jax.random.split(jax.random.key(seed), 24)
    return {
        "token_ids": draw_token_ids(jax.random.fold_in(streams_of[23], 71), 0),
        "prompt_mask": draw_prompt_mask(jax.random.fold_in(streams_of[23], 71), 0),
        "loss_pos": touch_ends(jax.random.randint(streams_of[2], (N_REP, INNER, MICRO, N_WIDE, LROWS), 0, SEQS * (ROWS_SEQ - 1)), jax.random.fold_in(streams_of[2], 1), 0, (SEQS * (ROWS_SEQ - 1)) - 1).astype(jnp.int32),
        "tables": draw_tables(jax.random.fold_in(streams_of[23], 71), 0),
        "attention": draw_attention(jax.random.fold_in(streams_of[23], 71), 0),
        "feedforward": draw_feedforward(jax.random.fold_in(streams_of[23], 71), 0),
        "key_value": normal_values(streams_of[6], (D, 2 * HD), D ** -0.5, 0.25, ((0, 8), (1, 4)), jnp.float32),
        "gains_biases": draw_gains_biases(jax.random.fold_in(streams_of[23], 71), 0),
        "first_tables": draw_first_tables(jax.random.fold_in(streams_of[23], 71), 0),
        "first_attention": normal_values(streams_of[9], (N_REP, L, 2, D, D), (0.011 / NPARAMS ** 0.5), 2.288818359375e-05, ((0, 4), (3, 8)), jnp.float32),
        "first_feedforward": normal_values(streams_of[10], (N_REP, L, 2, D, FF), (0.011 / NPARAMS ** 0.5), 2.288818359375e-05, ((0, 4), (3, 8)), jnp.float32),
        "first_key_value": normal_values(streams_of[11], (N_REP, D, 2 * HD), (0.011 / NPARAMS ** 0.5), 2.288818359375e-05, ((0, 4), (1, 8)), jnp.float32),
        "first_gains": normal_values(streams_of[12], (N_REP, SMALL), (0.05 / NPARAMS ** 0.5), 9.1552734375e-05, ((0, 4),), jnp.float32),
        "second_tables": draw_second_tables(jax.random.fold_in(streams_of[23], 71), 0),
        "second_attention": jnp.clip(jnp.exp(math.log(3.6950931897594685e-11) - 1.38439145 * jax.random.uniform(streams_of[14], (N_REP, L, 2, D, D), jnp.float32) ** block_levels(streams_of[14], (N_REP, L, 2, D, D), ((0, 4), (3, 8)), -0.2, 0.2)), 9.255328274615504e-12, 3.6950931897594685e-11),
        "second_feedforward": jnp.clip(jnp.exp(math.log(3.6950931897594685e-11) - 1.38439145 * jax.random.uniform(streams_of[15], (N_REP, L, 2, D, FF), jnp.float32) ** block_levels(streams_of[15], (N_REP, L, 2, D, FF), ((0, 4), (3, 8)), -0.2, 0.2)), 9.255328274615504e-12, 3.6950931897594685e-11),
        "second_key_value": jnp.clip(jnp.exp(math.log(3.6950931897594685e-11) - 1.38439145 * jax.random.uniform(streams_of[16], (N_REP, D, 2 * HD), jnp.float32) ** block_levels(streams_of[16], (N_REP, D, 2 * HD), ((0, 4), (1, 8)), -0.2, 0.2)), 9.255328274615504e-12, 3.6950931897594685e-11),
        "second_gains": jnp.clip(jnp.exp(math.log(7.038272187287475e-10) - 1.3862944 * jax.random.uniform(streams_of[17], (N_REP, SMALL), jnp.float32) ** block_levels(streams_of[17], (N_REP, SMALL), ((0, 4),), -0.2, 0.2)), 1.7595680468218688e-10, 7.038272187287475e-10),
        "outer_tables": normal_values(streams_of[18], (2, VOCAB, D), 0.02, 0.3125, ((1, 8), (2, 4)), jnp.float32),
        "outer_attention": normal_values(streams_of[19], (L, 2, D, D), 0.02, 0.3125, ((2, 8), (3, 4)), jnp.float32),
        "outer_feedforward": normal_values(streams_of[20], (L, 2, D, FF), 0.02, 0.3125, ((2, 8), (3, 4)), jnp.float32),
        "outer_key_value": normal_values(streams_of[21], (D, 2 * HD), 0.02, 0.3125, ((0, 8), (1, 4)), jnp.float32),
        "outer_gains": normal_values(streams_of[22], (SMALL,), 0.02, 0.3125, ((0, 4),), jnp.float32),
    }


NORM_EPSILON = 1e-05
CLIP = 0.1
LEARN_RATES = (0.02, 0.2, 0.02, 0.02, 0.2)
BETA_ONE = 0.9
BETA_TWO = 0.95
ADAM_EPSILON = 1e-08
DECAY = 0.1
OUTER_RATE = 0.7
OUTER_MOMENTUM = 0.9
HIGHEST = lax.Precision.HIGHEST

@jax.custom_vjp
def low(v):
    return lax.optimization_barrier(v.astype(jnp.bfloat16)).astype(jnp.float32)

@jax.custom_vjp
def low_back(v):
    return v

def low_keep(v):
    return (low(v), None)

def low_pass(kept, grad):
    return (grad,)

def back_keep(v):
    return (v, None)

def back_low(kept, grad):
    return (low(grad),)
low.defvjp(low_keep, low_pass)
low_back.defvjp(back_keep, back_low)

def product(left, right):
    return jnp.dot(left, right, precision=HIGHEST, preferred_element_type=jnp.float32)

def layer_norm(stream, gain, bias):
    centred = stream - lax.optimization_barrier(jnp.mean(stream, axis=-1, keepdims=True))
    return centred * lax.rsqrt(lax.optimization_barrier(jnp.mean(centred * centred, axis=-1, keepdims=True)) + NORM_EPSILON) * gain + bias

def rotary_tables(places):
    frequency = 10000.0 ** (-2.0 * jnp.arange(ROT // 2, dtype=jnp.float32) / ROT)
    angles = places[:, None] * frequency[None, :]
    return (jnp.cos(angles), jnp.sin(angles))

def rotate(values, cosine_table, sine_table):
    half_dim = ROT // 2
    leading = values[..., :half_dim]
    trailing = values[..., half_dim:ROT]
    cosine = cosine_table[:, None, :]
    sine_part = sine_table[:, None, :]
    return jnp.concatenate([leading * cosine - trailing * sine_part, trailing * cosine + leading * sine_part, values[..., ROT:]], axis=-1)

def unpack_small(gains_biases):
    span = 7 * D + FF
    layers = gains_biases[:L * span].reshape(L, span)
    remain = gains_biases[L * span:]
    return (layers, remain[:2 * HD], remain[2 * HD:2 * HD + D], remain[2 * HD + D:])

def attend_one(inputs):
    queries, pairs = inputs
    scores = low_back(jnp.einsum('qhd,kd->hqk', queries, pairs[:, :HD], precision=HIGHEST) * 0.125)
    places = jnp.arange(LEN)
    scores = jnp.where((places[:, None] >= places[None, :])[None], scores, -1e+30)
    weights = jax.nn.softmax(scores, axis=-1)
    return jnp.einsum('hqk,kd->qhd', low(weights), pairs[:, HD:], precision=HIGHEST)

def loss_rows(loss_now):
    seq_index = loss_now // (ROWS_SEQ - 1)
    place_index = jnp.arange(N_WIDE, dtype=jnp.int32)[:, None] * ROWS_SEQ + loss_now % (ROWS_SEQ - 1)
    return (seq_index.reshape(-1), place_index.reshape(-1))

def forward_micro(values, ids_now, mask_now, loss_now):
    tables, attention, feedforward, key_value, gains_biases = values
    layers, pair_bias, final_gain, final_bias = unpack_small(gains_biases)
    table_low = low(tables)
    stream = table_low[0][ids_now.reshape(-1)]
    cosine_table, sine_table = rotary_tables(jnp.tile(jnp.arange(LEN, dtype=jnp.float32), SEQS))
    pairs = None
    for layer_number in range(L):
        vectors = layers[layer_number]
        normed = low(layer_norm(stream, vectors[0:D], vectors[D:2 * D]))
        feed_input = low(layer_norm(stream, vectors[2 * D:3 * D], vectors[3 * D:4 * D]))
        queries = low_back(product(normed, low(attention[layer_number, 0])) + vectors[4 * D:5 * D])
        queries = low_back(low(rotate(queries.reshape(-1, HEADS, HD), cosine_table, sine_table)))
        if pairs is None:
            projected = low_back(product(normed, low(key_value)) + pair_bias)
            turned = rotate(projected[:, None, :HD], cosine_table, sine_table)[:, 0]
            pairs = low_back(low(jnp.concatenate([turned, projected[:, HD:]], axis=1)))
        context = lax.map(jax.checkpoint(attend_one), (queries.reshape(SEQS, LEN, HEADS, HD), pairs.reshape(SEQS, LEN, 2 * HD)))
        context = low_back(low(context.reshape(SEQS * LEN, D)))
        branch = low_back(product(context, low(attention[layer_number, 1])) + vectors[5 * D:6 * D])
        hidden = low_back(product(feed_input, low(feedforward[layer_number, 0])) + vectors[7 * D:])
        active = low(jax.nn.gelu(hidden, approximate=False))
        output = low_back(product(active, low(feedforward[layer_number, 1]).T) + vectors[6 * D:7 * D])
        stream = stream + branch + output
    final_norm = layer_norm(stream, final_gain, final_bias)
    seq_index, place_index = loss_rows(loss_now)
    picked = low(final_norm[seq_index * LEN + place_index])
    logits = low_back(product(picked, table_low[1].T))
    targets = ids_now[seq_index, place_index + 1]
    weight = mask_now[seq_index, place_index + 1].astype(jnp.float32)
    chosen = jnp.take_along_axis(logits, targets[:, None], axis=1)[:, 0]
    return jnp.sum(weight * (jax.scipy.special.logsumexp(logits, axis=1) - chosen))

def adam_update(weight, gradient, moment_one, moment_two, clip_factor, step_number, rate):
    gradient = gradient * clip_factor
    moment_one = BETA_ONE * moment_one + (1.0 - BETA_ONE) * gradient
    moment_two = BETA_TWO * moment_two + (1.0 - BETA_TWO) * gradient * gradient
    first_hat = moment_one / (1.0 - BETA_ONE ** step_number)
    second_hat = moment_two / (1.0 - BETA_TWO ** step_number)
    weight = weight - rate * (first_hat / (jnp.sqrt(second_hat) + ADAM_EPSILON) + DECAY * weight)
    return (weight, moment_one, moment_two)

def reference(token_ids, prompt_mask, loss_pos, tables, attention, feedforward, key_value, gains_biases, first_tables, first_attention, first_feedforward, first_key_value, first_gains, second_tables, second_attention, second_feedforward, second_key_value, second_gains, outer_tables, outer_attention, outer_feedforward, outer_key_value, outer_gains):
    masters = (tables, attention, feedforward, key_value, gains_biases)
    firsts_in = (first_tables, first_attention, first_feedforward, first_key_value, first_gains)
    seconds_in = (second_tables, second_attention, second_feedforward, second_key_value, second_gains)
    outers = (outer_tables, outer_attention, outer_feedforward, outer_key_value, outer_gains)
    summed = [jnp.zeros_like(piece) for piece in masters]
    loss_sums = []
    loss_counts = []
    firsts_out = [[] for index in range(5)]
    seconds_out = [[] for index in range(5)]
    for group_index in range(N_REP):
        current = list(masters)
        moment_one = [piece[group_index] for piece in firsts_in]
        moment_two = [piece[group_index] for piece in seconds_in]
        loss_total = jnp.zeros((), jnp.float32)
        count_total = jnp.zeros((), jnp.float32)
        for step_index in range(INNER):
            ids_step = token_ids[group_index, step_index]
            mask_step = prompt_mask[group_index, step_index]
            loss_step = loss_pos[group_index, step_index]
            count = jnp.zeros((), jnp.float32)
            for micro_index in range(MICRO):
                seq_index, place_index = loss_rows(loss_step[micro_index])
                count = count + jnp.sum(mask_step[micro_index][seq_index, place_index + 1].astype(jnp.float32))
            denominator = count

            def objective(*values):
                total = forward_micro(values, ids_step[0], mask_step[0], loss_step[0])
                for micro_index in range(1, MICRO):
                    total = total + forward_micro(values, ids_step[micro_index], mask_step[micro_index], loss_step[micro_index])
                return (total / denominator, total)
            value_now, pull, total = jax.vjp(objective, *current, has_aux=True)
            gradients = pull(jnp.ones_like(value_now))
            squares = jnp.sum(gradients[0] * gradients[0])
            for piece in gradients[1:]:
                squares = squares + jnp.sum(piece * piece)
            clip_factor = jnp.minimum(1.0, CLIP / (jnp.sqrt(squares) + 1e-06))
            for index in range(5):
                current[index], moment_one[index], moment_two[index] = adam_update(current[index], gradients[index], moment_one[index], moment_two[index], clip_factor, STEP + step_index, LEARN_RATES[index])
            loss_total = loss_total + total
            count_total = count_total + count
        for index in range(5):
            summed[index] = summed[index] + (masters[index] - current[index])
            firsts_out[index].append(moment_one[index])
            seconds_out[index].append(moment_two[index])
        loss_sums.append(loss_total)
        loss_counts.append(count_total)
    new_masters = []
    new_outers = []
    for index in range(5):
        mean_diff = summed[index] / N_REP
        momentum = OUTER_MOMENTUM * outers[index] + mean_diff
        new_outers.append(momentum)
        new_masters.append(masters[index] - OUTER_RATE * (mean_diff + OUTER_MOMENTUM * momentum))
    stacked_one = [jnp.stack(piece) for piece in firsts_out]
    stacked_two = [jnp.stack(piece) for piece in seconds_out]
    return (jnp.stack(loss_sums), jnp.stack(loss_counts), new_masters[0], new_masters[1], new_masters[2], new_masters[3], new_masters[4], stacked_one[0], stacked_one[1], stacked_one[2], stacked_one[3], stacked_one[4], stacked_two[0], stacked_two[1], stacked_two[2], stacked_two[3], stacked_two[4], new_outers[0], new_outers[1], new_outers[2], new_outers[3], new_outers[4])
```

```python
from functools import partial

import jax
import jax.numpy as jnp
from jax import lax
from jax.sharding import PartitionSpec as P

D = 512
HEADS = 8
HD = 64
ROT = 16
FF = 2048
L = 2
LEN = 2048
MICRO = 2
STEP = 5

NORM_EPSILON = 1e-05
CLIP = 0.1
LEARN_RATES = (0.02, 0.2, 0.02, 0.02, 0.2)
BETA_ONE = 0.9
BETA_TWO = 0.95
ADAM_EPSILON = 1e-08
DECAY = 0.1
OUTER_RATE = 0.7
OUTER_MOMENTUM = 0.9
FIX_ONE = 1.0 / (1.0 - BETA_ONE**STEP)
FIX_TWO = 1.0 / (1.0 - BETA_TWO**STEP)

BF = jnp.bfloat16
F4 = jnp.float32


def dot(left, right, dims):
    return lax.dot_general(left, right, (dims, ((), ())), preferred_element_type=F4)


def normal_of(stream):
    centred = stream - jnp.mean(stream, axis=-1, keepdims=True)
    scale = lax.rsqrt(jnp.mean(centred * centred, axis=-1, keepdims=True) + NORM_EPSILON)
    return centred * scale, scale


def norm_pull(shaped, normal, scale):
    return scale * (
        shaped
        - jnp.mean(shaped, axis=-1, keepdims=True)
        - normal * jnp.mean(shaped * normal, axis=-1, keepdims=True)
    )


def rotary(places):
    frequency = 10000.0 ** (-2.0 * jnp.arange(ROT // 2, dtype=F4) / ROT)
    angles = places.astype(F4)[:, None] * frequency[None, :]
    return jnp.cos(angles), jnp.sin(angles)


def rotate(values, cosine, sine):
    half = ROT // 2
    a = values[..., :half]
    b = values[..., half:ROT]
    c = cosine[:, None, :]
    s = sine[:, None, :]
    return jnp.concatenate([a * c - b * s, b * c + a * s, values[..., ROT:]], axis=-1)


def unpack_small(gains_biases):
    span = 7 * D + FF
    layers = gains_biases[: L * span].reshape(L, span)
    remain = gains_biases[L * span :]
    return layers, remain[: 2 * HD], remain[2 * HD : 2 * HD + D], remain[2 * HD + D :]


def moments_step(gradient, one, two):
    one = BETA_ONE * one + (1.0 - BETA_ONE) * gradient
    two = BETA_TWO * two + (1.0 - BETA_TWO) * gradient * gradient
    return one, two, (one * FIX_ONE) / (jnp.sqrt(two * FIX_TWO) + ADAM_EPSILON)


def attend_forward(queries, keys, values, allowed):
    def head(query):
        scores = jnp.einsum("mnd,mkd->mnk", query, keys, preferred_element_type=F4) * 0.125
        scores = jnp.where(allowed, scores, -1e30)
        top = jnp.max(scores, axis=2, keepdims=True)
        expo = jnp.exp(scores - top)
        total = jnp.sum(expo, axis=2, keepdims=True)
        probs = (expo / total).astype(BF)
        context = jnp.einsum("mnk,mkd->mnd", probs, values, preferred_element_type=F4)
        return context.astype(BF), top + jnp.log(total)

    context, log_total = lax.map(head, queries.transpose(2, 0, 1, 3))
    return context.transpose(1, 2, 0, 3), log_total


def attend_backward(queries, keys, values, allowed, log_total, grad_context):
    def head(so_far, inputs):
        query, logs, grad = inputs
        scores = jnp.einsum("mnd,mkd->mnk", query, keys, preferred_element_type=F4) * 0.125
        scores = jnp.where(allowed, scores, -1e30)
        probs = jnp.exp(scores - logs)
        grad_probs = jnp.einsum("mnd,mkd->mnk", grad, values, preferred_element_type=F4)
        inner = jnp.sum(probs * grad_probs, axis=2, keepdims=True)
        grad_scores = (probs * (grad_probs - inner)).astype(BF)
        grad_query = jnp.einsum("mnk,mkd->mnd", grad_scores, keys, preferred_element_type=F4)
        grad_keys = jnp.einsum("mnk,mnd->mkd", grad_scores, query, preferred_element_type=F4)
        grad_values = jnp.einsum(
            "mnk,mnd->mkd", probs.astype(BF), grad, preferred_element_type=F4
        )
        both = jnp.concatenate([grad_keys * 0.125, grad_values], axis=-1)
        return so_far + both, (grad_query * 0.125).astype(BF)

    start = jnp.zeros(keys.shape[:2] + (2 * HD,), F4)
    total, grad_queries = lax.scan(
        head, start, (queries.transpose(2, 0, 1, 3), log_total, grad_context.transpose(2, 0, 1, 3))
    )
    return grad_queries.transpose(1, 2, 0, 3), total


def body(
    token_ids,
    prompt_mask,
    loss_pos,
    tables,
    attention,
    feedforward,
    key_value,
    gains_biases,
    first_tables,
    first_attention,
    first_feedforward,
    first_key_value,
    first_gains,
    second_tables,
    second_attention,
    second_feedforward,
    second_key_value,
    second_gains,
    outer_tables,
    outer_attention,
    outer_feedforward,
    outer_key_value,
    outer_gains,
):
    width = lax.axis_size("wide")
    reps = lax.axis_size("rep")
    w = lax.axis_index("wide")
    seqs = token_ids.shape[3]
    rows_seq = LEN // width
    block = seqs * rows_seq
    cap = 2 * block // width
    vr = tables.shape[1]
    lrows = loss_pos.shape[4]
    n_loss = MICRO * width * lrows
    n_slots = MICRO * width * cap
    swap = [(i, i ^ 1) for i in range(width)]

    base_one = BETA_ONE * first_tables[0, 0]
    base_two = BETA_TWO * second_tables[0, 0]
    base_step = (base_one * FIX_ONE) / (jnp.sqrt(base_two * FIX_TWO) + ADAM_EPSILON)
    base_sum = lax.psum_scatter(
        base_step.astype(BF).reshape(vr, reps, D // reps).transpose(1, 0, 2),
        "rep",
        scatter_dimension=0,
        tiled=True,
    )[0]

    att_low = lax.all_gather(attention.astype(BF), "rep", axis=0)
    ff_low = lax.all_gather(feedforward.astype(BF), "rep", axis=0)
    kv_low = lax.all_gather(key_value.astype(BF), "rep", axis=1, tiled=True)
    att_low = lax.all_gather(att_low, "wide", axis=3, tiled=True)
    ff_low = lax.all_gather(ff_low, "wide", axis=3, tiled=True)
    kv_low = lax.all_gather(kv_low, "wide", axis=0, tiled=True)
    att_low = att_low.transpose(1, 2, 3, 0, 4).reshape(L, 2, D, D)
    ff_low = ff_low.transpose(1, 2, 3, 0, 4).reshape(L, 2, D, FF)
    unembed = lax.all_gather(tables[1].astype(BF), "rep", axis=1, tiled=True)
    small = lax.all_gather(gains_biases, "rep", axis=0, tiled=True)
    vectors, pair_bias, final_gain, final_bias = unpack_small(small)

    tokens_all = lax.all_gather(token_ids[0, 0], "rep")
    ordered_all = tokens_all.reshape(reps, MICRO, seqs, width, rows_seq).transpose(0, 1, 3, 2, 4)
    ordered_all = ordered_all.reshape(reps, MICRO, width, block)
    lower = (jnp.arange(block)[:, None] <= jnp.arange(block)[None, :]).astype(BF)

    def slots_of(labels_hit, payload):
        rank = jnp.einsum("...t,ts->...s", labels_hit.astype(BF), lower, preferred_element_type=F4)
        rank = rank.astype(jnp.int32) - 1
        hot = labels_hit[..., None] & (rank[..., None] == jnp.arange(cap, dtype=jnp.int32))
        valid = rank[..., -1:] >= jnp.arange(cap, dtype=jnp.int32)
        return jnp.sum(jnp.where(hot, payload[..., None], 0), axis=-2), valid

    local_all = ordered_all - w * vr
    slot_ids, slot_valid = slots_of((local_all >= 0) & (local_all < vr), local_all)
    slot_ids = slot_ids.reshape(reps, n_slots)
    slot_valid = slot_valid.reshape(reps, n_slots)

    mine_ordered = lax.dynamic_index_in_dim(ordered_all, lax.axis_index("rep"), 0, False)
    place_codes = (
        jnp.arange(seqs, dtype=jnp.int32)[None, :, None] * LEN
        + jnp.arange(width, dtype=jnp.int32)[:, None, None] * rows_seq
        + jnp.arange(rows_seq, dtype=jnp.int32)[None, None, :]
    ).reshape(width, block)
    shard_hit = (mine_ordered // vr)[None] == jnp.arange(width, dtype=jnp.int32)[
        :, None, None, None
    ]
    key_codes, key_valid = slots_of(
        shard_hit, jnp.broadcast_to(place_codes[None, None], shard_hit.shape)
    )
    key_codes = jnp.where(key_valid, key_codes, seqs * LEN)
    own_codes = lax.dynamic_index_in_dim(key_codes, w, 0, False)
    key_codes = key_codes.transpose(1, 0, 2, 3).reshape(MICRO, width * width * cap)

    rows = jnp.take(tables[0], slot_ids.reshape(-1), axis=0).astype(BF)
    rows = rows.reshape(reps, n_slots, D // reps)
    rows = lax.all_to_all(rows, "rep", 0, 0, tiled=True)
    rows = rows.transpose(1, 0, 2).reshape(n_slots, D)

    slot_normal, slot_scale = normal_of(rows.astype(F4))
    gain0, bias0 = vectors[0, :D], vectors[0, D : 2 * D]
    slot_normed = (slot_normal * gain0 + bias0).astype(BF)
    projected = dot(slot_normed, kv_low, ((1,), (0,))) + pair_bias
    slot_cos, slot_sin = rotary(own_codes.reshape(-1) % LEN)
    turned = rotate(projected[:, None, :HD], slot_cos, slot_sin)[:, 0]
    pairs = jnp.concatenate([turned, projected[:, HD:]], axis=1).astype(BF)
    pairs_all = lax.all_gather(pairs.reshape(MICRO, width * cap, 2 * HD), "wide", axis=1)
    pairs_all = pairs_all.reshape(MICRO, width * width * cap, 2 * HD)
    keys, values = pairs_all[..., :HD], pairs_all[..., HD:]

    codes = loss_pos[0, 0]
    row_seq = codes // (rows_seq - 1)
    row_place = jnp.arange(width, dtype=jnp.int32)[:, None] * rows_seq + codes % (rows_seq - 1)
    row_code = (row_seq * LEN + row_place).reshape(MICRO, width * lrows)
    row_pos = row_place.reshape(-1)
    flat_tokens = token_ids[0, 0].reshape(MICRO, seqs * LEN)
    flat_mask = prompt_mask[0, 0].reshape(MICRO, seqs * LEN)
    targets = jnp.take_along_axis(flat_tokens, row_code + 1, axis=1).reshape(-1)
    weight = jnp.take_along_axis(flat_mask, row_code + 1, axis=1).reshape(-1).astype(F4)
    count = jnp.sum(weight)
    own_micro = own_codes.reshape(MICRO, width * cap)
    pick = jnp.concatenate(
        [
            jnp.concatenate(
                [
                    (row_code[m][:, None] == own_micro[n][None, :])
                    if m == n
                    else jnp.zeros((width * lrows, width * cap), bool)
                    for n in range(MICRO)
                ],
                axis=1,
            )
            for m in range(MICRO)
        ],
        axis=0,
    ).astype(BF)
    picked_rows = dot(pick, rows, ((1,), (0,)))
    stream = lax.psum(picked_rows, "wide")

    allowed = (key_codes[:, None, :] <= row_code[:, :, None]) & (
        key_codes[:, None, :] >= (row_code // LEN * LEN)[:, :, None]
    )
    row_cos, row_sin = rotary(row_pos)
    parity = w % 2
    half = D // 2

    def half_of(array):
        return lax.dynamic_slice_in_dim(array, parity * half, half, axis=1)

    def join(part):
        other = lax.ppermute(part, "wide", swap)
        low_part = jnp.where(parity == 0, part, other)
        high_part = jnp.where(parity == 0, other, part)
        return jnp.concatenate([low_part, high_part], axis=1)

    def heads_of(array):
        return half_of(array).reshape(MICRO, width * lrows, HEADS // 2, HD)

    kept = []
    for k in range(L):
        vec = vectors[k]
        normal, scale = normal_of(stream)
        normed = (normal * vec[:D] + vec[D : 2 * D]).astype(BF)
        feed = (normal * vec[2 * D : 3 * D] + vec[3 * D : 4 * D]).astype(BF)
        query = dot(normed, att_low[k, 0], ((1,), (0,))) + vec[4 * D : 5 * D]
        query = rotate(query.reshape(-1, HEADS, HD), row_cos, row_sin).astype(BF).reshape(-1, D)
        query = heads_of(query)
        context, log_total = attend_forward(query, keys, values, allowed)
        context = join(context.reshape(n_loss, half))
        branch = dot(context, att_low[k, 1], ((1,), (0,))) + vec[5 * D : 6 * D]
        hidden = dot(feed, ff_low[k, 0], ((1,), (0,))) + vec[7 * D :]
        active = jax.nn.gelu(hidden, approximate=False).astype(BF)
        output = dot(active, ff_low[k, 1], ((1,), (1,))) + vec[6 * D : 7 * D]
        kept.append((normal, scale, normed, feed, query, log_total, context, hidden, active))
        stream = stream + branch + output

    final_normal, final_scale = normal_of(stream)
    picked = (final_normal * final_gain + final_bias).astype(BF)
    logits = dot(picked, unembed, ((1,), (1,)))
    hits = jnp.arange(vr, dtype=jnp.int32)[None, :] == (targets - w * vr)[:, None]
    target_part = jnp.sum(jnp.where(hits, logits, 0.0), axis=1)
    top_part = jnp.max(logits, axis=1)
    total_part = jnp.sum(jnp.exp(logits - top_part[:, None]), axis=1)
    stats = lax.all_gather(jnp.stack([top_part, total_part, target_part]), "wide")
    top = jnp.max(stats[:, 0], axis=0)
    total = jnp.sum(stats[:, 1] * jnp.exp(stats[:, 0] - top), axis=0)
    log_all = top + jnp.log(total)
    loss_sum = jnp.sum(weight * (log_all - jnp.sum(stats[:, 2], axis=0)))
    grad_logits = (jnp.exp(logits - log_all[:, None]) - hits.astype(F4)) * (weight / count)[:, None]
    grad_logits = grad_logits.astype(BF)
    grad_picked = lax.psum(dot(grad_logits, unembed, ((1,), (0,))), "wide")
    grad_unembed = dot(grad_logits, picked, ((0,), (0,)))

    grad_final_gain = jnp.sum(grad_picked * final_normal, axis=0)
    grad_final_bias = jnp.sum(grad_picked, axis=0)
    grad_stream = norm_pull(grad_picked * final_gain, final_normal, final_scale)
    own_rows = D // width

    def own_of(array):
        return lax.dynamic_slice_in_dim(array, w * own_rows, own_rows, axis=1)

    grad_pairs = 0.0
    grad_vectors = [None] * L
    grad_weights = [None] * L
    for k in reversed(range(L)):
        vec = vectors[k]
        normal, scale, normed, feed, query, log_total, context, hidden, active = kept[k]
        grad_low = grad_stream.astype(BF)
        grad_bias_out = jnp.sum(grad_low, axis=0, dtype=F4)
        grad_down = dot(own_of(grad_low), active, ((0,), (0,)))
        grad_active = dot(grad_low, ff_low[k, 1], ((1,), (0,)))
        unused, pull = jax.vjp(partial(jax.nn.gelu, approximate=False), hidden)
        grad_hidden = pull(grad_active)[0].astype(BF)
        grad_bias_up = jnp.sum(grad_hidden, axis=0, dtype=F4)
        grad_up = dot(own_of(feed), grad_hidden, ((0,), (0,)))
        grad_feed = dot(grad_hidden, ff_low[k, 0], ((1,), (1,)))
        grad_out = dot(own_of(context), grad_low, ((0,), (0,)))
        grad_context = dot(grad_low, att_low[k, 1], ((1,), (1,))).astype(BF)
        grad_query, pairs_part = attend_backward(
            query, keys, values, allowed, log_total, heads_of(grad_context)
        )
        grad_pairs = grad_pairs + pairs_part
        grad_query = join(grad_query.reshape(n_loss, half))
        grad_query = rotate(grad_query.astype(F4).reshape(-1, HEADS, HD), row_cos, -row_sin)
        grad_query = grad_query.reshape(-1, D).astype(BF)
        grad_wq = dot(own_of(normed), grad_query, ((0,), (0,)))
        grad_normed = dot(grad_query, att_low[k, 0], ((1,), (1,)))
        grad_vectors[k] = jnp.concatenate(
            [
                jnp.sum(grad_normed * normal, axis=0),
                jnp.sum(grad_normed, axis=0),
                jnp.sum(grad_feed * normal, axis=0),
                jnp.sum(grad_feed, axis=0),
                jnp.sum(grad_query, axis=0, dtype=F4),
                grad_bias_out,
                grad_bias_out,
                grad_bias_up,
            ]
        )
        grad_weights[k] = (grad_wq, grad_out, grad_up, grad_down)
        shaped = grad_normed * vec[:D] + grad_feed * vec[2 * D : 3 * D]
        grad_stream = grad_stream + norm_pull(shaped, normal, scale)

    partial_pairs = grad_pairs.reshape(MICRO, width, width * cap, 2 * HD)
    own_part = lax.dynamic_index_in_dim(partial_pairs, w, 1, False)
    other_part = lax.dynamic_index_in_dim(partial_pairs, w ^ 1, 1, False)
    grad_own = own_part + lax.ppermute(other_part, "wide", swap)
    grad_own = grad_own.reshape(n_slots, 2 * HD).astype(BF).astype(F4)
    turned = rotate(grad_own[:, None, :HD], slot_cos, -slot_sin)[:, 0]
    grad_projected = jnp.concatenate([turned, grad_own[:, HD:]], axis=1).astype(BF)
    own_valid = (own_codes.reshape(-1) < seqs * LEN)
    grad_projected = jnp.where(own_valid[:, None], grad_projected, jnp.zeros((), BF))
    kv_part = dot(slot_normed, grad_projected, ((0,), (0,)))
    slot_grad_normed = dot(grad_projected, kv_low, ((1,), (1,)))
    grad_rows = norm_pull(slot_grad_normed * gain0, slot_normal, slot_scale)
    grad_rows = grad_rows + lax.dot_general(
        pick.astype(F4),
        grad_stream,
        (((0,), (0,)), ((), ())),
        precision=lax.Precision.HIGHEST,
        preferred_element_type=F4,
    )
    grad_rows = jnp.where(own_valid[:, None], grad_rows, 0.0)
    own_ids = jnp.where(
        own_valid, lax.dynamic_index_in_dim(slot_ids, lax.axis_index("rep"), 0, False), vr
    )
    same = own_ids[:, None] == own_ids[None, :]
    order = jnp.arange(n_slots, dtype=jnp.int32)
    earlier = same & (order[None, :] < order[:, None])
    lead = own_valid & ~jnp.any(earlier, axis=1)
    same = same.astype(BF)
    high = grad_rows.astype(BF)
    rest = (grad_rows - high.astype(F4)).astype(BF)
    grad_rows = dot(same, high, ((1,), (0,))) + dot(same, rest, ((1,), (0,)))

    squares = jnp.sum(jnp.where(lead[:, None], grad_rows * grad_rows, 0.0))
    squares = squares + jnp.sum(grad_unembed * grad_unembed)
    for parts in grad_weights:
        for piece in parts:
            squares = squares + jnp.sum(piece * piece)
    kv_total, gain_part, bias_part, pair_bias_grad, square_total = lax.psum(
        (
            kv_part,
            jnp.sum(slot_grad_normed * slot_normal * own_valid[:, None], axis=0),
            jnp.sum(slot_grad_normed * own_valid[:, None], axis=0),
            jnp.sum(grad_projected, axis=0, dtype=F4),
            squares,
        ),
        "wide",
    )
    grad_small = jnp.concatenate(
        [
            grad_vectors[0].at[:D].add(gain_part).at[D : 2 * D].add(bias_part),
            grad_vectors[1],
            pair_bias_grad,
            grad_final_gain,
            grad_final_bias,
        ]
    )
    square_total = square_total + jnp.sum(kv_total * kv_total) + jnp.sum(grad_small * grad_small)
    clip_factor = jnp.minimum(1.0, CLIP / (jnp.sqrt(square_total) + 1e-06))

    un_one, un_two, un_step = moments_step(
        grad_unembed * clip_factor, first_tables[0, 1], second_tables[0, 1]
    )
    un_sum = lax.psum_scatter(
        un_step.astype(BF).reshape(vr, reps, D // reps).transpose(1, 0, 2),
        "rep",
        scatter_dimension=0,
        tiled=True,
    )[0]
    clipped_ids = jnp.minimum(own_ids, vr - 1)
    old_one = jnp.take(first_tables[0, 0], clipped_ids, axis=0)
    old_two = jnp.take(second_tables[0, 0], clipped_ids, axis=0)
    row_one, row_two, row_step = moments_step(grad_rows * clip_factor, old_one, old_two)
    old_step = (BETA_ONE * old_one * FIX_ONE) / (
        jnp.sqrt(BETA_TWO * old_two * FIX_TWO) + ADAM_EPSILON
    )
    em_one = base_one.at[own_ids].set(row_one, mode="drop")
    em_two = base_two.at[own_ids].set(row_two, mode="drop")
    extra = jnp.where(lead[:, None], row_step - old_step.astype(BF).astype(F4), 0.0).astype(BF)
    extra = lax.all_to_all(
        extra.reshape(n_slots, reps, D // reps).transpose(1, 0, 2), "rep", 0, 0, tiled=True
    )
    em_sum = base_sum.astype(F4).at[jnp.where(slot_valid, slot_ids, vr).reshape(-1)].add(
        extra.reshape(reps * n_slots, D // reps).astype(F4), mode="drop"
    )
    table_sum = jnp.stack([em_sum, un_sum.astype(F4)])

    att_grad = jnp.stack([jnp.stack(parts[:2]) for parts in grad_weights])
    ff_grad = jnp.stack([jnp.stack(parts[2:]) for parts in grad_weights])
    kv_grad = lax.dynamic_slice_in_dim(kv_total, w * own_rows, own_rows, axis=0)
    att_one, att_two, att_step = moments_step(
        att_grad * clip_factor, first_attention[0], second_attention[0]
    )
    ff_one, ff_two, ff_step = moments_step(
        ff_grad * clip_factor, first_feedforward[0], second_feedforward[0]
    )
    kv_one, kv_two, kv_step = moments_step(
        kv_grad * clip_factor, first_key_value[0], second_key_value[0]
    )
    sm_one, sm_two, sm_step = moments_step(
        grad_small * clip_factor, first_gains[0], second_gains[0]
    )
    scattered = partial(lax.psum_scatter, axis_name="rep", tiled=True)
    sums = (
        table_sum,
        scattered(att_step.astype(BF), scatter_dimension=3).astype(F4),
        scattered(ff_step.astype(BF), scatter_dimension=3).astype(F4),
        scattered(kv_step, scatter_dimension=1),
        scattered(sm_step, scatter_dimension=0),
    )
    masters = (tables, attention, feedforward, key_value, gains_biases)
    outers = (outer_tables, outer_attention, outer_feedforward, outer_key_value, outer_gains)
    new_masters = []
    new_outers = []
    for index in range(5):
        mean_diff = LEARN_RATES[index] * (sums[index] / reps + DECAY * masters[index])
        momentum = OUTER_MOMENTUM * outers[index] + mean_diff
        new_outers.append(momentum)
        new_masters.append(masters[index] - OUTER_RATE * (mean_diff + OUTER_MOMENTUM * momentum))
    return (
        loss_sum.reshape(1),
        count.reshape(1),
        *new_masters,
        jnp.stack([em_one, un_one])[None],
        att_one[None],
        ff_one[None],
        kv_one[None],
        sm_one[None],
        jnp.stack([em_two, un_two])[None],
        att_two[None],
        ff_two[None],
        kv_two[None],
        sm_two[None],
        *new_outers,
    )


def solution(mesh):
    split = (
        P(None, "wide", "rep"),
        P(None, None, "wide", "rep"),
        P(None, None, "wide", "rep"),
        P("wide", "rep"),
        P("rep"),
    )
    moments = (
        P("rep", None, "wide", None),
        P("rep", None, None, "wide", None),
        P("rep", None, None, "wide", None),
        P("rep", "wide", None),
        P("rep", None),
    )
    tokens = P("rep", None, None, None, None)
    return jax.shard_map(
        body,
        mesh=mesh,
        in_specs=(tokens,) * 3 + split + moments + moments + split,
        out_specs=(P("rep"), P("rep")) + split + moments + moments + split,
        check_vma=False,
    )
```

```python
from functools import partial

import jax
import jax.numpy as jnp
from jax import lax
from jax.experimental import pallas as pl
from jax.experimental.pallas import tpu as pltpu
from jax.sharding import Mesh
from jax.sharding import PartitionSpec as P

D = 512
HEADS = 8
HD = 64
ROT = 16
FF = 2048
L = 2
LEN = 2048
MICRO = 2
STEP = 5
WIDE_AXES = ("chip", "core")

NORM_EPSILON = 1e-05
CLIP = 0.1
LEARN_RATES = (0.02, 0.2, 0.02, 0.02, 0.2)
BETA_ONE = 0.9
BETA_TWO = 0.95
ADAM_EPSILON = 1e-08
DECAY = 0.1
OUTER_RATE = 0.7
OUTER_MOMENTUM = 0.9
FIX_ONE = 1.0 / (1.0 - BETA_ONE**STEP)
FIX_TWO = 1.0 / (1.0 - BETA_TWO**STEP)

BF = jnp.bfloat16
F4 = jnp.float32


def dot(left, right, dims):
    return lax.dot_general(left, right, (dims, ((), ())), preferred_element_type=F4)


def normal_of(stream):
    centred = stream - jnp.mean(stream, axis=-1, keepdims=True)
    scale = lax.rsqrt(jnp.mean(centred * centred, axis=-1, keepdims=True) + NORM_EPSILON)
    return centred * scale, scale


def norm_pull(shaped, normal, scale):
    return scale * (
        shaped
        - jnp.mean(shaped, axis=-1, keepdims=True)
        - normal * jnp.mean(shaped * normal, axis=-1, keepdims=True)
    )


def rotary(places):
    frequency = 10000.0 ** (-2.0 * jnp.arange(ROT // 2, dtype=F4) / ROT)
    angles = places.astype(F4)[:, None] * frequency[None, :]
    return jnp.cos(angles), jnp.sin(angles)


def rotate(values, cosine, sine):
    half = ROT // 2
    a = values[..., :half]
    b = values[..., half:ROT]
    c = cosine[:, None, :]
    s = sine[:, None, :]
    return jnp.concatenate([a * c - b * s, b * c + a * s, values[..., ROT:]], axis=-1)


def unpack_small(gains_biases):
    span = 7 * D + FF
    layers = gains_biases[: L * span].reshape(L, span)
    remain = gains_biases[L * span :]
    return layers, remain[: 2 * HD], remain[2 * HD : 2 * HD + D], remain[2 * HD + D :]


def moments_step(gradient, one, two):
    one = BETA_ONE * one + (1.0 - BETA_ONE) * gradient
    two = BETA_TWO * two + (1.0 - BETA_TWO) * gradient * gradient
    return one, two, (one * FIX_ONE) / (jnp.sqrt(two * FIX_TWO) + ADAM_EPSILON)


def step_of(one, two):
    two = two * FIX_TWO
    under = two * lax.rsqrt(jnp.maximum(two, 1e-37)) + ADAM_EPSILON
    guess = pl.reciprocal(under, approx=True)
    return one * FIX_ONE * (guess * (2.0 - under * guess))


def moments_fast(gradient, one, two):
    one = BETA_ONE * one + (1.0 - BETA_ONE) * gradient
    two = BETA_TWO * two + (1.0 - BETA_TWO) * gradient * gradient
    return one, two, step_of(one, two)


VM = pl.BlockSpec(memory_space=pltpu.VMEM)
SM = pl.BlockSpec(memory_space=pltpu.SMEM)
LANES = 128
BLOCKS = D // LANES
ROWS = 64
RUN = 1572
SPREAD = 4
FAR = 1 << 30


def shaped(*dims, kind=F4):
    return jax.ShapeDtypeStruct(dims, kind)


def call(kernel, outs, ins, smem=0, scratch=(), out_specs=None, name=None, room=58, far=()):
    return pl.pallas_call(
        kernel,
        out_shape=outs,
        in_specs=[SM if i < smem else ANY if i in far else VM for i in range(len(ins))],
        out_specs=[VM] * len(outs) if out_specs is None else out_specs,
        scratch_shapes=list(scratch),
        compiler_params=pltpu.CompilerParams(vmem_limit_bytes=room * 1024 * 1024),
        name=name,
    )(*ins)


ANY = pl.BlockSpec(memory_space=pltpu.HBM)
ATT = L * 2 * LANES
WIDE = 2 * FF // BLOCKS


class Fetch:
    def __init__(self, sc_ref, weights, scr, sems, start):
        w, rep = sc_ref[0], sc_ref[2]
        cols = pl.ds(start, scr.shape[2])
        self.copies = []
        for core in range(2):
            mine = weights[5 * core : 5 * core + 5]
            spots = [(mine[k], k, i, i) for k in range(3) for i in range(mine[0].shape[0])]
            cut = mine[3].shape[0]
            spots += [(mine[3], 3, i, i) for i in range(cut)]
            spots += [(mine[4], 3, i, i + cut) for i in range(mine[4].shape[0])]
            for ref, k, i, chip in spots:
                own_rows = ref.shape[1]
                at = pl.multiple_of((w ^ (2 * chip + core)) * own_rows, own_rows)
                self.copies.append(
                    pltpu.make_async_copy(
                        ref.at[i, :, cols],
                        scr.at[rep ^ k, pl.ds(at, own_rows), :],
                        sems.at[core, k, chip],
                    )
                )
        for copy in self.copies:
            copy.start()

    def wait(self):
        for copy in self.copies:
            copy.wait()


def nn(left, right):
    return dot(left, right, ((1,), (0,)))


def nt(left, right):
    return dot(left, right, ((1,), (1,)))


def tn(left, right):
    return dot(left, right, ((0,), (0,)))


def split_two(value):
    high = value.astype(BF)
    return high, (value - high.astype(F4)).astype(BF)


def lanes_of(rows):
    return lax.broadcasted_iota(jnp.int32, (rows, LANES), 1)


def spin(value, cosine, sine):
    place = lanes_of(value.shape[0]) % HD
    ahead = pltpu.roll(value, LANES - ROT // 2, 1)
    behind = pltpu.roll(value, ROT // 2, 1)
    moved = jnp.where(place < ROT // 2, -ahead, behind)
    return value * cosine + moved * sine


def swap_halves(value):
    return pltpu.roll(value, HD, 1)


def blocks_of(value):
    return [value[:, LANES * i : LANES * (i + 1)] for i in range(value.shape[1] // LANES)]


def tile_of(vr):
    return 2096 if vr % 2096 == 0 else vr


def kv_kernel(
    sc_ref, rows_ref, cos_ref, sin_ref, vec_ref, pair_bias_ref, slot_code_ref, row_ref, *refs
):
    pairs_ref, picked_ref, kv_ref = refs[-3:]
    n_slots = rows_ref.shape[1]
    for k, piece in enumerate(refs[:-3]):
        own = piece.shape[0]
        kv_ref[pl.ds(pl.multiple_of((sc_ref[0] ^ k) * own, own), own), :] = piece[...]
    step = 256
    for start in range(0, n_slots, step):
        part = pl.ds(start, step)
        rows = jnp.concatenate([rows_ref[r, part, :] for r in range(BLOCKS)], axis=1)
        normal, unused = normal_of(rows.astype(F4))
        normed = (normal * vec_ref[0:1, :D] + vec_ref[0:1, D : 2 * D]).astype(BF)
        projected = pair_bias_ref[...] + nn(normed, kv_ref[...])
        pairs_ref[part, :] = spin(projected, cos_ref[part, :], sin_ref[part, :]).astype(BF)
    rows = jnp.concatenate([rows_ref[r] for r in range(BLOCKS)], axis=1)
    pick = jnp.where(row_ref[:, 0:1] == slot_code_ref[...], 1.0, 0.0).astype(BF)
    picked_ref[...] = nn(pick, rows).astype(BF)


def token_codes(place, m, first_block, seqs, rows_seq):
    block = seqs * rows_seq
    inside = lax.rem(place, block)
    code = m * (seqs * LEN) + (first_block + lax.div(place, block)) * rows_seq
    return code + lax.div(inside, rows_seq) * LEN + lax.rem(inside, rows_seq)


def order_kernel(seqs, rows_seq, width, cap, after_ref, code_ref, *refs):
    pieces, out_ref = refs[:-1], refs[-1]
    block = seqs * rows_seq

    def one(mb, carry):
        m, b = lax.div(mb, width), lax.rem(mb, width)
        part = pl.ds(pl.multiple_of(mb * cap, cap), cap)
        slots = jnp.concatenate([piece[part, :] for piece in pieces], axis=0)
        place = lax.broadcasted_iota(jnp.int32, (block, 1), 0)
        hot = token_codes(place, m, b, seqs, rows_seq) == code_ref[mb]
        out_ref[mb] = nn(jnp.where(hot, 1.0, 0.0).astype(BF), slots).astype(BF)
        return carry

    lax.fori_loop(0, MICRO * width, one, 0)


def stack_heads(block_of, part):
    low_lanes = lanes_of(ROWS) < HD
    pieces = []
    for b in range(2):
        block = block_of[b, part, :]
        pieces += [block, swap_halves(block)]
    return [jnp.where(low_lanes, piece, 0.0) for piece in pieces]


def masks_of(row_ref, part, m, kt, tile, seqs, rows_seq):
    place = lax.broadcasted_iota(jnp.int32, (1, tile), 1)
    code = token_codes(place, m, kt * SPREAD, seqs, rows_seq)
    allowed = code <= row_ref[part, 0:1]
    if seqs > 1:
        allowed = allowed & (code >= row_ref[part, 1:2])
    return allowed


def masked(scores, allowed):
    return jnp.concatenate(
        [
            jnp.where(allowed, scores[ROWS * h : ROWS * (h + 1), :], -1e30)
            for h in range(HEADS // 2)
        ],
        axis=0,
    )


def attend(q_scr, ctx_ref, log_ref, keys_ref, row_ref, scr, seqs, rows_seq):
    micros, tiles, tile, unused = keys_ref.shape
    low_lanes = lanes_of(ROWS) < HD
    high = ROWS * HEADS // 2

    def one(t, carry):
        m, c = lax.div(t, tiles), lax.rem(t, tiles)
        part = pl.ds(pl.multiple_of(t * ROWS, ROWS), ROWS)
        query = jnp.concatenate(stack_heads(q_scr, part), axis=0).astype(BF)

        def scores_at(kt, top):
            allowed = masks_of(row_ref, part, m, kt, tile, seqs, rows_seq)
            scores = masked(nt(query, keys_ref[m, kt]), allowed)
            scr[kt] = scores
            for piece in blocks_of(scores):
                top = jnp.maximum(top, piece)
            return top

        top = lax.fori_loop(0, c + 1, scores_at, jnp.full((high, LANES), -1e30, F4))
        top = jnp.max(top, axis=1, keepdims=True)

        def expo_at(kt, total):
            expo = jnp.exp(scr[kt] - top)
            scr[kt] = expo
            for piece in blocks_of(expo):
                total = total + piece
            return total

        total = lax.fori_loop(0, c + 1, expo_at, jnp.zeros((high, LANES), F4))
        total = jnp.sum(total, axis=1, keepdims=True)
        inverse = 1.0 / total

        def context_at(kt, so_far):
            return so_far + nn((scr[kt] * inverse).astype(BF), keys_ref[m, kt])

        context = lax.fori_loop(0, c + 1, context_at, jnp.zeros((high, LANES), F4))
        log_ref[t] = top + jnp.log(total)
        heads = [context[ROWS * h : ROWS * (h + 1), :] for h in range(HEADS // 2)]
        for b in range(2):
            ctx_ref[b, part, :] = jnp.where(
                low_lanes, swap_halves(heads[2 * b]), heads[2 * b + 1]
            )
        return carry

    lax.fori_loop(0, micros * tiles, one, 0)


def attend_pull(
    q_ref, ctx_ref, grad_scr, log_ref, keys_ref, row_ref, dq_ref, dkv_ref, seqs, rows_seq
):
    micros, tiles, tile, unused = keys_ref.shape
    low_lanes = lanes_of(ROWS) < HD
    high = ROWS * HEADS // 2

    def one(t, carry):
        m, c = lax.div(t, tiles), lax.rem(t, tiles)
        part = pl.ds(pl.multiple_of(t * ROWS, ROWS), ROWS)
        query = jnp.concatenate(stack_heads(q_ref, part), axis=0).astype(BF)
        grads = []
        inners = []
        for b in range(2):
            grad = grad_scr[b, part, :]
            product = grad * ctx_ref[b, part, :]
            for sub in range(2):
                moved = swap_halves(grad) if sub == 0 else grad
                grads.append(jnp.where(low_lanes, 0.0, moved))
                mine = low_lanes if sub == 0 else ~low_lanes
                inners.append(jnp.sum(jnp.where(mine, product, 0.0), axis=1, keepdims=True))
        grad = jnp.concatenate(grads, axis=0).astype(BF)
        inner = jnp.concatenate(inners, axis=0)
        log_total = log_ref[t]

        def pull_at(kt, so_far):
            both = keys_ref[m, kt]
            allowed = masks_of(row_ref, part, m, kt, tile, seqs, rows_seq)
            probs = jnp.exp(masked(nt(query, both), allowed) - log_total)
            grad_scores = (probs * (nt(grad, both) - inner)).astype(BF)
            dkv_ref[m, kt] += tn(grad_scores, query) + tn(probs.astype(BF), grad)
            return so_far + nn(grad_scores, both)

        total = lax.fori_loop(0, c + 1, pull_at, jnp.zeros((high, LANES), F4)) * 0.125
        heads = [total[ROWS * h : ROWS * (h + 1), :] for h in range(HEADS // 2)]
        for b in range(2):
            dq_ref[b, part, :] = jnp.where(
                low_lanes, heads[2 * b], swap_halves(heads[2 * b + 1])
            ).astype(BF)
        return carry

    lax.fori_loop(0, micros * tiles, one, 0)


def to_slots(dkv_ref, code_ref, own_out, near_out, seqs, rows_seq):
    micros, tiles, tile, unused = dkv_ref.shape
    block = seqs * rows_seq
    width = tiles * SPREAD
    cap = own_out.shape[0] // (micros * width)

    def one(mb, carry):
        m, b = lax.div(mb, width), lax.rem(mb, width)
        part = pl.ds(pl.multiple_of(mb * cap, cap), cap)
        inside = pl.ds(pl.multiple_of(lax.rem(b, SPREAD) * block, block), block)
        high, rest = split_two(dkv_ref[m, lax.div(b, SPREAD), inside, :])
        place = lax.broadcasted_iota(jnp.int32, (block, 1), 0)
        code = token_codes(place, m, b, seqs, rows_seq)
        hot = jnp.where(code == code_ref[mb], 1.0, 0.0).astype(BF)
        both = tn(hot, high) + tn(hot, rest)
        own_out[part, :] = both[:cap, :]
        near_out[part, :] = both[cap:, :]
        return carry

    lax.fori_loop(0, micros * width, one, 0)


def join_blocks(parity, own_ref, other_ref):
    return [
        jnp.where(parity == r // 2, own_ref[r % 2].astype(F4), other_ref[r % 2].astype(F4))
        for r in range(BLOCKS)
    ]


def branch_of(parity, k, own_ref, other_ref, att_ref):
    context = jnp.concatenate(join_blocks(parity, own_ref, other_ref), axis=1).astype(BF)
    at = k * 256 + LANES
    return jnp.concatenate(
        [nn(context, att_ref[r, :, at : at + LANES]) for r in range(BLOCKS)], axis=1
    )


def queries_of(k, stream, parity, vec_ref, att_ref, cos_ref, sin_ref, q_ref):
    normal, unused = normal_of(stream)
    normed = (normal * vec_ref[0:1, :D] + vec_ref[0:1, D : 2 * D]).astype(BF)
    cosine, sine = cos_ref[...], sin_ref[...]
    for i in range(2):
        weight = jnp.where(
            parity == 0,
            att_ref[i, :, k * 256 : k * 256 + LANES],
            att_ref[2 + i, :, k * 256 : k * 256 + LANES],
        )
        low = vec_ref[0:1, 4 * D + LANES * i : 4 * D + LANES * (i + 1)]
        high = vec_ref[0:1, 4 * D + LANES * (2 + i) : 4 * D + LANES * (3 + i)]
        query = nn(normed, weight) + jnp.where(parity == 0, low, high)
        query = spin(query, cosine, sine).astype(BF).astype(F4)
        q_ref[i] = query * 0.125


def first_kernel(
    seqs, rows_seq, sc_ref, low_ref, vec_ref, w0, w1, w2, w3, w4, w5, w6, w7, w8, w9, keys_ref, row_ref, cos_ref, sin_ref,
    stream_ref, q_ref, ctx_ref, log_ref, scr, att_ref, sem,
):
    copy = Fetch(sc_ref, (w0, w1, w2, w3, w4, w5, w6, w7, w8, w9), att_ref, sem, L * WIDE)
    stream_ref[...] = low_ref[...].astype(F4)
    copy.wait()
    queries_of(0, stream_ref[...], sc_ref[1], vec_ref, att_ref, cos_ref, sin_ref, q_ref)
    attend(q_ref, ctx_ref, log_ref, keys_ref, row_ref, scr, seqs, rows_seq)


def second_kernel(
    seqs, rows_seq, sc_ref, partial_ref, own_ref, other_ref, vec_ref, w0, w1, w2, w3, w4, w5, w6, w7, w8, w9, keys_ref, row_ref,
    cos_ref, sin_ref, stream_ref, q_ref, ctx_ref, log_ref, scr, att_ref, sem,
):
    parity = sc_ref[1]
    Fetch(sc_ref, (w0, w1, w2, w3, w4, w5, w6, w7, w8, w9), att_ref, sem, L * WIDE).wait()
    stream_ref[...] = partial_ref[...] + branch_of(parity, 0, own_ref, other_ref, att_ref)
    queries_of(1, stream_ref[...], parity, vec_ref, att_ref, cos_ref, sin_ref, q_ref)
    attend(q_ref, ctx_ref, log_ref, keys_ref, row_ref, scr, seqs, rows_seq)


ROOT_HALF = 0.7071067811865476
ROOT_TAU = 0.3989422804014327


def feed_kernel(k, sc_ref, stream_ref, vec_ref, w0, w1, w2, w3, w4, w5, w6, w7, w8, w9, out_ref, ff_ref, sem):
    copy = Fetch(sc_ref, (w0, w1, w2, w3, w4, w5, w6, w7, w8, w9), ff_ref, sem, k * WIDE)
    stream = stream_ref[...]
    normal, unused = normal_of(stream)
    feed = (normal * vec_ref[0:1, 2 * D : 3 * D] + vec_ref[0:1, 3 * D : 4 * D]).astype(BF)
    total = stream + vec_ref[0:1, 5 * D : 6 * D] + vec_ref[0:1, 6 * D : 7 * D]
    cols = FF // BLOCKS
    copy.wait()
    for r in range(BLOCKS):
        at_r = 7 * D + cols * r
        hidden = nn(feed, ff_ref[r, :, :cols]) + vec_ref[0:1, at_r : at_r + cols]
        active = (0.5 * hidden * (1.0 + lax.erf(hidden * ROOT_HALF))).astype(BF)
        total = total + nt(active, ff_ref[r, :, cols:])
    out_ref[...] = total


def runs_of(tables):
    runs = []
    base = 0
    for half in (tables[:4], tables[4:]):
        rows = half[0].shape[0]
        step = RUN if rows % RUN == 0 else rows
        runs += [((base, half), base + at, step) for at in range(0, rows, step)]
        base += rows
    return runs


def logits_kernel(
    sc_ref, partial_ref, own_ref, other_ref, w0, w1, w2, w3, w4, w5, w6, w7, w8, w9, final_ref, target_ref, *refs
):
    tables = refs[:8]
    logits_ref, stats_ref, stream_ref, picked_ref, pick_scr, att_ref, sem = refs[8:]
    parity, rep, offset = sc_ref[1], sc_ref[2], sc_ref[3]
    Fetch(sc_ref, (w0, w1, w2, w3, w4, w5, w6, w7, w8, w9), att_ref, sem, L * WIDE).wait()
    stream = partial_ref[...] + branch_of(parity, 1, own_ref, other_ref, att_ref)
    stream_ref[...] = stream
    normal, unused = normal_of(stream)
    picked = (normal * final_ref[0:1, :] + final_ref[1:2, :]).astype(BF)
    picked_ref[...] = picked
    for r in range(BLOCKS):
        pick_scr[r] = picked[:, LANES * r : LANES * (r + 1)]
    n_loss = picked.shape[0]
    ordered = jnp.concatenate([pick_scr[rep ^ k] for k in range(BLOCKS)], axis=1)
    top = jnp.full((1, n_loss), -1e30, F4)
    hit_total = jnp.zeros((1, n_loss), F4)
    target = target_ref[...] - offset
    for first, start, size in runs_of(tables):
        part = slice(start - first[0], start - first[0] + size)
        table = jnp.concatenate([ref[part, :] for ref in first[1]], axis=1)
        logits = nt(table, ordered)
        logits_ref[start : start + size, :] = logits
        top = jnp.maximum(top, jnp.max(logits, axis=0, keepdims=True))
        place = lax.broadcasted_iota(jnp.int32, (size, n_loss), 0) + start
        hit_total = hit_total + jnp.sum(
            jnp.where(place == target, logits, 0.0), axis=0, keepdims=True
        )
    total = jnp.zeros((1, n_loss), F4)
    for unused, start, size in runs_of(tables):
        total = total + jnp.sum(
            jnp.exp(logits_ref[start : start + size, :] - top), axis=0, keepdims=True
        )
    stats_ref[0:1, :] = top
    stats_ref[1:2, :] = total
    stats_ref[2:3, :] = hit_total
    stats_ref[3:8, :] = jnp.zeros((5, n_loss), F4)


def join_stats(one, two):
    top = jnp.maximum(one[0], two[0])
    total = one[1] * jnp.exp(one[0] - top) + two[1] * jnp.exp(two[0] - top)
    return top, total, one[2] + two[2]


def probs_kernel(
    sc_ref, stats_ref, weight_ref, target_ref, logits_ref, *refs
):
    tables = refs[:8]
    probs_ref, grad_ref, loss_ref = refs[8:]
    rep, offset = sc_ref[2], sc_ref[3]
    vr, n_loss = logits_ref.shape
    parts = [tuple(stats_ref[k, i : i + 1, :] for i in range(3)) for k in range(stats_ref.shape[0])]
    while len(parts) > 1:
        parts = [join_stats(parts[i], parts[i + 1]) for i in range(0, len(parts), 2)]
    top, total, hit = parts[0]
    log_all = top + jnp.log(total)
    weight = weight_ref[...]
    loss_ref[0, 0] = jnp.sum(weight * (log_all - hit))
    share = weight / jnp.sum(weight)
    target = target_ref[...] - offset
    grads = jnp.zeros((n_loss, D), F4)
    for first, start, size in runs_of(tables):
        place = lax.broadcasted_iota(jnp.int32, (size, n_loss), 0) + start
        probs = jnp.exp(logits_ref[start : start + size, :] - log_all)
        probs = (jnp.where(place == target, probs - 1.0, probs) * share).astype(BF)
        probs_ref[start : start + size, :] = probs
        part = slice(start - first[0], start - first[0] + size)
        table = jnp.concatenate([ref[part, :] for ref in first[1]], axis=1)
        grads = grads + tn(probs, table)
    for k in range(BLOCKS):
        grad_ref[rep ^ k] = grads[:, LANES * k : LANES * (k + 1)]


def squares_kernel(probs_ref, picked_ref, out_ref):
    vr = probs_ref.shape[0]
    tile = tile_of(vr)
    total = jnp.zeros((), F4)
    for start in range(0, vr, tile):
        grads = nn(probs_ref[start : start + tile, :], picked_ref[...])
        total = total + jnp.sum(grads * grads)
    out_ref[0, 0] = total


def layer_pull(
    k, seqs, rows_seq, sc_ref, grad_stream, stream, vec_ref, att_ref, ff_ref, copy, own_ref, other_ref, q_ref,
    log_ref, keys_ref, row_ref, dq_ref, dkv_ref, wide_ref, out_ref, vec_out,
    feed_scr, low_scr, grad_scr, prod_scr, square,
):
    parity = sc_ref[1]
    block, place = sc_ref[4], sc_ref[5]
    rows = wide_ref.shape[1]
    cols = FF // BLOCKS
    normal, unused = normal_of(stream)
    feed = (normal * vec_ref[0:1, 2 * D : 3 * D] + vec_ref[0:1, 3 * D : 4 * D]).astype(BF)
    low = grad_stream.astype(BF)
    for r in range(BLOCKS):
        feed_scr[r] = feed[:, LANES * r : LANES * (r + 1)]
        low_scr[r] = low[:, LANES * r : LANES * (r + 1)]
    feed_own = feed_scr[block]
    low_own = low_scr[block]

    at = k * 256 + LANES
    half = D // 2
    start = pl.ds(pl.multiple_of(parity * half, half), half)
    grad_context = nt(low_scr[0], att_ref[0, start, at : at + LANES])
    for r in range(1, BLOCKS):
        grad_context = grad_context + nt(low_scr[r], att_ref[r, start, at : at + LANES])
    grad_context = grad_context.astype(BF).astype(F4)
    grad_scr[0] = grad_context[:, :LANES]
    grad_scr[1] = grad_context[:, LANES:]
    attend_pull(
        q_ref, own_ref, grad_scr, log_ref, keys_ref, row_ref, dq_ref, dkv_ref, seqs,
        rows_seq,
    )

    vec_out[0:1, 5 * D : 6 * D] = jnp.sum(low.astype(F4), axis=0, keepdims=True)
    vec_out[0:1, 6 * D : 7 * D] = jnp.sum(low.astype(F4), axis=0, keepdims=True)
    grad_feed = jnp.zeros_like(grad_stream)
    copy.wait()
    for r in range(BLOCKS):
        at_r = 7 * D + cols * r
        hidden = nn(feed, ff_ref[r, :, :cols]) + vec_ref[0:1, at_r : at_r + cols]
        grown = 1.0 + lax.erf(hidden * ROOT_HALF)
        active = (0.5 * hidden * grown).astype(BF)
        slope = 0.5 * grown + hidden * (ROOT_TAU * jnp.exp(-0.5 * hidden * hidden))
        grad_hidden = (nn(low, ff_ref[r, :, cols:]) * slope).astype(BF)
        grad_feed = grad_feed + nt(grad_hidden, ff_ref[r, :, :cols])
        vec_out[0:1, at_r : at_r + cols] = jnp.sum(
            grad_hidden.astype(F4), axis=0, keepdims=True
        )
        for which, product in enumerate((tn(feed_own, grad_hidden), tn(low_own, active))):
            prod_scr[...] = product
            piece = prod_scr[pl.ds(pl.multiple_of(place, 16), rows), :]
            wide_ref[which, :, cols * r : cols * (r + 1)] = piece
            square = square + jnp.sum(piece * piece)
    blocks = join_blocks(parity, own_ref, other_ref)
    context_own = blocks[0]
    for r in range(1, BLOCKS):
        context_own = jnp.where(block == r, blocks[r], context_own)
    prod_scr[...] = tn(context_own.astype(BF), low)
    piece = prod_scr[pl.ds(pl.multiple_of(place, 16), rows), :]
    out_ref[...] = piece
    square = square + jnp.sum(piece * piece)
    vec_out[0:1, 2 * D : 3 * D] = jnp.sum(grad_feed * normal, axis=0, keepdims=True)
    vec_out[0:1, 3 * D : 4 * D] = jnp.sum(grad_feed, axis=0, keepdims=True)
    return grad_feed, square


def query_pull(
    k, sc_ref, stream, grad_feed, own_ref, other_ref, vec_ref, att_ref, cos_ref, sin_ref, wq_ref,
    head_out, normed_scr, prod_scr, square,
):
    parity = sc_ref[1]
    block, place = sc_ref[4], sc_ref[5]
    rows = wq_ref.shape[0]
    normal, scale = normal_of(stream)
    normed = (normal * vec_ref[0:1, :D] + vec_ref[0:1, D : 2 * D]).astype(BF)
    for r in range(BLOCKS):
        normed_scr[r] = normed[:, LANES * r : LANES * (r + 1)]
    cosine, sine = cos_ref[...], sin_ref[...]
    grad_normed = jnp.zeros_like(stream)
    pieces = []
    for r, part in enumerate(join_blocks(parity, own_ref, other_ref)):
        piece = spin(part.astype(F4), cosine, -sine).astype(BF)
        head_out[0:1, 2 * D + LANES * r : 2 * D + LANES * (r + 1)] = jnp.sum(
            piece.astype(F4), axis=0, keepdims=True
        )
        grad_normed = grad_normed + nt(piece, att_ref[r, :, k * 256 : k * 256 + LANES])
        pieces.append(piece)
    prod_scr[...] = tn(normed_scr[block], jnp.concatenate(pieces, axis=1))
    piece = prod_scr[pl.ds(pl.multiple_of(place, 16), rows), :]
    wq_ref[...] = piece
    square = square + jnp.sum(piece * piece)
    head_out[0:1, :D] = jnp.sum(grad_normed * normal, axis=0, keepdims=True)
    head_out[0:1, D : 2 * D] = jnp.sum(grad_normed, axis=0, keepdims=True)
    shaped_all = grad_normed * vec_ref[0:1, :D] + grad_feed * vec_ref[0:1, 2 * D : 3 * D]
    return norm_pull(shaped_all, normal, scale), square


def last_pull_kernel(
    seqs, rows_seq, sc_ref, before_ref, grads_ref, final_ref, final_stream_ref, stream_ref, vec_ref, w0, w1, w2, w3, w4, w5, w6, w7, w8, w9,
    own_ref, other_ref, q_ref, log_ref, keys_ref, row_ref, dq_ref, dkv_ref,
    wide_ref, out_ref, vec_out, final_out, grad_out, feed_out, square_ref, feed_scr, low_scr,
    grad_scr, prod_scr, att_ref, ff_ref, sems,
):
    att_copy = Fetch(sc_ref, (w0, w1, w2, w3, w4, w5, w6, w7, w8, w9), att_ref, sems.at[0], L * WIDE)
    copy = Fetch(sc_ref, (w0, w1, w2, w3, w4, w5, w6, w7, w8, w9), ff_ref, sems.at[1], WIDE)
    grad_picked = jnp.concatenate([grads_ref[r] for r in range(BLOCKS)], axis=1)
    normal, scale = normal_of(final_stream_ref[...])
    final_out[0:1, :] = jnp.sum(grad_picked * normal, axis=0, keepdims=True)
    final_out[1:2, :] = jnp.sum(grad_picked, axis=0, keepdims=True)
    grad_stream = norm_pull(grad_picked * final_ref[0:1, :], normal, scale)
    grad_out[...] = grad_stream
    dkv_ref[...] = jnp.zeros_like(dkv_ref)
    att_copy.wait()
    grad_feed, square = layer_pull(
        1, seqs, rows_seq, sc_ref, grad_stream, stream_ref[...], vec_ref, att_ref, ff_ref, copy, own_ref,
        other_ref, q_ref, log_ref, keys_ref, row_ref, dq_ref, dkv_ref,
        wide_ref, out_ref, vec_out, feed_scr, low_scr, grad_scr, prod_scr, before_ref[0, 0],
    )
    feed_out[...] = grad_feed
    square_ref[0, 0] = square


def first_pull_kernel(
    seqs, rows_seq, sc_ref, grad_in_ref, feed_in_ref, dq_own_ref, dq_other_ref, stream1_ref, vec1_ref,
    stream_ref, vec_ref, w0, w1, w2, w3, w4, w5, w6, w7, w8, w9, own_ref, other_ref, q_ref, log_ref, keys_ref,
    row_ref, cos_ref, sin_ref, dkv_in_ref, chip_code_ref, dq_ref, own_slots,
    near_slots, wide_ref, out_ref, vec_out, wq_ref, head_out, grad_out, feed_out, square_ref, feed_scr,
    low_scr, grad_scr, prod_scr, dkv_ref, att_ref, ff_ref, sems, dkv_sem,
):
    dkv_copy = pltpu.make_async_copy(dkv_in_ref, dkv_ref, dkv_sem)
    dkv_copy.start()
    att_copy = Fetch(sc_ref, (w0, w1, w2, w3, w4, w5, w6, w7, w8, w9), att_ref, sems.at[0], L * WIDE)
    copy = Fetch(sc_ref, (w0, w1, w2, w3, w4, w5, w6, w7, w8, w9), ff_ref, sems.at[1], 0)
    att_copy.wait()
    grad_part, square = query_pull(
        1, sc_ref, stream1_ref[...], feed_in_ref[...], dq_own_ref, dq_other_ref, vec1_ref, att_ref,
        cos_ref, sin_ref, wq_ref, head_out, feed_scr, prod_scr, jnp.zeros((), F4),
    )
    grad_stream = grad_in_ref[...] + grad_part
    grad_out[...] = grad_stream
    dkv_copy.wait()
    grad_feed, square = layer_pull(
        0, seqs, rows_seq, sc_ref, grad_stream, stream_ref[...], vec_ref, att_ref, ff_ref, copy, own_ref,
        other_ref, q_ref, log_ref, keys_ref, row_ref, dq_ref, dkv_ref,
        wide_ref, out_ref, vec_out, feed_scr, low_scr, grad_scr, prod_scr, square,
    )
    to_slots(dkv_ref, chip_code_ref, own_slots, near_slots, seqs, rows_seq)
    feed_out[...] = grad_feed
    square_ref[0, 0] = square


def embed_pull_kernel(
    sc_ref, grad_in_ref, feed_in_ref, dq_own_ref, dq_other_ref, stream_ref, vec_ref, w0, w1, w2, w3, w4, w5, w6, w7, w8, w9, kv_ref,
    cos_ref, sin_ref, dkv_own_ref, dkv_other_ref, rows_ref, slot_cos_ref, slot_sin_ref,
    slot_ref, row_code_ref, id_row_ref, wq_ref, head_out, rows_out, ids_out,
    kv_out, gain_out, square_ref, count_ref, normed_scr, prod_scr, high_scr, low_scr, att_ref, sem,
):
    Fetch(sc_ref, (w0, w1, w2, w3, w4, w5, w6, w7, w8, w9), att_ref, sem, L * WIDE).wait()
    grad_part, square = query_pull(
        0, sc_ref, stream_ref[...], feed_in_ref[...], dq_own_ref, dq_other_ref, vec_ref, att_ref,
        cos_ref, sin_ref, wq_ref, head_out, normed_scr, prod_scr, jnp.zeros((), F4),
    )
    grad_high, grad_low = split_two(grad_in_ref[...] + grad_part)
    n_slots = rows_ref.shape[1]
    step = 256
    kv_total = jnp.zeros((D, LANES), F4)
    gain_total = jnp.zeros((1, D), F4)
    bias_total = jnp.zeros((1, D), F4)
    pair_total = jnp.zeros((1, LANES), F4)
    gain = vec_ref[0:1, :D]
    for start in range(0, n_slots, step):
        part = pl.ds(start, step)
        real = slot_ref[part, 0:1] < FAR
        grad_pair = dkv_own_ref[part, :] + dkv_other_ref[part, :]
        grad_pair = grad_pair.astype(BF).astype(F4)
        grad_pair = spin(grad_pair, slot_cos_ref[part, :], -slot_sin_ref[part, :])
        grad_pair = jnp.where(real, grad_pair, 0.0).astype(BF)
        rows = jnp.concatenate([rows_ref[r, part, :] for r in range(BLOCKS)], axis=1)
        normal, scale = normal_of(rows.astype(F4))
        normed = (normal * gain + vec_ref[0:1, D : 2 * D]).astype(BF)
        kv_total = kv_total + tn(normed, grad_pair)
        pair_total = pair_total + jnp.sum(grad_pair.astype(F4), axis=0, keepdims=True)
        grad_normed = nt(grad_pair, kv_ref[...])
        gain_total = gain_total + jnp.sum(grad_normed * normal, axis=0, keepdims=True)
        bias_total = bias_total + jnp.sum(grad_normed, axis=0, keepdims=True)
        pick = (slot_ref[part, 0:1] == row_code_ref[...]).astype(F4).astype(BF)
        grad_rows = norm_pull(grad_normed * gain, normal, scale)
        grad_rows = grad_rows + (nn(pick, grad_high) + nn(pick, grad_low))
        grad_rows = jnp.where(real, grad_rows, 0.0)
        high_scr[part, :], low_scr[part, :] = split_two(grad_rows)
    kv_out[...] = kv_total
    gain_out[0:1, :] = gain_total
    gain_out[1:2, :] = bias_total
    gain_out[2:3, :] = jnp.concatenate([pair_total, jnp.zeros((1, D - LANES), F4)], axis=1)
    gain_out[3:8, :] = jnp.zeros((5, D), F4)
    vr = sc_ref[6]
    ids = id_row_ref[...]
    spot = lax.broadcasted_iota(jnp.int32, (1, n_slots), 1)
    later = jnp.zeros((1, n_slots), F4)
    for start in range(0, n_slots, step):
        at = lax.broadcasted_iota(jnp.int32, (step, 1), 0) + start
        same = (slot_ref[pl.ds(start, step), 1:2] == ids) & (at < spot)
        later = jnp.maximum(later, jnp.max(jnp.where(same, 1.0, 0.0), axis=0, keepdims=True))
    lead = jnp.where(ids < vr, 1.0 - later, 0.0)
    rank = jnp.zeros((8, n_slots), F4)
    many = jnp.broadcast_to(lead, (8, n_slots)).astype(BF)
    for start in range(0, n_slots, step):
        at = lax.broadcasted_iota(jnp.int32, (step, 1), 0) + start
        before = jnp.where(at < spot, 1.0, 0.0).astype(BF)
        rank = rank + nn(many[:, start : start + step], before)
    rank = jnp.where(lead > 0.0, rank[0:1, :].astype(jnp.int32), -1)
    count_ref[0, 0] = jnp.sum(lead).astype(jnp.int32)
    for start in range(0, n_slots, step):
        part = pl.ds(start, step)
        at = lax.broadcasted_iota(jnp.int32, (step, 1), 0) + start
        packed = jnp.max(jnp.where(rank == at, ids, -1), axis=1, keepdims=True)
        ids_out[part, :] = packed
        hot = jnp.where(packed == ids, 1.0, 0.0).astype(BF)
        total = nn(hot, high_scr[...]) + nn(hot, low_scr[...])
        rows_out[part, :] = total.astype(BF)
        square = square + jnp.sum(total * total)
    square_ref[0, 0] = square


TILE = 528
SETTLE = 1056


def params():
    return pltpu.CompilerParams(vmem_limit_bytes=58 * 1024 * 1024)


def base_kernel(first_ref, second_ref, after_ref, step_ref):
    one = BETA_ONE * first_ref[0, 0]
    two = BETA_TWO * second_ref[0, 0]
    step = step_of(one, two)
    for r in range(BLOCKS):
        step_ref[r] = step[:, LANES * r : LANES * (r + 1)].astype(BF)


def base_pass(first, second, after):
    vr = first.shape[2]
    whole = pl.BlockSpec((1, 1, SETTLE, D), lambda i: (0, 0, i, 0))
    return pl.pallas_call(
        base_kernel,
        grid=(pl.cdiv(vr, SETTLE),),
        in_specs=[whole, whole, pl.BlockSpec((16, LANES), lambda i: (0, 0))],
        out_specs=pl.BlockSpec((BLOCKS, SETTLE, LANES), lambda i: (0, i, 0)),
        out_shape=shaped(BLOCKS, vr, LANES, kind=BF),
        compiler_params=params(),
        name="embedding_base",
    )(first, second, after)


def unembed_kernel(sc_ref, clip_ref, probs_ref, picked_ref, first_ref, second_ref, *refs):
    one_ref, two_ref, b0_ref, b1_ref, b2_ref, b3_ref, step_scr = refs[-7:]
    gradient = nn(probs_ref[...], picked_ref[...]) * clip_ref[0]
    one, two, step = moments_fast(gradient, first_ref[0, 0], second_ref[0, 0])
    one_ref[0, 0] = one
    two_ref[0, 0] = two
    rep = sc_ref[2]
    for r in range(BLOCKS):
        step_scr[r] = step[:, LANES * r : LANES * (r + 1)].astype(BF)
    for k, ref in enumerate((b0_ref, b1_ref, b2_ref, b3_ref)):
        ref[...] = step_scr[rep ^ k]


def unembed_pass(scalars, clip, probs, picked, first, second, held, start, count):
    vr, n_loss = probs.shape
    rows = min(vr, (start + count) * TILE) - start * TILE
    whole = pl.BlockSpec((1, 1, TILE, D), lambda i: (0, 1, i + start, 0))
    part = pl.BlockSpec((TILE, LANES), lambda i: (i, 0))
    return pl.pallas_call(
        unembed_kernel,
        grid=(count,),
        in_specs=[
            SM,
            SM,
            pl.BlockSpec((TILE, n_loss), lambda i: (i + start, 0)),
            pl.BlockSpec((n_loss, D), lambda i: (0, 0)),
            whole,
            whole,
        ]
        + [ANY] * len(held),
        out_specs=[whole, whole] + [part] * BLOCKS,
        out_shape=[shaped(*first.shape)] * 2 + [shaped(rows, LANES, kind=BF)] * BLOCKS,
        scratch_shapes=[pltpu.VMEM((BLOCKS, TILE, LANES), BF)],
        input_output_aliases={6 + i: i for i in range(len(held))},
        compiler_params=params(),
        name="unembedding_adam",
    )(scalars, clip, probs, picked, first, second, *held)


GROUP = 256


def embed_kernel(
    start, last, clip_ref, count_ref, id_ref, col_ref, rows_ref, first_ref, second_ref, base_ref, *refs
):
    one_ref, two_ref, extra_ref, scr, extra_scr = refs[-5:]
    tile = one_ref.shape[2]
    first = (pl.program_id(0) + start) * tile
    place = lax.broadcasted_iota(jnp.int32, (tile, 1), 0) + first
    row = lax.broadcasted_iota(jnp.int32, (1, tile), 1) + first
    groups = lax.div(count_ref[0] + GROUP - 1, GROUP)

    @pl.when(pl.program_id(0) == 0)
    def _():
        extra_ref[...] = jnp.zeros_like(extra_ref)

    scr[...] = jnp.zeros_like(scr)

    def gather(i, carry):
        hot = jnp.where(place == id_ref[i], 1.0, 0.0).astype(BF)
        part = pl.ds(pl.multiple_of(i * GROUP, GROUP), GROUP)
        scr[...] += nn(hot, rows_ref[part, :])
        return carry

    lax.fori_loop(0, groups, gather, 0)
    one, two, step = moments_fast(scr[...] * clip_ref[0], first_ref[0, 0], second_ref[0, 0])
    one_ref[0, 0] = one
    two_ref[0, 0] = two
    base = jnp.concatenate([base_ref[r] for r in range(BLOCKS)], axis=1).astype(F4)
    extra_scr[...] = jnp.where(place < last, step - base, 0.0).astype(BF)

    def scatter(i, carry):
        part = pl.ds(pl.multiple_of(i * GROUP, GROUP), GROUP)
        hot = jnp.where(row == col_ref[part, :], 1.0, 0.0).astype(BF)
        picked = nn(hot, extra_scr[...])
        for r in range(BLOCKS):
            extra_ref[r, part, :] += picked[:, LANES * r : LANES * (r + 1)]
        return carry

    lax.fori_loop(0, groups, scatter, 0)


def embed_pass(clip, count, ids, rows, first, second, base, held, after, start, tiles):
    n_slots = rows.shape[0]
    vr = first.shape[2]
    whole = pl.BlockSpec((1, 1, SETTLE, D), lambda i: (0, 0, i + start, 0))
    blocks = pl.BlockSpec((BLOCKS, n_slots, LANES), lambda i: (0, 0, 0))
    groups = n_slots // GROUP
    return pl.pallas_call(
        partial(embed_kernel, start, vr),
        grid=(tiles,),
        in_specs=[
            SM,
            SM,
            pl.BlockSpec((groups, 1, GROUP), lambda i: (0, 0, 0)),
            pl.BlockSpec((n_slots, 1), lambda i: (0, 0)),
            pl.BlockSpec((n_slots, D), lambda i: (0, 0)),
            whole,
            whole,
            pl.BlockSpec((BLOCKS, SETTLE, LANES), lambda i: (0, i + start, 0)),
        ]
        + [ANY] * 3,
        out_specs=[whole, whole, blocks],
        out_shape=[shaped(*first.shape)] * 2 + [shaped(BLOCKS, n_slots, LANES)],
        input_output_aliases={8: 0, 9: 1},
        scratch_shapes=[pltpu.VMEM((SETTLE, D), F4), pltpu.VMEM((SETTLE, D), BF)],
        compiler_params=params(),
        name="embedding_adam",
    )(clip, count, ids.reshape(groups, 1, GROUP), ids, rows, first, second, base, *held, after)


def layers_kernel(
    clip_ref, after_ref, wq0, out0, wq1, out1, wide0, wide1, kv_ref, a1, a2, f1, f2, k1, k2, oa1, oa2, of1, of2,
    ok1, ok2, step_ref,
):
    clip = clip_ref[0]
    rows = wq0.shape[0]
    for k, grads in enumerate(((wq0, out0), (wq1, out1))):
        for i in range(2):
            one, two, step = moments_fast(grads[i][...] * clip, a1[0, k, i], a2[0, k, i])
            oa1[0, k, i] = one
            oa2[0, k, i] = two
            at = (2 * k + i) * rows
            for r in range(BLOCKS):
                step_ref[r, at : at + rows, :] = step[:, LANES * r : LANES * (r + 1)].astype(BF)
    cols = FF // BLOCKS // LANES
    for k, grads in enumerate((wide0, wide1)):
        for i in range(2):
            one, two, step = moments_fast(grads[i] * clip, f1[0, k, i], f2[0, k, i])
            of1[0, k, i] = one
            of2[0, k, i] = two
            for r in range(BLOCKS):
                for q in range(cols):
                    at = (2 * L + (2 * k + i) * cols + q) * rows
                    lane = LANES * (r * cols + q)
                    step_ref[r, at : at + rows, :] = step[:, lane : lane + LANES].astype(BF)
    one, two, step = moments_fast(kv_ref[...] * clip, k1[0], k2[0])
    ok1[0] = one
    ok2[0] = two
    at = (2 * L + 2 * L * cols) * rows
    for r in range(BLOCKS):
        moved = step if r == 0 else pltpu.roll(step, LANES - r * (LANES // BLOCKS), 1)
        step_ref[r, at : at + rows, :] = moved.astype(BF)


def settle(total, master, outer, rate, reps):
    mean_diff = rate * (total * (1.0 / reps) + DECAY * master)
    momentum = OUTER_MOMENTUM * outer + mean_diff
    return master - OUTER_RATE * (mean_diff + OUTER_MOMENTUM * momentum), momentum


def embed_settle_kernel(
    reps, rate, count_ref, id_ref, extra_ref, base_ref, master_ref, outer_ref, new_ref, mom_ref, scr
):
    tile = base_ref.shape[0]
    first = pl.program_id(0) * tile
    place = lax.broadcasted_iota(jnp.int32, (tile, 1), 0) + first
    scr[...] = base_ref[...].astype(F4)
    for g in range(reps):
        groups = lax.div(count_ref[g] + GROUP - 1, GROUP)

        def add(i, carry):
            hot = jnp.where(place == id_ref[g, i], 1.0, 0.0).astype(BF)
            part = pl.ds(pl.multiple_of(i * GROUP, GROUP), GROUP)
            scr[...] += nn(hot, extra_ref[g, part, :])
            return carry

        lax.fori_loop(0, groups, add, 0)
    new_ref[0], mom_ref[0] = settle(scr[...], master_ref[0], outer_ref[0], rate, reps)


def embed_settle(reps, counts, ids, extra, base, master, outer):
    vr = base.shape[0]
    slots = extra.shape[1]
    whole = pl.BlockSpec((1, SETTLE, LANES), lambda i: (0, i, 0))
    return pl.pallas_call(
        partial(embed_settle_kernel, reps, LEARN_RATES[0]),
        grid=(pl.cdiv(vr, SETTLE),),
        in_specs=[
            SM,
            pl.BlockSpec((reps, slots // GROUP, 1, GROUP), lambda i: (0, 0, 0, 0)),
            pl.BlockSpec((reps, slots, LANES), lambda i: (0, 0, 0)),
            pl.BlockSpec((SETTLE, LANES), lambda i: (i, 0)),
            whole,
            whole,
        ],
        out_specs=[whole, whole],
        out_shape=[shaped(*master.shape)] * 2,
        scratch_shapes=[pltpu.VMEM((SETTLE, LANES), F4)],
        compiler_params=params(),
        name="embedding_settle",
    )(counts, ids, extra, base, master, outer)


def unembed_settle_kernel(reps, rate, a_ref, b_ref, c_ref, master_ref, outer_ref, *refs):
    new_ref, mom_ref = refs[-2:]
    rows = a_ref.shape[0]
    total = a_ref[...].astype(F4) + b_ref[...].astype(F4) + c_ref[...].astype(F4)
    new_ref[0, :rows], mom_ref[0, :rows] = settle(
        total, master_ref[0, :rows], outer_ref[0, :rows], rate, reps
    )


def unembed_settle(reps, terms, master, outer, held, piece, size):
    whole = pl.BlockSpec((1, size, LANES), lambda i: (1, piece, 0))
    part = pl.BlockSpec(terms[0].shape, lambda i: (0, 0))
    return pl.pallas_call(
        partial(unembed_settle_kernel, reps, LEARN_RATES[0]),
        grid=(1,),
        in_specs=[part] * 3 + [whole, whole] + [ANY] * 2,
        out_specs=[whole, whole],
        out_shape=[shaped(*master.shape)] * 2,
        input_output_aliases={5: 0, 6: 1},
        compiler_params=params(),
        name="unembedding_settle",
    )(*terms, master, outer, *held)


def body(
    token_ids,
    prompt_mask,
    loss_pos,
    tables,
    attention,
    feedforward,
    key_value,
    gains_biases,
    first_tables,
    first_attention,
    first_feedforward,
    first_key_value,
    first_gains,
    second_tables,
    second_attention,
    second_feedforward,
    second_key_value,
    second_gains,
    outer_tables,
    outer_attention,
    outer_feedforward,
    outer_key_value,
    outer_gains,
):
    width = lax.axis_size(WIDE_AXES)
    reps = lax.axis_size("rep")
    w = lax.axis_index(WIDE_AXES)
    rep = lax.axis_index("rep")
    seqs = token_ids.shape[3]
    rows_seq = LEN // width
    block = seqs * rows_seq
    cap = 2 * block // width
    vr = tables.shape[1]
    lrows = loss_pos.shape[4]
    n_micro = width * lrows
    n_loss = MICRO * n_micro
    span = width * cap
    n_slots = MICRO * span
    own_rows = D // width
    parity = w % 2

    def over_wide(value, k):
        return lax.ppermute(value, WIDE_AXES, [(i, i ^ k) for i in range(width)])

    def over_rep(value, k):
        return lax.ppermute(value, "rep", [(i, i ^ k) for i in range(reps)])

    def sum_wide(value, kind, beside=()):
        half = value.shape[0] // 2
        keep = lax.dynamic_slice_in_dim(value, parity * half, half)
        give = lax.dynamic_slice_in_dim(value, (1 - parity) * half, half)
        mine = (keep + over_wide(give, 1)).astype(kind)
        parts = [mine] + [over_wide(mine, k) for k in range(2, width, 2)]
        parts, *beside = lax.optimization_barrier((parts, *beside))
        parts = [part.astype(F4) for part in parts]
        while len(parts) > 1:
            parts = [parts[i] + parts[i + 1] for i in range(0, len(parts), 2)]
        total = parts[0].astype(value.dtype)
        other = over_wide(total, 1)
        joined = jnp.concatenate(
            [jnp.where(parity == 0, total, other), jnp.where(parity == 0, other, total)]
        )
        return (joined, *beside) if beside else joined

    scalars = jnp.stack(
        [
            w,
            parity,
            rep,
            w * vr,
            w * own_rows // LANES,
            w * own_rows % LANES,
            jnp.asarray(vr, jnp.int32),
            jnp.zeros((), jnp.int32),
        ]
    ).astype(jnp.int32)

    pack = jnp.concatenate(
        [feedforward[k, i] for k in range(L) for i in range(2)]
        + [attention[k, i] for k in range(L) for i in range(2)],
        axis=1,
    ).astype(BF)
    pack_near = [over_wide(pack, k) for k in range(2, width, 2)]

    n_tok = MICRO * seqs * LEN
    flat = jnp.concatenate(
        [
            token_ids.reshape(-1).astype(F4),
            gains_biases,
            key_value.reshape(-1),
        ]
    )
    total = flat.shape[0]
    flat = jnp.pad(flat, (0, -total % 1024)).reshape(-1, LANES)
    everyone = lax.all_gather(flat, "rep").reshape(reps, -1)
    tokens_all = everyone[:, :n_tok].astype(jnp.int32)
    at_small = n_tok
    at_kv = at_small + gains_biases.shape[0]
    small = everyone[:, at_small:at_kv].reshape(-1)
    kv_mine = everyone[:, at_kv:total].reshape(reps, own_rows, -1).transpose(1, 0, 2)
    kv_near = kv_mine.reshape(own_rows, LANES).astype(BF)
    kv_near = [kv_near] + [over_wide(kv_near, k) for k in range(2, width, 2)]
    kv_near = [part for piece in kv_near for part in (piece, over_wide(piece, 1))]
    vectors, pair_bias, final_gain, final_bias = unpack_small(small)
    final_rows = jnp.stack([final_gain, final_bias])

    mine_w = jnp.stack([pack] + pack_near)
    half_w = mine_w.shape[0] // 2
    x_w, y_w = over_rep(mine_w, 1), over_rep(mine_w, 2)

    ordered_all = tokens_all.reshape(reps, MICRO, seqs, width, rows_seq).transpose(0, 1, 3, 2, 4)
    ordered_all = ordered_all.reshape(reps, MICRO, width, block)
    lower = (jnp.arange(block)[:, None] <= jnp.arange(block)[None, :]).astype(BF)
    ranks = jnp.arange(cap, dtype=jnp.int32)

    def slots_of(hit, payloads):
        rank = lax.dot_general(
            hit.astype(BF).reshape(-1, block),
            lower,
            (((1,), (0,)), ((), ())),
            preferred_element_type=F4,
        )
        rank = rank.astype(jnp.int32).reshape(hit.shape) - 1
        hot = hit[..., None] & (rank[..., None] == ranks)
        valid = rank[..., -1:] >= ranks
        return [jnp.sum(jnp.where(hot, p[..., None], 0), axis=-2) for p in payloads], valid

    places = jnp.arange(block, dtype=jnp.int32)
    place_codes = (
        jnp.arange(MICRO, dtype=jnp.int32)[:, None, None] * (seqs * LEN)
        + (places // rows_seq * LEN + places % rows_seq)[None, None, :]
        + jnp.arange(width, dtype=jnp.int32)[None, :, None] * rows_seq
    )
    local_all = ordered_all - w * vr
    (slot_ids, slot_codes), slot_valid = slots_of(
        (local_all >= 0) & (local_all < vr),
        (local_all, jnp.broadcast_to(place_codes[None], local_all.shape)),
    )
    slot_codes = jnp.where(slot_valid, slot_codes, FAR).reshape(reps, n_slots)
    slot_ids = slot_ids.reshape(reps, n_slots)
    scatter_ids = jnp.where(slot_valid.reshape(reps, n_slots), slot_ids, vr)
    own_codes = lax.dynamic_index_in_dim(slot_codes, rep, 0, False)
    own_ids = lax.dynamic_index_in_dim(scatter_ids, rep, 0, False)
    slot_own = lax.dynamic_index_in_dim(slot_ids, rep, 0, False)

    mine_ordered = lax.dynamic_index_in_dim(ordered_all, rep, 0, False)
    shards = w ^ jnp.arange(width, dtype=jnp.int32)
    hit = (mine_ordered // vr)[None] == shards[:, None, None, None]
    (key_codes,), key_valid = slots_of(hit, (jnp.broadcast_to(place_codes[None], hit.shape),))
    key_codes = jnp.where(key_valid, key_codes, FAR)
    chip_codes = key_codes[:2].transpose(1, 2, 0, 3).reshape(MICRO * width, 1, 2 * cap)
    key_codes = key_codes.transpose(1, 2, 0, 3).reshape(MICRO * width, 1, span)

    def row_codes_of(codes):
        codes = codes.reshape(codes.shape[:-1] + (MICRO, width, lrows))
        return (
            jnp.arange(MICRO, dtype=jnp.int32)[:, None, None] * (seqs * LEN)
            + codes // (rows_seq - 1) * LEN
            + jnp.arange(width, dtype=jnp.int32)[:, None] * rows_seq
            + codes % (rows_seq - 1)
        ).reshape(codes.shape[:-3] + (n_loss,))

    row_code = row_codes_of(loss_pos.reshape(-1))
    targets = jnp.take(token_ids.reshape(-1), row_code + 1)
    weight = jnp.take(prompt_mask.reshape(-1), row_code + 1).astype(F4)
    count = jnp.sum(weight)
    row_cols = jnp.stack([row_code, row_code // LEN * LEN], axis=1)

    rows = jnp.take(tables[0], slot_ids.reshape(-1), axis=0).astype(BF)
    rows = rows.reshape(reps, n_slots, D // reps)
    rows = lax.all_to_all(rows, "rep", 0, 0, tiled=True)

    cut = vr // 2 // 16 * 16
    halves_of = [tables[1, :cut].astype(BF), tables[1, cut:].astype(BF)]
    weights = [mine_w, x_w, y_w, over_rep(x_w[:half_w], 2), over_rep(y_w[half_w:], 1)]
    weights = weights + [over_wide(part, 1) for part in weights]
    *halves_of, rows = lax.optimization_barrier((*halves_of, rows))
    x_table = [over_rep(part, 1) for part in halves_of]
    y_table = [over_rep(part, 2) for part in halves_of]

    def turns(place, ends):
        frequency = 10000.0 ** (-2.0 * jnp.arange(ROT // 2, dtype=F4) / ROT)
        angles = place.astype(F4)[None, :] * frequency[:, None]
        cosine, sine = jnp.cos(angles), jnp.sin(angles)
        rest = HD - ROT
        ones = jnp.ones((rest, place.shape[0]), F4)
        zeros = jnp.zeros((rest, place.shape[0]), F4)
        cosine = [cosine, cosine, ones]
        sine = [sine, sine, zeros]
        if ends:
            cosine = cosine + [jnp.ones((HD, place.shape[0]), F4)]
            sine = sine + [jnp.zeros((HD, place.shape[0]), F4)]
        else:
            cosine, sine = cosine * 2, sine * 2
        return jnp.concatenate(cosine).T, jnp.concatenate(sine).T

    slot_cos, slot_sin = turns(own_codes % LEN, True)
    row_cos, row_sin = turns(row_code % LEN, False)
    vec = [vectors[k][None, :] for k in range(L)]
    pairs, stream, kv_low = call(
        kv_kernel,
        [shaped(n_slots, LANES, kind=BF), shaped(n_loss, D, kind=BF), shaped(D, LANES, kind=BF)],
        (
            scalars, rows, slot_cos, slot_sin, vec[0], pair_bias[None, :], own_codes[None, :],
            row_cols, *kv_near,
        ),
        smem=1,
        name="keys_values",
        room=24,
    )
    near = [pairs] + [over_wide(pairs, k) for k in range(2, width, 2)]
    base_step = base_pass(first_tables, second_tables, pairs)
    near, base_step = lax.optimization_barrier((near, base_step))
    pieces = []
    for piece in near:
        pieces += [piece, over_wide(piece, 1)]
    (keys,) = call(
        partial(order_kernel, seqs, rows_seq, width, cap),
        [shaped(MICRO * width, block, LANES, kind=BF)],
        (base_step, key_codes, *pieces),
        far=(0,),
        room=24,
        name="token_order",
    )
    stream = sum_wide(stream, BF)
    tiles = width // SPREAD
    keys, x_table[0], y_table[1] = lax.optimization_barrier((keys, x_table[0], y_table[1]))
    d_table = [over_rep(x_table[0], 2), over_rep(y_table[1], 1)]
    tables_low = [
        part[i] for i in range(2) for part in (halves_of, x_table, y_table, d_table)
    ]
    keys = keys.reshape(MICRO, tiles, SPREAD * block, LANES)

    base_step, *d_table = lax.optimization_barrier((base_step, *d_table))
    base_sum = lax.psum_scatter(base_step, "rep", scatter_dimension=0, tiled=True)[0]

    codes = (row_cols,)
    halves = shaped(2, n_loss, LANES)
    att_room = [pltpu.VMEM((reps, D, ATT), BF), pltpu.SemaphoreType.DMA((2, 4, width // 2))]
    ff_room = [pltpu.VMEM((reps, D, WIDE), BF), pltpu.SemaphoreType.DMA((2, 4, width // 2))]
    both_room = [att_room[0], ff_room[0], pltpu.SemaphoreType.DMA((2, 2, 4, width // 2))]
    stacked = ROWS * HEADS // 2
    logs = shaped(n_loss // ROWS, stacked, 1)
    scores = pltpu.VMEM((tiles, stacked, SPREAD * block), F4)
    whole = shaped(n_loss, D)

    def other_half(value):
        return over_wide(value.astype(BF), 1)

    stream0, q0, ctx0, log0 = call(
        partial(first_kernel, seqs, rows_seq),
        [whole, halves, halves, logs],
        (scalars, stream, vec[0], *weights, keys, *codes, row_cos, row_sin),
        smem=1,
        scratch=[scores] + att_room,
        far=range(3, 13),
        room=24 if tiles == 2 else 58,
        name="first_attention",
    )
    far0 = other_half(ctx0)
    (partial0,) = call(partial(feed_kernel, 0), [whole], (scalars, stream0, vec[0], *weights), smem=1, scratch=ff_room, far=range(3, 13), room=24, name="first_feed")
    stream1, q1, ctx1, log1 = call(
        partial(second_kernel, seqs, rows_seq),
        [whole, halves, halves, logs],
        (scalars, partial0, ctx0, far0, vec[1], *weights, keys, *codes, row_cos, row_sin),
        smem=1,
        scratch=[scores] + att_room,
        far=range(5, 15),
        room=24 if tiles == 2 else 58,
        name="second_attention",
    )
    far1 = other_half(ctx1)
    (partial1,) = call(partial(feed_kernel, 1), [whole], (scalars, stream1, vec[1], *weights), smem=1, scratch=ff_room, far=range(3, 13), room=24, name="second_feed")
    target_row = targets[None, :]
    logits, stats, stream2, picked = call(
        logits_kernel,
        [shaped(vr, n_loss), shaped(8, n_loss), whole, shaped(n_loss, D, kind=BF)],
        (scalars, partial1, ctx1, far1, *weights, final_rows, target_row, *tables_low),
        smem=1,
        scratch=[pltpu.VMEM((BLOCKS, n_loss, LANES), BF)] + att_room,
        far=range(4, 14),
        name="logits",
    )
    near = [stats] + [over_wide(stats, k) for k in range(2, width, 2)]
    stats = jnp.stack([part for piece in near for part in (piece, over_wide(piece, 1))])
    probs, grad_picked, loss_sum = call(
        probs_kernel,
        [shaped(vr, n_loss, kind=BF), shaped(BLOCKS, n_loss, LANES), shaped(1, 1)],
        (scalars, stats, weight[None, :], target_row, logits, *tables_low),
        smem=1,
        out_specs=[VM, VM, SM],
        name="loss_gradient",
    )
    (unembed_square,) = call(
        squares_kernel, [shaped(1, 1)], (probs, picked), out_specs=[SM], name="squares", room=24
    )
    grad_picked, unembed_square = sum_wide(grad_picked, BF, (unembed_square,))

    wide_shape = shaped(2, own_rows, FF)
    out_shape = shaped(own_rows, D)
    vec_shape = shaped(1, 7 * D + FF)
    head_shape = shaped(1, 3 * D)
    dq_shape = shaped(2, n_loss, LANES, kind=BF)
    dkv_shape = shaped(MICRO, tiles, SPREAD * block, LANES)
    slots_shape = shaped(n_slots, LANES)
    pull_scratch = [
        pltpu.VMEM((BLOCKS, n_loss, LANES), BF),
        pltpu.VMEM((BLOCKS, n_loss, LANES), BF),
        pltpu.VMEM((2, n_loss, LANES), F4),
        pltpu.VMEM((LANES, D), F4),
    ]
    dq1, dkv, wide1, out1, vec1, final_grad, grad_stream, grad_feed, square1 = call(
        partial(last_pull_kernel, seqs, rows_seq),
        [
            dq_shape, dkv_shape, wide_shape, out_shape, vec_shape, shaped(2, D), whole, whole,
            shaped(1, 1),
        ],
        (
            scalars, unembed_square, grad_picked, final_rows, stream2, stream1, vec[1], *weights, ctx1,
            far1, q1, log1, keys, *codes,
        ),
        smem=2,
        out_specs=[VM] * 8 + [SM],
        scratch=pull_scratch + both_room,
        far=range(7, 17),
        name="second_pull",
    )
    far_dq1 = over_wide(dq1, 1)
    dq0, own_dkv, near_dkv, wide0, out0, vec0, wq1, head1, grad_stream, grad_feed, square0 = call(
        partial(first_pull_kernel, seqs, rows_seq),
        [
            dq_shape, slots_shape, slots_shape, wide_shape, out_shape, vec_shape, out_shape,
            head_shape, whole, whole, shaped(1, 1),
        ],
        (
            scalars, grad_stream, grad_feed, dq1, far_dq1, stream1, vec[1], stream0, vec[0],
            *weights, ctx0, far0, q0, log0, keys, *codes, row_cos, row_sin, dkv,
            chip_codes,
        ),
        smem=1,
        out_specs=[VM] * 10 + [SM],
        scratch=pull_scratch
        + [pltpu.VMEM(dkv_shape.shape, F4)]
        + both_room
        + [pltpu.SemaphoreType.DMA],
        far=[*range(9, 19), 27],
        name="first_pull",
    )
    far_dq0 = over_wide(dq0, 1)
    far_dkv = over_wide(near_dkv, 1)
    wq0, head0, grad_rows, row_ids, kv_part, gain_part, square_rows, row_count = call(
        embed_pull_kernel,
        [
            out_shape, head_shape, shaped(n_slots, D, kind=BF), shaped(n_slots, 1, kind=jnp.int32),
            shaped(D, LANES), shaped(8, D), shaped(1, 1), shaped(1, 1, kind=jnp.int32),
        ],
        (
            scalars, grad_stream, grad_feed, dq0, far_dq0, stream0, vec[0], *weights, kv_low, row_cos,
            row_sin, own_dkv, far_dkv, rows, slot_cos, slot_sin,
            jnp.stack([own_codes, own_ids], axis=1), row_code[None, :], own_ids[None, :],
        ),
        smem=1,
        out_specs=[VM] * 6 + [SM, SM],
        scratch=[
            pltpu.VMEM((BLOCKS, n_loss, LANES), BF),
            pltpu.VMEM((LANES, D), F4),
            pltpu.VMEM((n_slots, D), BF),
            pltpu.VMEM((n_slots, D), BF),
        ]
        + att_room,
        far=range(7, 17),
        name="embedding_pull",
    )

    square = (square0 + square1 + square_rows)[0, 0]
    message = jnp.concatenate(
        [kv_part, gain_part.reshape(-1, LANES), jnp.full((16, LANES), square, F4)]
    )
    message = sum_wide(message, F4)
    kv_total = message[:D]
    gain_total = message[D : D + 8 * BLOCKS].reshape(8, D)
    square = message[D + 8 * BLOCKS, 0]

    def vector_grad(head, vec_part):
        return [head[0, : 2 * D], vec_part[0, 2 * D : 4 * D], head[0, 2 * D :], vec_part[0, 5 * D :]]

    grad_small = jnp.concatenate(
        [head0[0, : 2 * D] + gain_total[:2].reshape(-1)]
        + vector_grad(head0, vec0)[1:]
        + vector_grad(head1, vec1)
        + [gain_total[2, :LANES], final_grad.reshape(-1)]
    )
    square = square + jnp.sum(kv_total * kv_total) + jnp.sum(grad_small * grad_small)
    clip_factor = jnp.minimum(1.0, CLIP / (jnp.sqrt(square) + 1e-06))

    clip = clip_factor.reshape(1)

    def cross(blocks, first_axis):
        one, two = (1, 2) if first_axis == 0 else (2, 1)
        mine = over_rep(blocks[one], one)
        passing = over_rep(blocks[3], one)
        passing = (blocks[two].astype(F4) + passing.astype(F4)).astype(BF)
        return blocks[0], mine, over_rep(passing, two), passing

    n_tiles = pl.cdiv(vr, TILE)
    size = pl.cdiv(n_tiles, 4)
    pieces = pl.cdiv(n_tiles, size)
    bounds = [min(size * i, n_tiles) for i in range(pieces + 1)]
    held = []
    terms = []
    for i in range(pieces):
        *held, b0, b1, b2, b3 = unembed_pass(
            scalars, clip, probs, picked, first_tables, second_tables, held, bounds[i],
            bounds[i + 1] - bounds[i],
        )
        terms.append(cross((b0, b1, b2, b3), i % 2))

    e_tiles = pl.cdiv(vr, SETTLE)
    e_pieces = min(2, e_tiles)
    e_bounds = [e_tiles * i // e_pieces for i in range(e_pieces + 1)]
    extra = 0.0
    for i in range(e_pieces):
        *held, part = embed_pass(
            clip, row_count.reshape(1), row_ids, grad_rows, first_tables, second_tables, base_step, held,
            terms[min(i, pieces - 1)][3], e_bounds[i], e_bounds[i + 1] - e_bounds[i],
        )
        extra = extra + part
    one_tables, two_tables = held
    coded = jnp.concatenate([(row_ids + LANES) // LANES, (row_ids + LANES) % LANES])
    coded = jnp.broadcast_to(coded.astype(BF).reshape(1, -1, LANES), (reps, n_slots // 64, LANES))
    extra = jnp.concatenate([extra.astype(BF), coded], axis=1)
    extra = lax.all_to_all(extra, "rep", 0, 0, tiled=True)
    coded = extra[:, n_slots:].reshape(reps, 2, n_slots).astype(jnp.int32)
    coded = coded[:, 0] * LANES + coded[:, 1] - LANES
    counts = jnp.sum((coded >= 0).astype(jnp.int32), axis=1)

    kv_grad = lax.dynamic_slice_in_dim(kv_total, w * own_rows, own_rows, axis=0)
    sm_one, sm_two, sm_step = moments_step(
        grad_small * clip_factor, first_gains[0], second_gains[0]
    )
    pack_rows = own_rows * (2 * L + 2 * L * (FF // BLOCKS // LANES) + 1)
    att_one, att_two, ff_one, ff_two, kv_one, kv_two, packed = call(
        layers_kernel,
        [shaped(*first_attention.shape)] * 2
        + [shaped(*first_feedforward.shape)] * 2
        + [shaped(*first_key_value.shape)] * 2
        + [shaped(BLOCKS, pack_rows, LANES, kind=BF)],
        (
            clip, part, wq0, out0, wq1, out1, wide0, wide1, kv_grad, first_attention, second_attention,
            first_feedforward, second_feedforward, first_key_value, second_key_value,
        ),
        smem=1,
        far=(1,),
        name="layers_adam",
    )
    n_small = sm_step.shape[0] // reps
    sm_step = jnp.pad(sm_step.astype(BF).reshape(reps, n_small), ((0, 0), (0, -n_small % 2048)))
    packed = jnp.concatenate([packed, sm_step.reshape(reps, -1, LANES)], axis=1)
    packed = [lax.dynamic_index_in_dim(packed, rep ^ k, 0, False) for k in range(BLOCKS)]
    packed = cross(packed, 0)
    packed = sum(term.astype(F4) for term in packed[:3])

    new_tables = embed_settle(
        reps, counts, coded.reshape(reps, n_slots // GROUP, 1, GROUP), extra, base_sum, tables,
        outer_tables,
    )
    for i in range(pieces):
        new_tables = unembed_settle(
            reps, terms[i][:3], tables, outer_tables, new_tables, i, terms[0][0].shape[0]
        )

    cols = FF // BLOCKS // LANES
    at_ff = 2 * L * own_rows
    at_kv = at_ff + 2 * L * cols * own_rows
    masters = (attention, feedforward, key_value, gains_biases)
    outers = (outer_attention, outer_feedforward, outer_key_value, outer_gains)
    sums = (
        packed[:at_ff].reshape(L, 2, own_rows, LANES),
        packed[at_ff:at_kv]
        .reshape(L, 2, cols, own_rows, LANES)
        .transpose(0, 1, 3, 2, 4)
        .reshape(feedforward.shape),
        packed[at_kv : at_kv + own_rows, : LANES // BLOCKS],
        packed[pack_rows:].reshape(-1)[:n_small],
    )
    stepped = [new_tables] + [
        settle(sums[i], masters[i], outers[i], LEARN_RATES[i + 1], reps) for i in range(4)
    ]
    return (
        loss_sum.reshape(1),
        count.reshape(1),
        *[pair[0] for pair in stepped],
        one_tables,
        att_one,
        ff_one,
        kv_one,
        sm_one[None],
        two_tables,
        att_two,
        ff_two,
        kv_two,
        sm_two[None],
        *[pair[1] for pair in stepped],
    )


def solution(mesh):
    split = (
        P(None, WIDE_AXES, "rep"),
        P(None, None, WIDE_AXES, "rep"),
        P(None, None, WIDE_AXES, "rep"),
        P(WIDE_AXES, "rep"),
        P("rep"),
    )
    moments = (
        P("rep", None, WIDE_AXES, None),
        P("rep", None, None, WIDE_AXES, None),
        P("rep", None, None, WIDE_AXES, None),
        P("rep", WIDE_AXES, None),
        P("rep", None),
    )
    tokens = P("rep", None, None, None, None)
    parted = mesh.devices.reshape(mesh.shape["rep"], mesh.shape["wide"] // 2, 2)
    return jax.shard_map(
        body,
        mesh=Mesh(parted, ("rep",) + WIDE_AXES),
        in_specs=(tokens,) * 3 + split + moments + moments + split,
        out_specs=(P("rep"), P("rep")) + split + moments + moments + split,
        check_vma=False,
    )
```

```python
from functools import partial

import jax
import jax.numpy as jnp
from jax import lax
from jax.experimental import pallas as pl
from jax.experimental.pallas import tpu as pltpu
from jax.sharding import Mesh
from jax.sharding import PartitionSpec as P

D = 512
HEADS = 8
HD = 64
ROT = 16
FF = 2048
L = 2
LEN = 2048
MICRO = 2
STEP = 5
WIDE_AXES = ("chip", "core")

NORM_EPSILON = 1e-05
CLIP = 0.1
LEARN_RATES = (0.02, 0.2, 0.02, 0.02, 0.2)
BETA_ONE = 0.9
BETA_TWO = 0.95
ADAM_EPSILON = 1e-08
DECAY = 0.1
OUTER_RATE = 0.7
OUTER_MOMENTUM = 0.9
FIX_ONE = 1.0 / (1.0 - BETA_ONE**STEP)
FIX_TWO = 1.0 / (1.0 - BETA_TWO**STEP)

BF = jnp.bfloat16
F4 = jnp.float32


def dot(left, right, dims):
    return lax.dot_general(left, right, (dims, ((), ())), preferred_element_type=F4)


def normal_of(stream):
    centred = stream - jnp.mean(stream, axis=-1, keepdims=True)
    scale = lax.rsqrt(jnp.mean(centred * centred, axis=-1, keepdims=True) + NORM_EPSILON)
    return centred * scale, scale


def norm_pull(shaped, normal, scale):
    return scale * (
        shaped
        - jnp.mean(shaped, axis=-1, keepdims=True)
        - normal * jnp.mean(shaped * normal, axis=-1, keepdims=True)
    )


def rotary(places):
    frequency = 10000.0 ** (-2.0 * jnp.arange(ROT // 2, dtype=F4) / ROT)
    angles = places.astype(F4)[:, None] * frequency[None, :]
    return jnp.cos(angles), jnp.sin(angles)


def rotate(values, cosine, sine):
    half = ROT // 2
    a = values[..., :half]
    b = values[..., half:ROT]
    c = cosine[:, None, :]
    s = sine[:, None, :]
    return jnp.concatenate([a * c - b * s, b * c + a * s, values[..., ROT:]], axis=-1)


def unpack_small(gains_biases):
    span = 7 * D + FF
    layers = gains_biases[: L * span].reshape(L, span)
    remain = gains_biases[L * span :]
    return layers, remain[: 2 * HD], remain[2 * HD : 2 * HD + D], remain[2 * HD + D :]


def moments_step(gradient, one, two):
    one = BETA_ONE * one + (1.0 - BETA_ONE) * gradient
    two = BETA_TWO * two + (1.0 - BETA_TWO) * gradient * gradient
    return one, two, (one * FIX_ONE) / (jnp.sqrt(two * FIX_TWO) + ADAM_EPSILON)


def step_of(one, two):
    two = two * FIX_TWO
    under = two * lax.rsqrt(jnp.maximum(two, 1e-37)) + ADAM_EPSILON
    guess = pl.reciprocal(under, approx=True)
    return one * FIX_ONE * (guess * (2.0 - under * guess))


def moments_fast(gradient, one, two):
    one = BETA_ONE * one + (1.0 - BETA_ONE) * gradient
    two = BETA_TWO * two + (1.0 - BETA_TWO) * gradient * gradient
    return one, two, step_of(one, two)


VM = pl.BlockSpec(memory_space=pltpu.VMEM)
SM = pl.BlockSpec(memory_space=pltpu.SMEM)
LANES = 128
BLOCKS = D // LANES
ROWS = 64
RUN = 2096
SPREAD = 4
FAR = 1 << 24


def shaped(*dims, kind=F4):
    return jax.ShapeDtypeStruct(dims, kind)


def takes(micros):
    return pl.CostEstimate(flops=0, bytes_accessed=int(micros * 3e6), transcendentals=0)


def call(kernel, outs, ins, smem=0, scratch=(), out_specs=None, name=None, room=63, far=(), cost=5):
    return pl.pallas_call(
        kernel,
        out_shape=outs,
        in_specs=[SM if i < smem else ANY if i in far else VM for i in range(len(ins))],
        out_specs=[VM] * len(outs) if out_specs is None else out_specs,
        scratch_shapes=list(scratch),
        compiler_params=pltpu.CompilerParams(vmem_limit_bytes=room * 1024 * 1024),
        name=name,
        cost_estimate=takes(cost),
    )(*ins)


ANY = pl.BlockSpec(memory_space=pltpu.HBM)
ATT = L * 2 * LANES
WIDE = 2 * FF // BLOCKS


class Fetch:
    def __init__(self, sc_ref, weights, scr, sems, start):
        w, rep = sc_ref[0], sc_ref[2]
        cols = pl.ds(start, scr.shape[2])
        self.copies = []
        for core in range(2):
            mine = weights[5 * core : 5 * core + 5]
            spots = [(mine[k], k, i, i) for k in range(3) for i in range(mine[0].shape[0])]
            cut = mine[3].shape[0]
            spots += [(mine[3], 3, i, i) for i in range(cut)]
            spots += [(mine[4], 3, i, i + cut) for i in range(mine[4].shape[0])]
            for ref, k, i, chip in spots:
                own_rows = ref.shape[1]
                at = pl.multiple_of((w ^ (2 * chip + core)) * own_rows, own_rows)
                self.copies.append(
                    pltpu.make_async_copy(
                        ref.at[i, :, cols],
                        scr.at[rep ^ k, pl.ds(at, own_rows), :],
                        sems.at[core, k, chip],
                    )
                )
        for copy in self.copies:
            copy.start()

    def wait(self):
        for copy in self.copies:
            copy.wait()


def nn(left, right):
    return dot(left, right, ((1,), (0,)))


def nt(left, right):
    return dot(left, right, ((1,), (1,)))


def tn(left, right):
    return dot(left, right, ((0,), (0,)))


def split_two(value):
    high = value.astype(BF)
    return high, (value - high.astype(F4)).astype(BF)


def lanes_of(rows):
    return lax.broadcasted_iota(jnp.int32, (rows, LANES), 1)


def spin(value, cosine, sine):
    place = lanes_of(value.shape[0]) % HD
    ahead = pltpu.roll(value, LANES - ROT // 2, 1)
    behind = pltpu.roll(value, ROT // 2, 1)
    moved = jnp.where(place < ROT // 2, -ahead, behind)
    return value * cosine + moved * sine


def swap_halves(value):
    return pltpu.roll(value, HD, 1)


def blocks_of(value):
    return [value[:, LANES * i : LANES * (i + 1)] for i in range(value.shape[1] // LANES)]


def tile_of(vr):
    return 2096 if vr % 2096 == 0 else vr


def stack_kernel(*refs):
    for i, ref in enumerate(refs[:-1]):
        refs[-1][i] = ref[...]


def lower_ones(size):
    first = lax.broadcasted_iota(jnp.int32, (size, size), 0)
    second = lax.broadcasted_iota(jnp.int32, (size, size), 1)
    return jnp.where(first <= second, 1.0, 0.0).astype(BF)


def rows_of(values, block):
    rows = [jnp.broadcast_to(value, (1, block)) for value in values]
    rows.append(jnp.zeros((8 - len(rows), block), F4))
    return jnp.concatenate(rows, axis=0).astype(BF)


def code_of(place, mb, width, seqs, rows_seq):
    m, b = lax.div(mb, width), lax.rem(mb, width)
    code = m * (seqs * LEN) + b * rows_seq
    return code + lax.div(place, rows_seq) * LEN + lax.rem(place, rows_seq)


def slots_kernel(
    seqs, rows_seq, vr, cap, sc_ref, own_all, x_all, y_all, d_all, ids_ref, code_ref, own_ref, rest_ref,
    all_ref,
):
    for k, ref in enumerate((own_all, x_all, y_all, d_all)):
        all_ref[k] = ref[...]
    groups = all_ref.shape[0]
    micros_width = ids_ref.shape[1] * LANES // cap
    block = all_ref.shape[2]
    width = micros_width // MICRO
    offset = sc_ref[3].astype(F4)
    per = LANES // cap
    lower = lower_ones(block)
    slot = lax.broadcasted_iota(jnp.int32, (LANES, 1), 0)
    wanted = (slot % cap).astype(F4)
    lane = lax.broadcasted_iota(jnp.int32, (1, LANES), 1)
    place = lax.broadcasted_iota(jnp.int32, (1, block), 1).astype(F4)

    def one(g, carry):
        local = all_ref[g, :micros_width, :] - offset
        inside = (local >= 0.0) & (local < vr)
        rank = nn(jnp.where(inside, 1.0, 0.0).astype(BF), lower) - 1.0
        rank = jnp.where(inside, rank, -1.0)
        local = jnp.where(inside, local, 0.0)
        high = jnp.floor(local * (1.0 / 64.0))
        for row in range(ids_ref.shape[1]):
            total = jnp.zeros((8, LANES), F4)
            for i in range(per):
                mb = row * per + i
                one_row = slice(mb, mb + 1)
                hot = (rank[one_row] == wanted) & (slot // cap == i)
                values = rows_of(
                    (high[one_row], local[one_row] - 64.0 * high[one_row], place, jnp.ones((1, 1), F4)),
                    block,
                )
                total = total + nt(values, jnp.where(hot, 1.0, 0.0).astype(BF))
            ids = (total[0:1] * 64.0 + total[1:2]).astype(jnp.int32)
            valid = total[3:4] > 0.5
            ids_ref[g, row : row + 1, :] = ids

            @pl.when(g == 0)
            def _():
                code = code_of(
                    total[2:3].astype(jnp.int32), row * per + lane // cap, width, seqs, rows_seq
                )
                code_ref[row : row + 1, :] = jnp.where(valid, code, FAR)
                own_ref[row : row + 1, :] = jnp.where(valid, ids, vr)
        return carry

    lax.fori_loop(0, groups, one, 0)
    for g in range(groups):
        rest_ref[sc_ref[2] ^ g] = all_ref[g, micros_width:, :]


def places_kernel(
    seqs, rows_seq, vr, cap, sc_ref, token_ref, mask_ref, loss_ref, slot_ref, own_ref, row_ref, turn_ref,
    key_out, chip_out, slot_out, row_out, target_out, weight_out, slot_cos, slot_sin, row_cos, row_sin,
):
    many, block = token_ref.shape
    width = many // MICRO
    n_loss = row_ref.shape[1]
    lrows = n_loss // many
    lower = lower_ones(block)
    tokens = token_ref[...]
    shard = jnp.floor((tokens + 0.5) * (1.0 / vr)).astype(jnp.int32) ^ sc_ref[0]
    rank = jnp.zeros((many, block), F4)
    for k in range(width):
        inside = jnp.where(shard == k, 1.0, 0.0)
        rank = rank + inside * (nn(inside.astype(BF), lower) - 1.0)
    spot = shard.astype(F4) * cap + rank
    wanted = lax.broadcasted_iota(jnp.int32, (width * cap, 1), 0).astype(F4)
    place = lax.broadcasted_iota(jnp.int32, (1, block), 1).astype(F4)
    values = rows_of((place, jnp.ones((1, 1), F4)), block)
    for mb in range(many):
        hot = jnp.where(spot[mb : mb + 1] == wanted, 1.0, 0.0).astype(BF)
        total = nt(values, hot)
        code = code_of(total[0:1].astype(jnp.int32), mb, width, seqs, rows_seq)
        code = jnp.where(total[1:2] > 0.5, code, FAR)
        key_out[mb] = code
        chip_out[mb] = code[:, : 2 * cap]
    high = jnp.floor(tokens * (1.0 / 256.0))
    low = tokens - 256.0 * high
    at = lax.broadcasted_iota(jnp.int32, (block, 1), 0)
    lane = lax.broadcasted_iota(jnp.int32, (1, LANES), 1)
    per = LANES // lrows
    for row in range(n_loss // LANES):
        codes = loss_ref[row : row + 1, :]
        after = lax.div(codes, rows_seq - 1) * rows_seq + lax.rem(codes, rows_seq - 1) + 1
        total = jnp.zeros((8, LANES), F4)
        for i in range(per):
            mb = slice(row * per + i, row * per + i + 1)
            hot = (at == after) & (lane // lrows == i)
            total = total + nn(
                rows_of((high[mb], low[mb], mask_ref[mb, :]), block),
                jnp.where(hot, 1.0, 0.0).astype(BF),
            )
        part = slice(LANES * row, LANES * (row + 1))
        target_out[0:1, part] = (total[0:1] * 256.0 + total[1:2]).astype(jnp.int32)
        weight_out[0:1, part] = total[2:3]

    def column(row):
        return jnp.transpose(jnp.broadcast_to(row, (LANES, LANES)))[:, 0:1]

    n_slots = slot_out.shape[0]
    ones = jnp.ones((HD - ROT, LANES), F4)
    zeros = jnp.zeros((HD - ROT, LANES), F4)
    ends = (jnp.ones((HD, LANES), F4), jnp.zeros((HD, LANES), F4))
    for start in range(0, n_slots + n_loss, LANES):
        slots = start < n_slots
        into = start if slots else start - n_slots
        part = slice(into, into + LANES)
        cosine = turn_ref[0:8, start : start + LANES]
        sine = turn_ref[8:16, start : start + LANES]
        cosines = [cosine, cosine, ones]
        sines = [sine, sine, zeros]
        cosines, sines = (
            (cosines + [ends[0]], sines + [ends[1]]) if slots else (cosines * 2, sines * 2)
        )
        cos_out, sin_out = (slot_cos, slot_sin) if slots else (row_cos, row_sin)
        cos_out[part, :] = jnp.transpose(jnp.concatenate(cosines, axis=0))
        sin_out[part, :] = jnp.transpose(jnp.concatenate(sines, axis=0))
        if slots:
            i = start // LANES
            slot_out[part, 0:1] = column(slot_ref[i : i + 1, :].astype(F4)).astype(jnp.int32)
            slot_out[part, 1:2] = column(own_ref[i : i + 1, :].astype(F4)).astype(jnp.int32)
        else:
            code = row_ref[0:1, part]
            row_out[part, 0:1] = column(code.astype(F4)).astype(jnp.int32)
            row_out[part, 1:2] = column((lax.div(code, LEN) * LEN).astype(F4)).astype(jnp.int32)


def kv_kernel(
    sc_ref, r0, r1, r2, r3, cos_ref, sin_ref, vec_ref, pair_bias_ref, slot_code_ref, row_ref, *refs
):
    pairs_ref, picked_ref, kv_ref, rows_ref = refs[-4:]
    n_slots = rows_ref.shape[1]
    for k, piece in enumerate((r0, r1, r2, r3)):
        rows_ref[sc_ref[2] ^ k] = piece[...]
    for k, piece in enumerate(refs[:-4]):
        own = piece.shape[0]
        kv_ref[pl.ds(pl.multiple_of((sc_ref[0] ^ k) * own, own), own), :] = piece[...]
    step = 256
    for start in range(0, n_slots, step):
        part = pl.ds(start, step)
        rows = jnp.concatenate([rows_ref[r, part, :] for r in range(BLOCKS)], axis=1)
        normal, unused = normal_of(rows.astype(F4))
        normed = (normal * vec_ref[0:1, :D] + vec_ref[0:1, D : 2 * D]).astype(BF)
        projected = pair_bias_ref[...] + nn(normed, kv_ref[...])
        pairs_ref[part, :] = spin(projected, cos_ref[part, :], sin_ref[part, :]).astype(BF)
    rows = jnp.concatenate([rows_ref[r] for r in range(BLOCKS)], axis=1)
    pick = jnp.where(row_ref[:, 0:1] == slot_code_ref[...], 1.0, 0.0).astype(BF)
    for r in range(BLOCKS):
        picked_ref[r] = nn(pick, rows[:, LANES * r : LANES * (r + 1)]).astype(BF)


def token_codes(place, m, first_block, seqs, rows_seq):
    block = seqs * rows_seq
    inside = lax.rem(place, block)
    code = m * (seqs * LEN) + (first_block + lax.div(place, block)) * rows_seq
    return code + lax.div(inside, rows_seq) * LEN + lax.rem(inside, rows_seq)


def order_kernel(seqs, rows_seq, width, cap, sc_ref, after_ref, code_ref, *refs):
    pieces, out_ref, stream_ref = refs[:-2], refs[-2], refs[-1]
    n_loss = stream_ref.shape[1]
    n_slots = MICRO * width * cap
    for core in range(2):
        for i in range(2):
            part = slice(n_slots + n_loss * i, n_slots + n_loss * (i + 1))
            total = pieces[core][part, :].astype(F4)
            for piece in pieces[core + 2 :: 2]:
                total = total + piece[part, :].astype(F4)
            stream_ref[2 * (sc_ref[1] ^ core) + i] = total
    block = seqs * rows_seq

    def one(mb, carry):
        m, b = lax.div(mb, width), lax.rem(mb, width)
        part = pl.ds(pl.multiple_of(mb * cap, cap), cap)
        slots = jnp.concatenate([piece[part, :] for piece in pieces], axis=0)
        place = lax.broadcasted_iota(jnp.int32, (block, 1), 0)
        hot = token_codes(place, m, b, seqs, rows_seq) == code_ref[mb]
        out_ref[mb] = nn(jnp.where(hot, 1.0, 0.0).astype(BF), slots).astype(BF)
        return carry

    lax.fori_loop(0, MICRO * width, one, 0)


def stack_heads(block_of, part):
    low_lanes = lanes_of(ROWS) < HD
    pieces = []
    for b in range(2):
        block = block_of[b, part, :]
        pieces += [block, swap_halves(block)]
    return [jnp.where(low_lanes, piece, 0.0) for piece in pieces]


def masks_of(row_ref, part, m, kt, tile, seqs, rows_seq):
    place = lax.broadcasted_iota(jnp.int32, (1, tile), 1)
    code = token_codes(place, m, kt * SPREAD, seqs, rows_seq)
    allowed = code <= row_ref[part, 0:1]
    if seqs > 1:
        allowed = allowed & (code >= row_ref[part, 1:2])
    return allowed


def masked(scores, allowed):
    return jnp.concatenate(
        [
            jnp.where(allowed, scores[ROWS * h : ROWS * (h + 1), :], -1e30)
            for h in range(HEADS // 2)
        ],
        axis=0,
    )


def attend(q_scr, ctx_ref, log_ref, keys_ref, row_ref, scr, seqs, rows_seq):
    micros, tiles, tile, unused = keys_ref.shape
    low_lanes = lanes_of(ROWS) < HD
    high = ROWS * HEADS // 2

    def one(t, carry):
        m, c = lax.div(t, tiles), lax.rem(t, tiles)
        part = pl.ds(pl.multiple_of(t * ROWS, ROWS), ROWS)
        query = jnp.concatenate(stack_heads(q_scr, part), axis=0).astype(BF)

        def scores_at(kt, top):
            allowed = masks_of(row_ref, part, m, kt, tile, seqs, rows_seq)
            scores = masked(nt(query, keys_ref[m, kt]), allowed)
            scr[kt] = scores
            for piece in blocks_of(scores):
                top = jnp.maximum(top, piece)
            return top

        top = lax.fori_loop(0, c + 1, scores_at, jnp.full((high, LANES), -1e30, F4))
        top = jnp.max(top, axis=1, keepdims=True)

        def expo_at(kt, total):
            expo = jnp.exp(scr[kt] - top)
            scr[kt] = expo
            for piece in blocks_of(expo):
                total = total + piece
            return total

        total = lax.fori_loop(0, c + 1, expo_at, jnp.zeros((high, LANES), F4))
        total = jnp.sum(total, axis=1, keepdims=True)
        inverse = 1.0 / total

        def context_at(kt, so_far):
            return so_far + nn((scr[kt] * inverse).astype(BF), keys_ref[m, kt])

        context = lax.fori_loop(0, c + 1, context_at, jnp.zeros((high, LANES), F4))
        log_ref[t] = top + jnp.log(total)
        heads = [context[ROWS * h : ROWS * (h + 1), :] for h in range(HEADS // 2)]
        for b in range(2):
            ctx_ref[b, part, :] = jnp.where(
                low_lanes, swap_halves(heads[2 * b]), heads[2 * b + 1]
            )
        return carry

    lax.fori_loop(0, micros * tiles, one, 0)


def attend_pull(
    q_ref, ctx_ref, grad_scr, log_ref, keys_ref, row_ref, dq_ref, dkv_ref, seqs, rows_seq
):
    micros, tiles, tile, unused = keys_ref.shape
    low_lanes = lanes_of(ROWS) < HD
    high = ROWS * HEADS // 2

    def one(t, carry):
        m, c = lax.div(t, tiles), lax.rem(t, tiles)
        part = pl.ds(pl.multiple_of(t * ROWS, ROWS), ROWS)
        query = jnp.concatenate(stack_heads(q_ref, part), axis=0).astype(BF)
        grads = []
        inners = []
        for b in range(2):
            grad = grad_scr[b, part, :]
            product = grad * ctx_ref[b, part, :]
            for sub in range(2):
                moved = swap_halves(grad) if sub == 0 else grad
                grads.append(jnp.where(low_lanes, 0.0, moved))
                mine = low_lanes if sub == 0 else ~low_lanes
                inners.append(jnp.sum(jnp.where(mine, product, 0.0), axis=1, keepdims=True))
        grad = jnp.concatenate(grads, axis=0).astype(BF)
        inner = jnp.concatenate(inners, axis=0)
        log_total = log_ref[t]

        def pull_at(kt, so_far):
            both = keys_ref[m, kt]
            allowed = masks_of(row_ref, part, m, kt, tile, seqs, rows_seq)
            probs = jnp.exp(masked(nt(query, both), allowed) - log_total)
            grad_scores = (probs * (nt(grad, both) - inner)).astype(BF)
            dkv_ref[m, kt] += tn(grad_scores, query) + tn(probs.astype(BF), grad)
            return so_far + nn(grad_scores, both)

        total = lax.fori_loop(0, c + 1, pull_at, jnp.zeros((high, LANES), F4)) * 0.125
        heads = [total[ROWS * h : ROWS * (h + 1), :] for h in range(HEADS // 2)]
        for b in range(2):
            dq_ref[b, part, :] = jnp.where(
                low_lanes, heads[2 * b], swap_halves(heads[2 * b + 1])
            ).astype(BF)
        return carry

    lax.fori_loop(0, micros * tiles, one, 0)


def to_slots(dkv_ref, code_ref, own_out, near_out, seqs, rows_seq):
    micros, tiles, tile, unused = dkv_ref.shape
    block = seqs * rows_seq
    width = tiles * SPREAD
    cap = own_out.shape[0] // (micros * width)

    def one(mb, carry):
        m, b = lax.div(mb, width), lax.rem(mb, width)
        part = pl.ds(pl.multiple_of(mb * cap, cap), cap)
        inside = pl.ds(pl.multiple_of(lax.rem(b, SPREAD) * block, block), block)
        high, rest = split_two(dkv_ref[m, lax.div(b, SPREAD), inside, :])
        place = lax.broadcasted_iota(jnp.int32, (block, 1), 0)
        code = token_codes(place, m, b, seqs, rows_seq)
        hot = jnp.where(code == code_ref[mb], 1.0, 0.0).astype(BF)
        both = tn(hot, high) + tn(hot, rest)
        own_out[part, :] = both[:cap, :]
        near_out[part, :] = both[cap:, :]
        return carry

    lax.fori_loop(0, micros * width, one, 0)


def join_blocks(parity, own_ref, other_ref):
    return [
        jnp.where(parity == r // 2, own_ref[r % 2].astype(F4), other_ref[r % 2].astype(F4))
        for r in range(BLOCKS)
    ]


def branch_of(parity, k, own_ref, other_ref, att_ref):
    context = jnp.concatenate(join_blocks(parity, own_ref, other_ref), axis=1).astype(BF)
    at = k * 256 + LANES
    return jnp.concatenate(
        [nn(context, att_ref[r, :, at : at + LANES]) for r in range(BLOCKS)], axis=1
    )


def queries_of(k, stream, parity, vec_ref, att_ref, cos_ref, sin_ref, q_ref):
    normal, unused = normal_of(stream)
    normed = (normal * vec_ref[0:1, :D] + vec_ref[0:1, D : 2 * D]).astype(BF)
    cosine, sine = cos_ref[...], sin_ref[...]
    for i in range(2):
        weight = jnp.where(
            parity == 0,
            att_ref[i, :, k * 256 : k * 256 + LANES],
            att_ref[2 + i, :, k * 256 : k * 256 + LANES],
        )
        low = vec_ref[0:1, 4 * D + LANES * i : 4 * D + LANES * (i + 1)]
        high = vec_ref[0:1, 4 * D + LANES * (2 + i) : 4 * D + LANES * (3 + i)]
        query = nn(normed, weight) + jnp.where(parity == 0, low, high)
        query = spin(query, cosine, sine).astype(BF).astype(F4)
        q_ref[i] = query * 0.125


def first_kernel(
    seqs, rows_seq, sc_ref, low_ref, vec_ref, w0, w1, w2, w3, w4, w5, w6, w7, w8, w9, keys_ref, row_ref, cos_ref, sin_ref,
    stream_ref, q_ref, ctx_ref, log_ref, scr, att_ref, sem,
):
    copy = Fetch(sc_ref, (w0, w1, w2, w3, w4, w5, w6, w7, w8, w9), att_ref, sem, L * WIDE)
    stream_ref[...] = jnp.concatenate([low_ref[r] for r in range(BLOCKS)], axis=1)
    copy.wait()
    queries_of(0, stream_ref[...], sc_ref[1], vec_ref, att_ref, cos_ref, sin_ref, q_ref)
    attend(q_ref, ctx_ref, log_ref, keys_ref, row_ref, scr, seqs, rows_seq)


def second_kernel(
    seqs, rows_seq, sc_ref, partial_ref, own_ref, other_ref, vec_ref, w0, w1, w2, w3, w4, w5, w6, w7, w8, w9, keys_ref, row_ref,
    cos_ref, sin_ref, stream_ref, q_ref, ctx_ref, log_ref, scr, att_ref, sem,
):
    parity = sc_ref[1]
    Fetch(sc_ref, (w0, w1, w2, w3, w4, w5, w6, w7, w8, w9), att_ref, sem, L * WIDE).wait()
    stream_ref[...] = partial_ref[...] + branch_of(parity, 0, own_ref, other_ref, att_ref)
    queries_of(1, stream_ref[...], parity, vec_ref, att_ref, cos_ref, sin_ref, q_ref)
    attend(q_ref, ctx_ref, log_ref, keys_ref, row_ref, scr, seqs, rows_seq)


ROOT_HALF = 0.7071067811865476
ROOT_TAU = 0.3989422804014327


def feed_kernel(k, sc_ref, stream_ref, vec_ref, w0, w1, w2, w3, w4, w5, w6, w7, w8, w9, out_ref, ff_ref, sem):
    copy = Fetch(sc_ref, (w0, w1, w2, w3, w4, w5, w6, w7, w8, w9), ff_ref, sem, k * WIDE)
    stream = stream_ref[...]
    normal, unused = normal_of(stream)
    feed = (normal * vec_ref[0:1, 2 * D : 3 * D] + vec_ref[0:1, 3 * D : 4 * D]).astype(BF)
    total = stream + vec_ref[0:1, 5 * D : 6 * D] + vec_ref[0:1, 6 * D : 7 * D]
    cols = FF // BLOCKS
    copy.wait()
    for r in range(BLOCKS):
        at_r = 7 * D + cols * r
        hidden = nn(feed, ff_ref[r, :, :cols]) + vec_ref[0:1, at_r : at_r + cols]
        active = (0.5 * hidden * (1.0 + lax.erf(hidden * ROOT_HALF))).astype(BF)
        total = total + nt(active, ff_ref[r, :, cols:])
    out_ref[...] = total


def runs_of(tables_ref):
    vr = tables_ref.shape[1]
    step = RUN if vr % RUN == 0 else vr
    for start in range(0, vr, step):
        part = slice(start, start + step)
        yield start, step, jnp.concatenate([tables_ref[r, part, :] for r in range(BLOCKS)], axis=1)


def logits_kernel(
    sc_ref, partial_ref, own_ref, other_ref, w0, w1, w2, w3, w4, w5, w6, w7, w8, w9, final_ref, target_ref, tables_ref,
    logits_ref, stats_ref, stream_ref, picked_ref, att_ref, sem,
):
    parity, offset = sc_ref[1], sc_ref[3]
    Fetch(sc_ref, (w0, w1, w2, w3, w4, w5, w6, w7, w8, w9), att_ref, sem, L * WIDE).wait()
    stream = partial_ref[...] + branch_of(parity, 1, own_ref, other_ref, att_ref)
    stream_ref[...] = stream
    normal, unused = normal_of(stream)
    picked = (normal * final_ref[0:1, :] + final_ref[1:2, :]).astype(BF)
    picked_ref[...] = picked
    n_loss = picked.shape[0]
    top = jnp.full((1, n_loss), -1e30, F4)
    hit_total = jnp.zeros((1, n_loss), F4)
    target = target_ref[...] - offset
    for start, size, table in runs_of(tables_ref):
        logits = nt(table, picked)
        logits_ref[start : start + size, :] = logits
        top = jnp.maximum(top, jnp.max(logits, axis=0, keepdims=True))
        place = lax.broadcasted_iota(jnp.int32, (size, n_loss), 0) + start
        hit_total = hit_total + jnp.sum(
            jnp.where(place == target, logits, 0.0), axis=0, keepdims=True
        )
    total = jnp.zeros((1, n_loss), F4)
    step = tile_of(logits_ref.shape[0])
    for start in range(0, logits_ref.shape[0], step):
        total = total + jnp.sum(
            jnp.exp(logits_ref[start : start + step, :] - top), axis=0, keepdims=True
        )
    stats_ref[0:1, :] = top
    stats_ref[1:2, :] = total
    stats_ref[2:3, :] = hit_total
    stats_ref[3:8, :] = jnp.zeros((5, n_loss), F4)


def join_stats(one, two):
    top = jnp.maximum(one[0], two[0])
    total = one[1] * jnp.exp(one[0] - top) + two[1] * jnp.exp(two[0] - top)
    return top, total, one[2] + two[2]


def probs_kernel(
    sc_ref, stats_ref, weight_ref, target_ref, logits_ref, tables_ref, probs_ref, grad_ref,
    loss_ref,
):
    offset = sc_ref[3]
    vr, n_loss = logits_ref.shape
    parts = [tuple(stats_ref[k, i : i + 1, :] for i in range(3)) for k in range(stats_ref.shape[0])]
    while len(parts) > 1:
        parts = [join_stats(parts[i], parts[i + 1]) for i in range(0, len(parts), 2)]
    top, total, hit = parts[0]
    log_all = top + jnp.log(total)
    weight = weight_ref[...]
    loss_ref[0, 0] = jnp.sum(weight * (log_all - hit))
    share = weight / jnp.sum(weight)
    target = target_ref[...] - offset
    grads = jnp.zeros((n_loss, D), F4)
    for start, size, table in runs_of(tables_ref):
        place = lax.broadcasted_iota(jnp.int32, (size, n_loss), 0) + start
        probs = jnp.exp(logits_ref[start : start + size, :] - log_all)
        probs = (jnp.where(place == target, probs - 1.0, probs) * share).astype(BF)
        probs_ref[start : start + size, :] = probs
        grads = grads + tn(probs, table)
    for r in range(BLOCKS):
        grad_ref[r] = grads[:, LANES * r : LANES * (r + 1)]


def squares_kernel(probs_ref, picked_ref, out_ref):
    vr = probs_ref.shape[0]
    tile = tile_of(vr)
    total = jnp.zeros((), F4)
    for start in range(0, vr, tile):
        grads = nn(probs_ref[start : start + tile, :], picked_ref[...])
        total = total + jnp.sum(grads * grads)
    out_ref[0, 0] = total


def layer_pull(
    k, seqs, rows_seq, sc_ref, grad_stream, stream, vec_ref, att_ref, ff_ref, copy, own_ref, other_ref, q_ref,
    log_ref, keys_ref, row_ref, dq_ref, dkv_ref, wide_ref, out_ref, vec_out,
    feed_scr, low_scr, grad_scr, prod_scr, square,
):
    parity = sc_ref[1]
    block, place = sc_ref[4], sc_ref[5]
    rows = wide_ref.shape[1]
    cols = FF // BLOCKS
    normal, unused = normal_of(stream)
    feed = (normal * vec_ref[0:1, 2 * D : 3 * D] + vec_ref[0:1, 3 * D : 4 * D]).astype(BF)
    low = grad_stream.astype(BF)
    for r in range(BLOCKS):
        feed_scr[r] = feed[:, LANES * r : LANES * (r + 1)]
        low_scr[r] = low[:, LANES * r : LANES * (r + 1)]
    feed_own = feed_scr[block]
    low_own = low_scr[block]

    at = k * 256 + LANES
    half = D // 2
    start = pl.ds(pl.multiple_of(parity * half, half), half)
    grad_context = nt(low_scr[0], att_ref[0, start, at : at + LANES])
    for r in range(1, BLOCKS):
        grad_context = grad_context + nt(low_scr[r], att_ref[r, start, at : at + LANES])
    grad_context = grad_context.astype(BF).astype(F4)
    grad_scr[0] = grad_context[:, :LANES]
    grad_scr[1] = grad_context[:, LANES:]
    attend_pull(
        q_ref, own_ref, grad_scr, log_ref, keys_ref, row_ref, dq_ref, dkv_ref, seqs,
        rows_seq,
    )

    vec_out[0:1, 5 * D : 6 * D] = jnp.sum(low.astype(F4), axis=0, keepdims=True)
    vec_out[0:1, 6 * D : 7 * D] = jnp.sum(low.astype(F4), axis=0, keepdims=True)
    grad_feed = jnp.zeros_like(grad_stream)
    copy.wait()
    for r in range(BLOCKS):
        at_r = 7 * D + cols * r
        hidden = nn(feed, ff_ref[r, :, :cols]) + vec_ref[0:1, at_r : at_r + cols]
        grown = 1.0 + lax.erf(hidden * ROOT_HALF)
        active = (0.5 * hidden * grown).astype(BF)
        slope = 0.5 * grown + hidden * (ROOT_TAU * jnp.exp(-0.5 * hidden * hidden))
        grad_hidden = (nn(low, ff_ref[r, :, cols:]) * slope).astype(BF)
        grad_feed = grad_feed + nt(grad_hidden, ff_ref[r, :, :cols])
        vec_out[0:1, at_r : at_r + cols] = jnp.sum(
            grad_hidden.astype(F4), axis=0, keepdims=True
        )
        for which, product in enumerate((tn(feed_own, grad_hidden), tn(low_own, active))):
            prod_scr[...] = product
            piece = prod_scr[pl.ds(pl.multiple_of(place, 16), rows), :]
            wide_ref[which, :, cols * r : cols * (r + 1)] = piece
            square = square + jnp.sum(piece * piece)
    blocks = join_blocks(parity, own_ref, other_ref)
    context_own = blocks[0]
    for r in range(1, BLOCKS):
        context_own = jnp.where(block == r, blocks[r], context_own)
    prod_scr[...] = tn(context_own.astype(BF), low)
    piece = prod_scr[pl.ds(pl.multiple_of(place, 16), rows), :]
    out_ref[...] = piece
    square = square + jnp.sum(piece * piece)
    vec_out[0:1, 2 * D : 3 * D] = jnp.sum(grad_feed * normal, axis=0, keepdims=True)
    vec_out[0:1, 3 * D : 4 * D] = jnp.sum(grad_feed, axis=0, keepdims=True)
    return grad_feed, square


def query_pull(
    k, sc_ref, stream, grad_feed, own_ref, other_ref, vec_ref, att_ref, cos_ref, sin_ref, wq_ref,
    head_out, normed_scr, prod_scr, square,
):
    parity = sc_ref[1]
    block, place = sc_ref[4], sc_ref[5]
    rows = wq_ref.shape[0]
    normal, scale = normal_of(stream)
    normed = (normal * vec_ref[0:1, :D] + vec_ref[0:1, D : 2 * D]).astype(BF)
    for r in range(BLOCKS):
        normed_scr[r] = normed[:, LANES * r : LANES * (r + 1)]
    cosine, sine = cos_ref[...], sin_ref[...]
    grad_normed = jnp.zeros_like(stream)
    pieces = []
    for r, part in enumerate(join_blocks(parity, own_ref, other_ref)):
        piece = spin(part.astype(F4), cosine, -sine).astype(BF)
        head_out[0:1, 2 * D + LANES * r : 2 * D + LANES * (r + 1)] = jnp.sum(
            piece.astype(F4), axis=0, keepdims=True
        )
        grad_normed = grad_normed + nt(piece, att_ref[r, :, k * 256 : k * 256 + LANES])
        pieces.append(piece)
    prod_scr[...] = tn(normed_scr[block], jnp.concatenate(pieces, axis=1))
    piece = prod_scr[pl.ds(pl.multiple_of(place, 16), rows), :]
    wq_ref[...] = piece
    square = square + jnp.sum(piece * piece)
    head_out[0:1, :D] = jnp.sum(grad_normed * normal, axis=0, keepdims=True)
    head_out[0:1, D : 2 * D] = jnp.sum(grad_normed, axis=0, keepdims=True)
    shaped_all = grad_normed * vec_ref[0:1, :D] + grad_feed * vec_ref[0:1, 2 * D : 3 * D]
    return norm_pull(shaped_all, normal, scale), square


def last_pull_kernel(
    seqs, rows_seq, sc_ref, before_ref, grads_ref, final_ref, final_stream_ref, stream_ref, vec_ref, w0, w1, w2, w3, w4, w5, w6, w7, w8, w9,
    own_ref, other_ref, q_ref, log_ref, keys_ref, row_ref, dq_ref, dkv_ref,
    wide_ref, out_ref, vec_out, final_out, grad_out, feed_out, square_ref, feed_scr, low_scr,
    grad_scr, prod_scr, att_ref, ff_ref, sems,
):
    att_copy = Fetch(sc_ref, (w0, w1, w2, w3, w4, w5, w6, w7, w8, w9), att_ref, sems.at[0], L * WIDE)
    copy = Fetch(sc_ref, (w0, w1, w2, w3, w4, w5, w6, w7, w8, w9), ff_ref, sems.at[1], WIDE)
    grad_picked = jnp.concatenate([grads_ref[r] for r in range(BLOCKS)], axis=1)
    normal, scale = normal_of(final_stream_ref[...])
    final_out[0:1, :] = jnp.sum(grad_picked * normal, axis=0, keepdims=True)
    final_out[1:2, :] = jnp.sum(grad_picked, axis=0, keepdims=True)
    grad_stream = norm_pull(grad_picked * final_ref[0:1, :], normal, scale)
    grad_out[...] = grad_stream
    dkv_ref[...] = jnp.zeros_like(dkv_ref)
    att_copy.wait()
    grad_feed, square = layer_pull(
        1, seqs, rows_seq, sc_ref, grad_stream, stream_ref[...], vec_ref, att_ref, ff_ref, copy, own_ref,
        other_ref, q_ref, log_ref, keys_ref, row_ref, dq_ref, dkv_ref,
        wide_ref, out_ref, vec_out, feed_scr, low_scr, grad_scr, prod_scr, before_ref[0, 0],
    )
    feed_out[...] = grad_feed
    square_ref[0, 0] = square


def first_pull_kernel(
    seqs, rows_seq, sc_ref, grad_in_ref, feed_in_ref, dq_own_ref, dq_other_ref, stream1_ref, vec1_ref,
    stream_ref, vec_ref, w0, w1, w2, w3, w4, w5, w6, w7, w8, w9, own_ref, other_ref, q_ref, log_ref, keys_ref,
    row_ref, cos_ref, sin_ref, dkv_in_ref, chip_code_ref, dq_ref, own_slots,
    near_slots, wide_ref, out_ref, vec_out, wq_ref, head_out, grad_out, feed_out, square_ref, feed_scr,
    low_scr, grad_scr, prod_scr, dkv_ref, att_ref, ff_ref, sems, dkv_sem,
):
    dkv_copy = pltpu.make_async_copy(dkv_in_ref, dkv_ref, dkv_sem)
    dkv_copy.start()
    att_copy = Fetch(sc_ref, (w0, w1, w2, w3, w4, w5, w6, w7, w8, w9), att_ref, sems.at[0], L * WIDE)
    copy = Fetch(sc_ref, (w0, w1, w2, w3, w4, w5, w6, w7, w8, w9), ff_ref, sems.at[1], 0)
    att_copy.wait()
    grad_part, square = query_pull(
        1, sc_ref, stream1_ref[...], feed_in_ref[...], dq_own_ref, dq_other_ref, vec1_ref, att_ref,
        cos_ref, sin_ref, wq_ref, head_out, feed_scr, prod_scr, jnp.zeros((), F4),
    )
    grad_stream = grad_in_ref[...] + grad_part
    grad_out[...] = grad_stream
    dkv_copy.wait()
    grad_feed, square = layer_pull(
        0, seqs, rows_seq, sc_ref, grad_stream, stream_ref[...], vec_ref, att_ref, ff_ref, copy, own_ref,
        other_ref, q_ref, log_ref, keys_ref, row_ref, dq_ref, dkv_ref,
        wide_ref, out_ref, vec_out, feed_scr, low_scr, grad_scr, prod_scr, square,
    )
    to_slots(dkv_ref, chip_code_ref, own_slots, near_slots, seqs, rows_seq)
    feed_out[...] = grad_feed
    square_ref[0, 0] = square


def embed_pull_kernel(
    sc_ref, grad_in_ref, feed_in_ref, dq_own_ref, dq_other_ref, stream_ref, vec_ref, w0, w1, w2, w3, w4, w5, w6, w7, w8, w9, kv_ref,
    cos_ref, sin_ref, dkv_own_ref, dkv_other_ref, rows_ref, slot_cos_ref, slot_sin_ref,
    slot_ref, row_code_ref, id_row_ref, wq_ref, head_out, rows_out, ids_out,
    kv_out, gain_out, square_ref, count_ref, normed_scr, prod_scr, high_scr, low_scr, att_ref, sem,
):
    Fetch(sc_ref, (w0, w1, w2, w3, w4, w5, w6, w7, w8, w9), att_ref, sem, L * WIDE).wait()
    grad_part, square = query_pull(
        0, sc_ref, stream_ref[...], feed_in_ref[...], dq_own_ref, dq_other_ref, vec_ref, att_ref,
        cos_ref, sin_ref, wq_ref, head_out, normed_scr, prod_scr, jnp.zeros((), F4),
    )
    grad_high, grad_low = split_two(grad_in_ref[...] + grad_part)
    n_slots = rows_ref.shape[1]
    step = 256
    kv_total = jnp.zeros((D, LANES), F4)
    gain_total = jnp.zeros((1, D), F4)
    bias_total = jnp.zeros((1, D), F4)
    pair_total = jnp.zeros((1, LANES), F4)
    gain = vec_ref[0:1, :D]
    for start in range(0, n_slots, step):
        part = pl.ds(start, step)
        real = slot_ref[part, 0:1] < FAR
        grad_pair = dkv_own_ref[part, :] + dkv_other_ref[part, :]
        grad_pair = grad_pair.astype(BF).astype(F4)
        grad_pair = spin(grad_pair, slot_cos_ref[part, :], -slot_sin_ref[part, :])
        grad_pair = jnp.where(real, grad_pair, 0.0).astype(BF)
        rows = jnp.concatenate([rows_ref[r, part, :] for r in range(BLOCKS)], axis=1)
        normal, scale = normal_of(rows.astype(F4))
        normed = (normal * gain + vec_ref[0:1, D : 2 * D]).astype(BF)
        kv_total = kv_total + tn(normed, grad_pair)
        pair_total = pair_total + jnp.sum(grad_pair.astype(F4), axis=0, keepdims=True)
        grad_normed = nt(grad_pair, kv_ref[...])
        gain_total = gain_total + jnp.sum(grad_normed * normal, axis=0, keepdims=True)
        bias_total = bias_total + jnp.sum(grad_normed, axis=0, keepdims=True)
        pick = (slot_ref[part, 0:1] == row_code_ref[...]).astype(F4).astype(BF)
        grad_rows = norm_pull(grad_normed * gain, normal, scale)
        grad_rows = grad_rows + (nn(pick, grad_high) + nn(pick, grad_low))
        grad_rows = jnp.where(real, grad_rows, 0.0)
        high_scr[part, :], low_scr[part, :] = split_two(grad_rows)
    kv_out[...] = kv_total
    gain_out[0:1, :] = gain_total
    gain_out[1:2, :] = bias_total
    gain_out[2:3, :] = jnp.concatenate([pair_total, jnp.zeros((1, D - LANES), F4)], axis=1)
    gain_out[3:8, :] = jnp.zeros((5, D), F4)
    vr = sc_ref[6]
    ids = id_row_ref[...]
    spot = lax.broadcasted_iota(jnp.int32, (1, n_slots), 1)
    later = jnp.zeros((1, n_slots), F4)
    for start in range(0, n_slots, step):
        at = lax.broadcasted_iota(jnp.int32, (step, 1), 0) + start
        same = (slot_ref[pl.ds(start, step), 1:2] == ids) & (at < spot)
        later = jnp.maximum(later, jnp.max(jnp.where(same, 1.0, 0.0), axis=0, keepdims=True))
    lead = jnp.where(ids < vr, 1.0 - later, 0.0)
    rank = jnp.zeros((8, n_slots), F4)
    many = jnp.broadcast_to(lead, (8, n_slots)).astype(BF)
    for start in range(0, n_slots, step):
        before = jnp.where(slot_ref[pl.ds(start, step), 1:2] < ids, 1.0, 0.0).astype(BF)
        rank = rank + nn(many[:, start : start + step], before)
    rank = jnp.where(lead > 0.0, rank[0:1, :].astype(jnp.int32), -1)
    count_ref[0, 0] = jnp.sum(lead).astype(jnp.int32)
    for start in range(0, n_slots, step):
        part = pl.ds(start, step)
        at = lax.broadcasted_iota(jnp.int32, (step, 1), 0) + start
        packed = jnp.max(jnp.where(rank == at, ids, -1), axis=1, keepdims=True)
        ids_out[part, :] = packed
        hot = jnp.where(packed == ids, 1.0, 0.0).astype(BF)
        total = nn(hot, high_scr[...]) + nn(hot, low_scr[...])
        rows_out[part, :] = total.astype(BF)
        square = square + jnp.sum(total * total)
    square_ref[0, 0] = square


TILE = 528
SETTLE = 1056


def params():
    return pltpu.CompilerParams(vmem_limit_bytes=63 * 1024 * 1024)


def base_kernel(first_ref, second_ref, after_ref, step_ref):
    one = BETA_ONE * first_ref[0, 0]
    two = BETA_TWO * second_ref[0, 0]
    step = step_of(one, two)
    for r in range(BLOCKS):
        step_ref[r] = step[:, LANES * r : LANES * (r + 1)].astype(BF)


def base_pass(first, second, after):
    vr = first.shape[2]
    whole = pl.BlockSpec((1, 1, SETTLE, D), lambda i: (0, 0, i, 0))
    return pl.pallas_call(
        base_kernel,
        grid=(pl.cdiv(vr, SETTLE),),
        in_specs=[whole, whole, pl.BlockSpec((16, LANES), lambda i: (0, 0))],
        out_specs=pl.BlockSpec((BLOCKS, SETTLE, LANES), lambda i: (0, i, 0)),
        out_shape=shaped(BLOCKS, vr, LANES, kind=BF),
        compiler_params=params(),
        name="embedding_base",
        cost_estimate=takes(14),
    )(first, second, after)


def unembed_kernel(clip_ref, probs_ref, picked_ref, first_ref, second_ref, *refs):
    one_ref, two_ref, step_ref = refs[-3:]
    gradient = nn(probs_ref[...], picked_ref[...]) * clip_ref[0]
    one, two, step = moments_fast(gradient, first_ref[0, 0], second_ref[0, 0])
    one_ref[0, 0] = one
    two_ref[0, 0] = two
    for r in range(BLOCKS):
        step_ref[r] = step[:, LANES * r : LANES * (r + 1)].astype(BF)


def unembed_pass(clip, probs, picked, first, second, held, start, count):
    vr, n_loss = probs.shape
    rows = min(vr, (start + count) * TILE) - start * TILE
    whole = pl.BlockSpec((1, 1, TILE, D), lambda i: (0, 1, i + start, 0))
    return pl.pallas_call(
        unembed_kernel,
        grid=(count,),
        in_specs=[
            SM,
            pl.BlockSpec((TILE, n_loss), lambda i: (i + start, 0)),
            pl.BlockSpec((n_loss, D), lambda i: (0, 0)),
            whole,
            whole,
        ]
        + [ANY] * len(held),
        out_specs=[whole, whole, pl.BlockSpec((BLOCKS, TILE, LANES), lambda i: (0, i, 0))],
        out_shape=[shaped(*first.shape)] * 2 + [shaped(BLOCKS, rows, LANES, kind=BF)],
        input_output_aliases={5 + i: i for i in range(len(held))},
        compiler_params=params(),
        name="unembedding_adam",
        cost_estimate=takes(16),
    )(clip, probs, picked, first, second, *held)


GROUP = 128


def overlapping(id_at, count, first, tile, step):
    def one(i, carry):
        least = id_at(i * GROUP)
        most = id_at(jnp.minimum(i * GROUP + GROUP, count) - 1)

        @pl.when((least < first + tile) & (most >= first))
        def _():
            step(i, pl.ds(pl.multiple_of(i * GROUP, GROUP), GROUP))

        return carry

    lax.fori_loop(0, lax.div(count + GROUP - 1, GROUP), one, 0)


def embed_kernel(
    start, last, clip_ref, count_ref, at_ref, id_ref, col_ref, rows_ref, first_ref, second_ref, base_ref,
    *refs,
):
    one_ref, two_ref, extra_ref, scr, extra_scr = refs[-5:]
    tile = one_ref.shape[2]
    first = (pl.program_id(0) + start) * tile
    place = lax.broadcasted_iota(jnp.int32, (tile, 1), 0) + first
    row = lax.broadcasted_iota(jnp.int32, (1, tile), 1) + first

    @pl.when(pl.program_id(0) == 0)
    def _():
        extra_ref[...] = jnp.zeros_like(extra_ref)

    scr[...] = jnp.zeros_like(scr)

    def gather(i, part):
        hot = jnp.where(place == id_ref[i], 1.0, 0.0).astype(BF)
        scr[...] += nn(hot, rows_ref[part, :])

    overlapping(lambda k: at_ref[k], count_ref[0], first, tile, gather)
    one, two, step = moments_fast(scr[...] * clip_ref[0], first_ref[0, 0], second_ref[0, 0])
    one_ref[0, 0] = one
    two_ref[0, 0] = two
    base = jnp.concatenate([base_ref[r] for r in range(BLOCKS)], axis=1).astype(F4)
    extra_scr[...] = jnp.where(place < last, step - base, 0.0).astype(BF)

    def scatter(i, part):
        hot = jnp.where(row == col_ref[part, :], 1.0, 0.0).astype(BF)
        picked = nn(hot, extra_scr[...])
        for r in range(BLOCKS):
            extra_ref[r, part, :] += picked[:, LANES * r : LANES * (r + 1)]

    overlapping(lambda k: at_ref[k], count_ref[0], first, tile, scatter)


def embed_pass(clip, count, ids, rows, first, second, base, held, after, start, tiles):
    n_slots = rows.shape[0]
    vr = first.shape[2]
    whole = pl.BlockSpec((1, 1, TILE, D), lambda i: (0, 0, i + start, 0))
    blocks = pl.BlockSpec((BLOCKS, n_slots, LANES), lambda i: (0, 0, 0))
    groups = n_slots // GROUP
    return pl.pallas_call(
        partial(embed_kernel, start, vr),
        grid=(tiles,),
        in_specs=[
            SM,
            SM,
            SM,
            pl.BlockSpec((groups, 1, GROUP), lambda i: (0, 0, 0)),
            pl.BlockSpec((n_slots, 1), lambda i: (0, 0)),
            pl.BlockSpec((n_slots, D), lambda i: (0, 0)),
            whole,
            whole,
            pl.BlockSpec((BLOCKS, TILE, LANES), lambda i: (0, i + start, 0)),
        ]
        + [ANY] * 3,
        out_specs=[whole, whole, blocks],
        out_shape=[shaped(*first.shape)] * 2 + [shaped(BLOCKS, n_slots, LANES)],
        input_output_aliases={9: 0, 10: 1},
        scratch_shapes=[pltpu.VMEM((TILE, D), F4), pltpu.VMEM((TILE, D), BF)],
        compiler_params=params(),
        name="embedding_adam",
        cost_estimate=takes(17),
    )(clip, count, ids.reshape(-1), ids.reshape(groups, 1, GROUP), ids, rows, first, second, base, *held, after)


def layers_kernel(
    clip_ref, after_ref, wq0, out0, wq1, out1, wide0, wide1, kv_ref, a1, a2, f1, f2, k1, k2, oa1, oa2, of1, of2,
    ok1, ok2, step_ref,
):
    clip = clip_ref[0]
    rows = wq0.shape[0]
    for k, grads in enumerate(((wq0, out0), (wq1, out1))):
        for i in range(2):
            one, two, step = moments_fast(grads[i][...] * clip, a1[0, k, i], a2[0, k, i])
            oa1[0, k, i] = one
            oa2[0, k, i] = two
            at = (2 * k + i) * rows
            for r in range(BLOCKS):
                step_ref[r, at : at + rows, :] = step[:, LANES * r : LANES * (r + 1)].astype(BF)
    cols = FF // BLOCKS // LANES
    for k, grads in enumerate((wide0, wide1)):
        for i in range(2):
            one, two, step = moments_fast(grads[i] * clip, f1[0, k, i], f2[0, k, i])
            of1[0, k, i] = one
            of2[0, k, i] = two
            for r in range(BLOCKS):
                for q in range(cols):
                    at = (2 * L + (2 * k + i) * cols + q) * rows
                    lane = LANES * (r * cols + q)
                    step_ref[r, at : at + rows, :] = step[:, lane : lane + LANES].astype(BF)
    one, two, step = moments_fast(kv_ref[...] * clip, k1[0], k2[0])
    ok1[0] = one
    ok2[0] = two
    at = (2 * L + 2 * L * cols) * rows
    for r in range(BLOCKS):
        moved = step if r == 0 else pltpu.roll(step, LANES - r * (LANES // BLOCKS), 1)
        step_ref[r, at : at + rows, :] = moved.astype(BF)


def settle(total, master, outer, rate, reps):
    mean_diff = rate * (total * (1.0 / reps) + DECAY * master)
    momentum = OUTER_MOMENTUM * outer + mean_diff
    return master - OUTER_RATE * (mean_diff + OUTER_MOMENTUM * momentum), momentum


def embed_settle_kernel(
    reps, rate, count_ref, at_ref, id_ref, extra_ref, base_ref, master_ref, outer_ref, *refs
):
    new_ref, mom_ref, scr = refs[-3:]
    tile = base_ref.shape[0]
    first = pl.program_id(0) * tile
    place = lax.broadcasted_iota(jnp.int32, (tile, 1), 0) + first
    scr[...] = base_ref[...].astype(F4)
    for g in range(reps):

        def add(i, part, g=g):
            hot = jnp.where(place == id_ref[g, i], 1.0, 0.0).astype(BF)
            scr[...] += nn(hot, extra_ref[g, part, :])

        overlapping(lambda k, g=g: at_ref[g, k], count_ref[g], first, tile, add)
    new_ref[0], mom_ref[0] = settle(scr[...], master_ref[0], outer_ref[0], rate, reps)


def embed_settle(reps, counts, ids, extra, base, master, outer, held):
    vr = base.shape[0]
    slots = extra.shape[1]
    whole = pl.BlockSpec((1, SETTLE, LANES), lambda i: (0, i, 0))
    return pl.pallas_call(
        partial(embed_settle_kernel, reps, LEARN_RATES[0]),
        grid=(pl.cdiv(vr, SETTLE),),
        in_specs=[
            SM,
            SM,
            pl.BlockSpec((reps, slots // GROUP, 1, GROUP), lambda i: (0, 0, 0, 0)),
            pl.BlockSpec((reps, slots, LANES), lambda i: (0, 0, 0)),
            pl.BlockSpec((SETTLE, LANES), lambda i: (i, 0)),
            whole,
            whole,
        ]
        + [ANY] * len(held),
        out_specs=[whole, whole],
        out_shape=[shaped(*master.shape)] * 2,
        input_output_aliases={7 + i: i for i in range(len(held))},
        scratch_shapes=[pltpu.VMEM((SETTLE, LANES), F4)],
        compiler_params=params(),
        name="embedding_settle",
        cost_estimate=takes(13),
    )(counts, ids.reshape(reps, -1), ids, extra, base, master, outer, *held)


def unembed_settle_kernel(reps, rate, sum_ref, master_ref, outer_ref, *refs):
    new_ref, mom_ref = refs[-2:]
    rows = sum_ref.shape[0]
    new_ref[0, :rows], mom_ref[0, :rows] = settle(
        sum_ref[...].astype(F4), master_ref[0, :rows], outer_ref[0, :rows], rate, reps
    )


def unembed_settle(reps, total, master, outer, held, piece, size):
    whole = pl.BlockSpec((1, size, LANES), lambda i: (1, piece, 0))
    return pl.pallas_call(
        partial(unembed_settle_kernel, reps, LEARN_RATES[0]),
        grid=(1,),
        in_specs=[pl.BlockSpec(total.shape, lambda i: (0, 0)), whole, whole] + [ANY] * len(held),
        out_specs=[whole, whole],
        out_shape=[shaped(*master.shape)] * 2,
        input_output_aliases={3 + i: i for i in range(len(held))},
        compiler_params=params(),
        name="unembedding_settle",
        cost_estimate=takes(3),
    )(total, master, outer, *held)


def body(
    token_ids,
    prompt_mask,
    loss_pos,
    tables,
    attention,
    feedforward,
    key_value,
    gains_biases,
    first_tables,
    first_attention,
    first_feedforward,
    first_key_value,
    first_gains,
    second_tables,
    second_attention,
    second_feedforward,
    second_key_value,
    second_gains,
    outer_tables,
    outer_attention,
    outer_feedforward,
    outer_key_value,
    outer_gains,
):
    width = lax.axis_size(WIDE_AXES)
    reps = lax.axis_size("rep")
    w = lax.axis_index(WIDE_AXES)
    rep = lax.axis_index("rep")
    seqs = token_ids.shape[3]
    rows_seq = LEN // width
    block = seqs * rows_seq
    cap = 2 * block // width
    vr = tables.shape[1]
    lrows = loss_pos.shape[4]
    n_micro = width * lrows
    n_loss = MICRO * n_micro
    span = width * cap
    n_slots = MICRO * span
    own_rows = D // width
    parity = w % 2

    def over_wide(value, k):
        return lax.ppermute(value, WIDE_AXES, [(i, i ^ k) for i in range(width)])

    def over_rep(value, k):
        return lax.ppermute(value, "rep", [(i, i ^ k) for i in range(reps)])

    def sum_wide(value, kind, beside=()):
        half = value.shape[0] // 2
        keep = lax.dynamic_slice_in_dim(value, parity * half, half)
        give = lax.dynamic_slice_in_dim(value, (1 - parity) * half, half)
        mine = (keep + over_wide(give, 1)).astype(kind)
        parts = [mine] + [over_wide(mine, k) for k in range(2, width, 2)]
        parts, *beside = lax.optimization_barrier((parts, *beside))
        parts = [part.astype(F4) for part in parts]
        while len(parts) > 1:
            parts = [parts[i] + parts[i + 1] for i in range(0, len(parts), 2)]
        total = parts[0].astype(value.dtype)
        other = over_wide(total, 1)
        joined = jnp.concatenate(
            [jnp.where(parity == 0, total, other), jnp.where(parity == 0, other, total)]
        )
        return (joined, *beside) if beside else joined

    scalars = jnp.stack(
        [
            w,
            parity,
            rep,
            w * vr,
            w * own_rows // LANES,
            w * own_rows % LANES,
            jnp.asarray(vr, jnp.int32),
            jnp.zeros((), jnp.int32),
        ]
    ).astype(jnp.int32)

    pack = jnp.concatenate(
        [feedforward[k, i] for k in range(L) for i in range(2)]
        + [attention[k, i] for k in range(L) for i in range(2)],
        axis=1,
    ).astype(BF)

    own_table = tables[1].astype(BF)

    n_mb = MICRO * width

    def by_block(array):
        array = array.reshape(MICRO, seqs, width, rows_seq).transpose(0, 2, 1, 3)
        return array.reshape(n_mb, block).astype(F4)

    tokens = by_block(token_ids)
    flat = jnp.concatenate([gains_biases, key_value.reshape(-1)])
    n_flat = flat.shape[0]
    n_small = gains_biases.shape[0]
    flat = jnp.pad(flat, (0, -n_flat % (8 * block))).reshape(-1, block)
    message = jnp.concatenate([tokens, flat])
    message, pack = lax.optimization_barrier((message, pack))
    pack_near = [over_wide(pack, k) for k in range(2, width, 2)]
    everyone = [message] + [over_rep(message, k) for k in range(1, reps)]
    lines = n_slots // LANES
    slot_ids, slot_codes, slot_rows, rest = call(
        partial(slots_kernel, seqs, rows_seq, vr, cap),
        [shaped(reps, lines, LANES, kind=jnp.int32)]
        + [shaped(lines, LANES, kind=jnp.int32)] * 2
        + [shaped(reps, *flat.shape)],
        (scalars, *everyone),
        scratch=[pltpu.VMEM((reps, *message.shape), F4)],
        smem=1,
        cost=7, name="slots",
    )
    (mine_w,) = call(
        stack_kernel,
        [shaped(width // 2, *pack.shape, kind=BF)],
        (pack, *pack_near),
        cost=2, name="stack_weights",
    )
    half_w = mine_w.shape[0] // 2
    x_w, y_w = over_rep(mine_w, 1), over_rep(mine_w, 2)
    slot_ids, mine_w = lax.optimization_barrier((slot_ids, mine_w))
    asked = [None] * reps
    for k in range(reps - 1, -1, -1):
        asked[k] = tables[0].at[slot_ids[k].reshape(-1)].get(mode="promise_in_bounds").astype(BF)
    rows = [asked[0]] + [over_rep(asked[k], k) for k in range(1, reps)]
    own_codes, own_ids = slot_codes.reshape(-1), slot_rows.reshape(-1)

    rest = rest.reshape(reps, -1)
    vectors, pair_bias, final_gain, final_bias = unpack_small(rest[:, :n_small].reshape(-1))
    final_rows = jnp.stack([final_gain, final_bias])
    vec = [vectors[k][None, :] for k in range(L)]
    kv_near = rest[:, n_small:n_flat].reshape(reps, own_rows, -1).transpose(1, 0, 2)
    kv_near = kv_near.reshape(own_rows, LANES).astype(BF)
    kv_near = [kv_near] + [over_wide(kv_near, k) for k in range(2, width, 2)]
    kv_near = [part for piece in kv_near for part in (piece, over_wide(piece, 1))]

    codes = loss_pos.reshape(n_mb, lrows)
    blocks = jnp.arange(n_mb, dtype=jnp.int32)[:, None]
    row_code = (
        blocks // width * (seqs * LEN)
        + codes // (rows_seq - 1) * LEN
        + blocks % width * rows_seq
        + codes % (rows_seq - 1)
    ).reshape(1, n_loss)
    frequency = 10000.0 ** (-2.0 * jnp.arange(ROT // 2, dtype=F4) / ROT)
    angles = jnp.concatenate([own_codes, row_code[0]]) % LEN
    angles = angles.astype(F4)[None, :] * frequency[:, None]
    turns = jnp.concatenate([jnp.cos(angles), jnp.sin(angles)])
    int_of = partial(shaped, kind=jnp.int32)
    (
        key_codes, chip_codes, slot_cols, row_cols, target_row, weight, slot_cos, slot_sin, row_cos,
        row_sin,
    ) = call(
        partial(places_kernel, seqs, rows_seq, vr, cap),
        [
            int_of(n_mb, 1, span), int_of(n_mb, 1, 2 * cap), int_of(n_slots, 2), int_of(n_loss, 2),
            int_of(1, n_loss), shaped(1, n_loss), shaped(n_slots, LANES), shaped(n_slots, LANES),
            shaped(n_loss, LANES), shaped(n_loss, LANES),
        ],
        (
            scalars, tokens, by_block(prompt_mask), loss_pos.reshape(-1, LANES), slot_codes, slot_rows,
            row_code, turns,
        ),
        smem=1,
        cost=4, name="places",
    )
    count = jnp.sum(weight)

    rows, x_w, y_w, kv_near, own_table = lax.optimization_barrier(
        (rows, x_w, y_w, kv_near, own_table)
    )

    unembed = lax.all_gather(own_table, "rep")
    d_w = [over_rep(x_w[:half_w], 2), over_rep(y_w[half_w:], 1)]
    pairs, stream, kv_low, rows = call(
        kv_kernel,
        [shaped(n_slots, LANES, kind=BF), shaped(BLOCKS, n_loss, LANES, kind=BF), shaped(D, LANES, kind=BF), shaped(reps, n_slots, LANES, kind=BF)],
        (
            scalars, *rows, slot_cos, slot_sin, vec[0], pair_bias[None, :], own_codes[None, :],
            row_cols, *kv_near,
        ),
        smem=1,
        cost=2, name="keys_values",
    )
    keep = lax.dynamic_slice_in_dim(stream, 2 * parity, 2)
    give = lax.dynamic_slice_in_dim(stream, 2 * (1 - parity), 2)
    keep = (keep + over_wide(give, 1)).reshape(2 * n_loss, LANES)
    near = jnp.concatenate([pairs, keep])
    near = [near] + [over_wide(near, k) for k in range(2, width, 2)]
    base_step = base_pass(first_tables, second_tables, pairs)
    near, base_step, d_w = lax.optimization_barrier((near, base_step, d_w))
    pieces = []
    for piece in near:
        pieces += [piece, over_wide(piece, 1)]
    weights = [mine_w, x_w, y_w, *d_w]
    weights = weights + [over_wide(part, 1) for part in weights]


    keys, stream = call(
        partial(order_kernel, seqs, rows_seq, width, cap),
        [shaped(MICRO * width, block, LANES, kind=BF), shaped(BLOCKS, n_loss, LANES)],
        (scalars, base_step, key_codes, *pieces),
        smem=1,
        far=(1,),
        cost=5, name="token_order",
    )
    weights = [mine_w, x_w, y_w, *d_w]
    weights = weights + [over_wide(part, 1) for part in weights]

    tiles = width // SPREAD
    keys = keys.reshape(MICRO, tiles, SPREAD * block, LANES)

    codes = (row_cols,)
    halves = shaped(2, n_loss, LANES)
    att_room = [pltpu.VMEM((reps, D, ATT), BF), pltpu.SemaphoreType.DMA((2, 4, width // 2))]
    ff_room = [pltpu.VMEM((reps, D, WIDE), BF), pltpu.SemaphoreType.DMA((2, 4, width // 2))]
    both_room = [att_room[0], ff_room[0], pltpu.SemaphoreType.DMA((2, 2, 4, width // 2))]
    stacked = ROWS * HEADS // 2
    logs = shaped(n_loss // ROWS, stacked, 1)
    scores = pltpu.VMEM((tiles, stacked, SPREAD * block), F4)
    whole = shaped(n_loss, D)

    def other_half(value):
        return over_wide(value.astype(BF), 1)

    stream0, q0, ctx0, log0 = call(
        partial(first_kernel, seqs, rows_seq),
        [whole, halves, halves, logs],
        (scalars, stream, vec[0], *weights, keys, *codes, row_cos, row_sin),
        smem=1,
        scratch=[scores] + att_room,
        far=range(3, 13),
        cost=9, name="first_attention",
    )
    far0 = other_half(ctx0)
    (partial0,) = call(partial(feed_kernel, 0), [whole], (scalars, stream0, vec[0], *weights), smem=1, scratch=ff_room, far=range(3, 13), name="first_feed")
    partial0, unembed = lax.optimization_barrier((partial0, unembed))
    stream1, q1, ctx1, log1 = call(
        partial(second_kernel, seqs, rows_seq),
        [whole, halves, halves, logs],
        (scalars, partial0, ctx0, far0, vec[1], *weights, keys, *codes, row_cos, row_sin),
        smem=1,
        scratch=[scores] + att_room,
        far=range(5, 15),
        cost=9, name="second_attention",
    )
    far1 = other_half(ctx1)

    (partial1,) = call(partial(feed_kernel, 1), [whole], (scalars, stream1, vec[1], *weights), smem=1, scratch=ff_room, far=range(3, 13), name="second_feed")
    logits, stats, stream2, picked = call(
        logits_kernel,
        [shaped(vr, n_loss), shaped(8, n_loss), whole, shaped(n_loss, D, kind=BF)],
        (scalars, partial1, ctx1, far1, *weights, final_rows, target_row, unembed),
        smem=1,
        scratch=att_room,
        far=range(4, 14),
        cost=10, name="logits",
    )
    near = [stats] + [over_wide(stats, k) for k in range(2, width, 2)]
    stats = jnp.stack([part for piece in near for part in (piece, over_wide(piece, 1))])
    probs, grad_picked, loss_sum = call(
        probs_kernel,
        [shaped(vr, n_loss, kind=BF), shaped(BLOCKS, n_loss, LANES), shaped(1, 1)],
        (scalars, stats, weight, target_row, logits, unembed),
        smem=1,
        out_specs=[VM, VM, SM],
        cost=9, name="loss_gradient",
    )
    base_step, grad_picked = lax.optimization_barrier((base_step, grad_picked))
    base_sum = lax.psum_scatter(base_step, "rep", scatter_dimension=0, tiled=True)[0]

    (unembed_square,) = call(
        squares_kernel, [shaped(1, 1)], (probs, picked), out_specs=[SM], cost=3, name="squares"
    )
    grad_picked, unembed_square = sum_wide(grad_picked, BF, (unembed_square,))

    wide_shape = shaped(2, own_rows, FF)
    out_shape = shaped(own_rows, D)
    vec_shape = shaped(1, 7 * D + FF)
    head_shape = shaped(1, 3 * D)
    dq_shape = shaped(2, n_loss, LANES, kind=BF)
    dkv_shape = shaped(MICRO, tiles, SPREAD * block, LANES)
    slots_shape = shaped(n_slots, LANES)
    pull_scratch = [
        pltpu.VMEM((BLOCKS, n_loss, LANES), BF),
        pltpu.VMEM((BLOCKS, n_loss, LANES), BF),
        pltpu.VMEM((2, n_loss, LANES), F4),
        pltpu.VMEM((LANES, D), F4),
    ]
    dq1, dkv, wide1, out1, vec1, final_grad, grad_stream, grad_feed, square1 = call(
        partial(last_pull_kernel, seqs, rows_seq),
        [
            dq_shape, dkv_shape, wide_shape, out_shape, vec_shape, shaped(2, D), whole, whole,
            shaped(1, 1),
        ],
        (
            scalars, unembed_square, grad_picked, final_rows, stream2, stream1, vec[1], *weights, ctx1,
            far1, q1, log1, keys, *codes,
        ),
        smem=2,
        out_specs=[VM] * 8 + [SM],
        scratch=pull_scratch + both_room,
        far=range(7, 17),
        cost=16, name="second_pull",
    )
    far_dq1 = over_wide(dq1, 1)
    dq0, own_dkv, near_dkv, wide0, out0, vec0, wq1, head1, grad_stream, grad_feed, square0 = call(
        partial(first_pull_kernel, seqs, rows_seq),
        [
            dq_shape, slots_shape, slots_shape, wide_shape, out_shape, vec_shape, out_shape,
            head_shape, whole, whole, shaped(1, 1),
        ],
        (
            scalars, grad_stream, grad_feed, dq1, far_dq1, stream1, vec[1], stream0, vec[0],
            *weights, ctx0, far0, q0, log0, keys, *codes, row_cos, row_sin, dkv,
            chip_codes,
        ),
        smem=1,
        out_specs=[VM] * 10 + [SM],
        scratch=pull_scratch
        + [pltpu.VMEM(dkv_shape.shape, F4)]
        + both_room
        + [pltpu.SemaphoreType.DMA],
        far=[*range(9, 19), 27],
        cost=23, name="first_pull",
    )
    far_dq0 = over_wide(dq0, 1)
    far_dkv = over_wide(near_dkv, 1)
    wq0, head0, grad_rows, row_ids, kv_part, gain_part, square_rows, row_count = call(
        embed_pull_kernel,
        [
            out_shape, head_shape, shaped(n_slots, D, kind=BF), shaped(n_slots, 1, kind=jnp.int32),
            shaped(D, LANES), shaped(8, D), shaped(1, 1), shaped(1, 1, kind=jnp.int32),
        ],
        (
            scalars, grad_stream, grad_feed, dq0, far_dq0, stream0, vec[0], *weights, kv_low, row_cos,
            row_sin, own_dkv, far_dkv, rows, slot_cos, slot_sin,
            slot_cols, row_code, own_ids[None, :],
        ),
        smem=1,
        out_specs=[VM] * 6 + [SM, SM],
        scratch=[
            pltpu.VMEM((BLOCKS, n_loss, LANES), BF),
            pltpu.VMEM((LANES, D), F4),
            pltpu.VMEM((n_slots, D), BF),
            pltpu.VMEM((n_slots, D), BF),
        ]
        + att_room,
        far=range(7, 17),
        cost=12, name="embedding_pull",
    )

    square = (square0 + square1 + square_rows)[0, 0]
    message = jnp.concatenate(
        [kv_part, gain_part.reshape(-1, LANES), jnp.full((16, LANES), square, F4)]
    )
    message, base_sum = sum_wide(message, F4, (base_sum,))
    kv_total = message[:D]
    gain_total = message[D : D + 8 * BLOCKS].reshape(8, D)
    square = message[D + 8 * BLOCKS, 0]

    def vector_grad(head, vec_part):
        return [head[0, : 2 * D], vec_part[0, 2 * D : 4 * D], head[0, 2 * D :], vec_part[0, 5 * D :]]

    grad_small = jnp.concatenate(
        [head0[0, : 2 * D] + gain_total[:2].reshape(-1)]
        + vector_grad(head0, vec0)[1:]
        + vector_grad(head1, vec1)
        + [gain_total[2, :LANES], final_grad.reshape(-1)]
    )
    square = square + jnp.sum(kv_total * kv_total) + jnp.sum(grad_small * grad_small)
    clip_factor = jnp.minimum(1.0, CLIP / (jnp.sqrt(square) + 1e-06))

    clip = clip_factor.reshape(1)

    n_tiles = pl.cdiv(vr, TILE)
    size = n_tiles
    pieces = pl.cdiv(n_tiles, size)
    bounds = [min(size * i, n_tiles) for i in range(pieces + 1)]
    held = []
    terms = []

    for i in range(pieces):
        *held, step = unembed_pass(
            clip, probs, picked, first_tables, second_tables, held, bounds[i],
            bounds[i + 1] - bounds[i],
        )
        terms.append(lax.psum_scatter(step, "rep", scatter_dimension=0, tiled=True)[0])

    kv_grad = lax.dynamic_slice_in_dim(kv_total, w * own_rows, own_rows, axis=0)
    sm_one, sm_two, sm_step = moments_step(
        grad_small * clip_factor, first_gains[0], second_gains[0]
    )
    pack_rows = own_rows * (2 * L + 2 * L * (FF // BLOCKS // LANES) + 1)
    att_one, att_two, ff_one, ff_two, kv_one, kv_two, packed = call(
        layers_kernel,
        [shaped(*first_attention.shape)] * 2
        + [shaped(*first_feedforward.shape)] * 2
        + [shaped(*first_key_value.shape)] * 2
        + [shaped(BLOCKS, pack_rows, LANES, kind=BF)],
        (
            clip, step, wq0, out0, wq1, out1, wide0, wide1, kv_grad, first_attention, second_attention,
            first_feedforward, second_feedforward, first_key_value, second_key_value,
        ),
        smem=1,
        far=(1,),
        cost=8, name="layers_adam",
    )
    n_small = sm_step.shape[0] // reps
    sm_step = jnp.pad(sm_step.astype(BF).reshape(reps, n_small), ((0, 0), (0, -n_small % 2048)))
    packed = jnp.concatenate([packed, sm_step.reshape(reps, -1, LANES)], axis=1)
    steps = packed
    packed = lax.all_to_all(packed, "rep", 0, 0, tiled=True)
    packed = jnp.sum(packed.astype(F4), axis=0)

    e_tiles = pl.cdiv(vr, TILE)
    e_pieces = min(2, e_tiles)
    e_bounds = [e_tiles * i // e_pieces for i in range(e_pieces + 1)]
    extra = 0.0
    for i in range(e_pieces):
        *held, part = embed_pass(
            clip, row_count.reshape(1), row_ids, grad_rows, first_tables, second_tables, base_step, held,
            steps, e_bounds[i], e_bounds[i + 1] - e_bounds[i],
        )
        extra = extra + part
    one_tables, two_tables = held
    coded = jnp.concatenate([(row_ids + LANES) // LANES, (row_ids + LANES) % LANES])
    coded = jnp.broadcast_to(coded.astype(BF).reshape(1, -1, LANES), (reps, n_slots // 64, LANES))
    extra = jnp.concatenate([extra.astype(BF), coded], axis=1)
    extra = lax.all_to_all(extra, "rep", 0, 0, tiled=True)
    coded = extra[:, n_slots:].reshape(reps, 2, n_slots).astype(jnp.int32)
    coded = coded[:, 0] * LANES + coded[:, 1] - LANES
    counts = jnp.sum((coded >= 0).astype(jnp.int32), axis=1)

    new_tables = ()
    for i in range(pieces - 1):
        new_tables = unembed_settle(
            reps, terms[i], tables, outer_tables, new_tables, i, terms[0].shape[0]
        )
    new_tables = embed_settle(
        reps, counts, coded.reshape(reps, n_slots // GROUP, 1, GROUP), extra, base_sum, tables,
        outer_tables, new_tables,
    )
    new_tables = unembed_settle(
        reps, terms[-1], tables, outer_tables, new_tables, pieces - 1, terms[0].shape[0]
    )

    cols = FF // BLOCKS // LANES
    at_ff = 2 * L * own_rows
    at_kv = at_ff + 2 * L * cols * own_rows
    masters = (attention, feedforward, key_value, gains_biases)
    outers = (outer_attention, outer_feedforward, outer_key_value, outer_gains)
    sums = (
        packed[:at_ff].reshape(L, 2, own_rows, LANES),
        packed[at_ff:at_kv]
        .reshape(L, 2, cols, own_rows, LANES)
        .transpose(0, 1, 3, 2, 4)
        .reshape(feedforward.shape),
        packed[at_kv : at_kv + own_rows, : LANES // BLOCKS],
        packed[pack_rows:].reshape(-1)[:n_small],
    )
    stepped = [new_tables] + [
        settle(sums[i], masters[i], outers[i], LEARN_RATES[i + 1], reps) for i in range(4)
    ]
    return (
        loss_sum.reshape(1),
        count.reshape(1),
        *[pair[0] for pair in stepped],
        one_tables,
        att_one,
        ff_one,
        kv_one,
        sm_one[None],
        two_tables,
        att_two,
        ff_two,
        kv_two,
        sm_two[None],
        *[pair[1] for pair in stepped],
    )


def solution(mesh):
    split = (
        P(None, WIDE_AXES, "rep"),
        P(None, None, WIDE_AXES, "rep"),
        P(None, None, WIDE_AXES, "rep"),
        P(WIDE_AXES, "rep"),
        P("rep"),
    )
    moments = (
        P("rep", None, WIDE_AXES, None),
        P("rep", None, None, WIDE_AXES, None),
        P("rep", None, None, WIDE_AXES, None),
        P("rep", WIDE_AXES, None),
        P("rep", None),
    )
    tokens = P("rep", None, None, None, None)
    parted = mesh.devices.reshape(mesh.shape["rep"], mesh.shape["wide"] // 2, 2)
    return jax.shard_map(
        body,
        mesh=Mesh(parted, ("rep",) + WIDE_AXES),
        in_specs=(tokens,) * 3 + split + moments + moments + split,
        out_specs=(P("rep"), P("rep")) + split + moments + moments + split,
        check_vma=False,
    )
```

```python
from functools import partial

import jax
import jax.numpy as jnp
from jax import lax
from jax.experimental import pallas as pl
from jax.experimental.pallas import tpu as pltpu
from jax.sharding import Mesh
from jax.sharding import PartitionSpec as P

D = 512
HEADS = 8
HD = 64
ROT = 16
FF = 2048
L = 2
LEN = 2048
MICRO = 2
STEP = 5
WIDE_AXES = ("chip", "core")

NORM_EPSILON = 1e-05
CLIP = 0.1
LEARN_RATES = (0.02, 0.2, 0.02, 0.02, 0.2)
BETA_ONE = 0.9
BETA_TWO = 0.95
ADAM_EPSILON = 1e-08
DECAY = 0.1
OUTER_RATE = 0.7
OUTER_MOMENTUM = 0.9
FIX_ONE = 1.0 / (1.0 - BETA_ONE**STEP)
FIX_TWO = 1.0 / (1.0 - BETA_TWO**STEP)

BF = jnp.bfloat16
F4 = jnp.float32


def dot(left, right, dims):
    return lax.dot_general(left, right, (dims, ((), ())), preferred_element_type=F4)


def normal_of(stream):
    centred = stream - jnp.mean(stream, axis=-1, keepdims=True)
    scale = lax.rsqrt(jnp.mean(centred * centred, axis=-1, keepdims=True) + NORM_EPSILON)
    return centred * scale, scale


def norm_pull(shaped, normal, scale):
    return scale * (
        shaped
        - jnp.mean(shaped, axis=-1, keepdims=True)
        - normal * jnp.mean(shaped * normal, axis=-1, keepdims=True)
    )


def rotary(places):
    frequency = 10000.0 ** (-2.0 * jnp.arange(ROT // 2, dtype=F4) / ROT)
    angles = places.astype(F4)[:, None] * frequency[None, :]
    return jnp.cos(angles), jnp.sin(angles)


def rotate(values, cosine, sine):
    half = ROT // 2
    a = values[..., :half]
    b = values[..., half:ROT]
    c = cosine[:, None, :]
    s = sine[:, None, :]
    return jnp.concatenate([a * c - b * s, b * c + a * s, values[..., ROT:]], axis=-1)


def unpack_small(gains_biases):
    span = 7 * D + FF
    layers = gains_biases[: L * span].reshape(L, span)
    remain = gains_biases[L * span :]
    return layers, remain[: 2 * HD], remain[2 * HD : 2 * HD + D], remain[2 * HD + D :]


def moments_step(gradient, one, two):
    one = BETA_ONE * one + (1.0 - BETA_ONE) * gradient
    two = BETA_TWO * two + (1.0 - BETA_TWO) * gradient * gradient
    return one, two, (one * FIX_ONE) / (jnp.sqrt(two * FIX_TWO) + ADAM_EPSILON)


def step_of(one, two):
    two = two * FIX_TWO
    under = two * lax.rsqrt(jnp.maximum(two, 1e-37)) + ADAM_EPSILON
    guess = pl.reciprocal(under, approx=True)
    return one * FIX_ONE * (guess * (2.0 - under * guess))


def moments_fast(gradient, one, two):
    one = BETA_ONE * one + (1.0 - BETA_ONE) * gradient
    two = BETA_TWO * two + (1.0 - BETA_TWO) * gradient * gradient
    return one, two, step_of(one, two)


VM = pl.BlockSpec(memory_space=pltpu.VMEM)
SM = pl.BlockSpec(memory_space=pltpu.SMEM)
LANES = 128
BLOCKS = D // LANES
ROWS = 64
RUN = 2096
SPREAD = 4
FAR = 1 << 24


def shaped(*dims, kind=F4):
    return jax.ShapeDtypeStruct(dims, kind)


def takes(micros):
    return pl.CostEstimate(flops=0, bytes_accessed=int(micros * 3e6), transcendentals=0)


def call(kernel, outs, ins, smem=0, scratch=(), out_specs=None, name=None, room=63, far=(), cost=5):
    return pl.pallas_call(
        kernel,
        out_shape=outs,
        in_specs=[SM if i < smem else ANY if i in far else VM for i in range(len(ins))],
        out_specs=[VM] * len(outs) if out_specs is None else out_specs,
        scratch_shapes=list(scratch),
        compiler_params=pltpu.CompilerParams(vmem_limit_bytes=room * 1024 * 1024),
        name=name,
        cost_estimate=takes(cost),
    )(*ins)


ANY = pl.BlockSpec(memory_space=pltpu.HBM)
ATT = L * 2 * LANES
WIDE = 2 * FF // BLOCKS


class Fetch:
    def __init__(self, sc_ref, weights, scr, sems, start):
        w, rep = sc_ref[0], sc_ref[2]
        cols = pl.ds(start, scr.shape[2])
        self.copies = []
        for core in range(2):
            mine = weights[5 * core : 5 * core + 5]
            spots = [(mine[k], k, i, i) for k in range(3) for i in range(mine[0].shape[0])]
            cut = mine[3].shape[0]
            spots += [(mine[3], 3, i, i) for i in range(cut)]
            spots += [(mine[4], 3, i, i + cut) for i in range(mine[4].shape[0])]
            for ref, k, i, chip in spots:
                own_rows = ref.shape[1]
                at = pl.multiple_of((w ^ (2 * chip + core)) * own_rows, own_rows)
                self.copies.append(
                    pltpu.make_async_copy(
                        ref.at[i, :, cols],
                        scr.at[rep ^ k, pl.ds(at, own_rows), :],
                        sems.at[core, k, chip],
                    )
                )
        for copy in self.copies:
            copy.start()

    def wait(self):
        for copy in self.copies:
            copy.wait()


def nn(left, right):
    return dot(left, right, ((1,), (0,)))


def nt(left, right):
    return dot(left, right, ((1,), (1,)))


def tn(left, right):
    return dot(left, right, ((0,), (0,)))


def split_two(value):
    high = value.astype(BF)
    return high, (value - high.astype(F4)).astype(BF)


def lanes_of(rows):
    return lax.broadcasted_iota(jnp.int32, (rows, LANES), 1)


def spin(value, cosine, sine):
    place = lanes_of(value.shape[0]) % HD
    ahead = pltpu.roll(value, LANES - ROT // 2, 1)
    behind = pltpu.roll(value, ROT // 2, 1)
    moved = jnp.where(place < ROT // 2, -ahead, behind)
    return value * cosine + moved * sine


def swap_halves(value):
    return pltpu.roll(value, HD, 1)


def blocks_of(value):
    return [value[:, LANES * i : LANES * (i + 1)] for i in range(value.shape[1] // LANES)]


def tile_of(vr):
    return 2096 if vr % 2096 == 0 else vr


def stack_kernel(*refs):
    for i, ref in enumerate(refs[:-1]):
        refs[-1][i] = ref[...]


def lower_ones(size):
    first = lax.broadcasted_iota(jnp.int32, (size, size), 0)
    second = lax.broadcasted_iota(jnp.int32, (size, size), 1)
    return jnp.where(first <= second, 1.0, 0.0).astype(BF)


def rows_of(values, block):
    rows = [jnp.broadcast_to(value, (1, block)) for value in values]
    rows.append(jnp.zeros((8 - len(rows), block), F4))
    return jnp.concatenate(rows, axis=0).astype(BF)


def code_of(place, mb, width, seqs, rows_seq):
    m, b = lax.div(mb, width), lax.rem(mb, width)
    code = m * (seqs * LEN) + b * rows_seq
    return code + lax.div(place, rows_seq) * LEN + lax.rem(place, rows_seq)


def slots_kernel(
    seqs, rows_seq, vr, cap, sc_ref, own_all, x_all, y_all, d_all, ids_ref, code_ref, own_ref, rest_ref,
    all_ref,
):
    for k, ref in enumerate((own_all, x_all, y_all, d_all)):
        all_ref[k] = ref[...]
    groups = all_ref.shape[0]
    micros_width = ids_ref.shape[1] * LANES // cap
    block = all_ref.shape[2]
    width = micros_width // MICRO
    offset = sc_ref[3].astype(F4)
    per = LANES // cap
    lower = lower_ones(block)
    slot = lax.broadcasted_iota(jnp.int32, (LANES, 1), 0)
    wanted = (slot % cap).astype(F4)
    lane = lax.broadcasted_iota(jnp.int32, (1, LANES), 1)
    place = lax.broadcasted_iota(jnp.int32, (1, block), 1).astype(F4)

    def one(g, carry):
        local = all_ref[g, :micros_width, :] - offset
        inside = (local >= 0.0) & (local < vr)
        rank = nn(jnp.where(inside, 1.0, 0.0).astype(BF), lower) - 1.0
        rank = jnp.where(inside, rank, -1.0)
        local = jnp.where(inside, local, 0.0)
        high = jnp.floor(local * (1.0 / 64.0))
        for row in range(ids_ref.shape[1]):
            total = jnp.zeros((8, LANES), F4)
            for i in range(per):
                mb = row * per + i
                one_row = slice(mb, mb + 1)
                hot = (rank[one_row] == wanted) & (slot // cap == i)
                values = rows_of(
                    (high[one_row], local[one_row] - 64.0 * high[one_row], place, jnp.ones((1, 1), F4)),
                    block,
                )
                total = total + nt(values, jnp.where(hot, 1.0, 0.0).astype(BF))
            ids = (total[0:1] * 64.0 + total[1:2]).astype(jnp.int32)
            valid = total[3:4] > 0.5
            ids_ref[g, row : row + 1, :] = ids

            @pl.when(g == 0)
            def _():
                code = code_of(
                    total[2:3].astype(jnp.int32), row * per + lane // cap, width, seqs, rows_seq
                )
                code_ref[row : row + 1, :] = jnp.where(valid, code, FAR)
                own_ref[row : row + 1, :] = jnp.where(valid, ids, vr)
        return carry

    lax.fori_loop(0, groups, one, 0)
    for g in range(groups):
        rest_ref[sc_ref[2] ^ g] = all_ref[g, micros_width:, :]


def places_kernel(
    seqs, rows_seq, vr, cap, sc_ref, token_ref, mask_ref, loss_ref, slot_ref, own_ref, row_ref, turn_ref,
    key_out, chip_out, slot_out, row_out, target_out, weight_out, slot_cos, slot_sin, row_cos, row_sin,
):
    many, block = token_ref.shape
    width = many // MICRO
    n_loss = row_ref.shape[1]
    lrows = n_loss // many
    lower = lower_ones(block)
    tokens = token_ref[...]
    shard = jnp.floor((tokens + 0.5) * (1.0 / vr)).astype(jnp.int32) ^ sc_ref[0]
    rank = jnp.zeros((many, block), F4)
    for k in range(width):
        inside = jnp.where(shard == k, 1.0, 0.0)
        rank = rank + inside * (nn(inside.astype(BF), lower) - 1.0)
    spot = shard.astype(F4) * cap + rank
    wanted = lax.broadcasted_iota(jnp.int32, (width * cap, 1), 0).astype(F4)
    place = lax.broadcasted_iota(jnp.int32, (1, block), 1).astype(F4)
    values = rows_of((place, jnp.ones((1, 1), F4)), block)
    for mb in range(many):
        hot = jnp.where(spot[mb : mb + 1] == wanted, 1.0, 0.0).astype(BF)
        total = nt(values, hot)
        code = code_of(total[0:1].astype(jnp.int32), mb, width, seqs, rows_seq)
        code = jnp.where(total[1:2] > 0.5, code, FAR)
        key_out[mb] = code
        chip_out[mb] = code[:, : 2 * cap]
    high = jnp.floor(tokens * (1.0 / 256.0))
    low = tokens - 256.0 * high
    at = lax.broadcasted_iota(jnp.int32, (block, 1), 0)
    lane = lax.broadcasted_iota(jnp.int32, (1, LANES), 1)
    per = LANES // lrows
    for row in range(n_loss // LANES):
        codes = loss_ref[row : row + 1, :]
        after = lax.div(codes, rows_seq - 1) * rows_seq + lax.rem(codes, rows_seq - 1) + 1
        total = jnp.zeros((8, LANES), F4)
        for i in range(per):
            mb = slice(row * per + i, row * per + i + 1)
            hot = (at == after) & (lane // lrows == i)
            total = total + nn(
                rows_of((high[mb], low[mb], mask_ref[mb, :]), block),
                jnp.where(hot, 1.0, 0.0).astype(BF),
            )
        part = slice(LANES * row, LANES * (row + 1))
        target_out[0:1, part] = (total[0:1] * 256.0 + total[1:2]).astype(jnp.int32)
        weight_out[0:1, part] = total[2:3]

    def column(row):
        return jnp.transpose(jnp.broadcast_to(row, (LANES, LANES)))[:, 0:1]

    n_slots = slot_out.shape[0]
    ones = jnp.ones((HD - ROT, LANES), F4)
    zeros = jnp.zeros((HD - ROT, LANES), F4)
    ends = (jnp.ones((HD, LANES), F4), jnp.zeros((HD, LANES), F4))
    for start in range(0, n_slots + n_loss, LANES):
        slots = start < n_slots
        into = start if slots else start - n_slots
        part = slice(into, into + LANES)
        cosine = turn_ref[0:8, start : start + LANES]
        sine = turn_ref[8:16, start : start + LANES]
        cosines = [cosine, cosine, ones]
        sines = [sine, sine, zeros]
        cosines, sines = (
            (cosines + [ends[0]], sines + [ends[1]]) if slots else (cosines * 2, sines * 2)
        )
        cos_out, sin_out = (slot_cos, slot_sin) if slots else (row_cos, row_sin)
        cos_out[part, :] = jnp.transpose(jnp.concatenate(cosines, axis=0))
        sin_out[part, :] = jnp.transpose(jnp.concatenate(sines, axis=0))
        if slots:
            i = start // LANES
            slot_out[part, 0:1] = column(slot_ref[i : i + 1, :].astype(F4)).astype(jnp.int32)
            slot_out[part, 1:2] = column(own_ref[i : i + 1, :].astype(F4)).astype(jnp.int32)
        else:
            code = row_ref[0:1, part]
            row_out[part, 0:1] = column(code.astype(F4)).astype(jnp.int32)
            row_out[part, 1:2] = column((lax.div(code, LEN) * LEN).astype(F4)).astype(jnp.int32)


def kv_kernel(
    sc_ref, r0, r1, r2, r3, cos_ref, sin_ref, vec_ref, pair_bias_ref, slot_code_ref, row_ref, *refs
):
    pairs_ref, picked_ref, kv_ref, rows_ref = refs[-4:]
    n_slots = rows_ref.shape[1]
    for k, piece in enumerate((r0, r1, r2, r3)):
        rows_ref[sc_ref[2] ^ k] = piece[...]
    for k, piece in enumerate(refs[:-4]):
        own = piece.shape[0]
        kv_ref[pl.ds(pl.multiple_of((sc_ref[0] ^ k) * own, own), own), :] = piece[...]
    step = 256
    for start in range(0, n_slots, step):
        part = pl.ds(start, step)
        rows = jnp.concatenate([rows_ref[r, part, :] for r in range(BLOCKS)], axis=1)
        normal, unused = normal_of(rows.astype(F4))
        normed = (normal * vec_ref[0:1, :D] + vec_ref[0:1, D : 2 * D]).astype(BF)
        projected = pair_bias_ref[...] + nn(normed, kv_ref[...])
        pairs_ref[part, :] = spin(projected, cos_ref[part, :], sin_ref[part, :]).astype(BF)
    rows = jnp.concatenate([rows_ref[r] for r in range(BLOCKS)], axis=1)
    pick = jnp.where(row_ref[:, 0:1] == slot_code_ref[...], 1.0, 0.0).astype(BF)
    for r in range(BLOCKS):
        picked_ref[r] = nn(pick, rows[:, LANES * r : LANES * (r + 1)]).astype(BF)


def token_codes(place, m, first_block, seqs, rows_seq):
    block = seqs * rows_seq
    inside = lax.rem(place, block)
    code = m * (seqs * LEN) + (first_block + lax.div(place, block)) * rows_seq
    return code + lax.div(inside, rows_seq) * LEN + lax.rem(inside, rows_seq)


def order_kernel(seqs, rows_seq, width, cap, sc_ref, after_ref, code_ref, *refs):
    pieces, out_ref, stream_ref = refs[:-2], refs[-2], refs[-1]
    n_loss = stream_ref.shape[1]
    n_slots = MICRO * width * cap
    for core in range(2):
        for i in range(2):
            part = slice(n_slots + n_loss * i, n_slots + n_loss * (i + 1))
            total = pieces[core][part, :].astype(F4)
            for piece in pieces[core + 2 :: 2]:
                total = total + piece[part, :].astype(F4)
            stream_ref[2 * (sc_ref[1] ^ core) + i] = total
    block = seqs * rows_seq

    def one(mb, carry):
        m, b = lax.div(mb, width), lax.rem(mb, width)
        part = pl.ds(pl.multiple_of(mb * cap, cap), cap)
        slots = jnp.concatenate([piece[part, :] for piece in pieces], axis=0)
        place = lax.broadcasted_iota(jnp.int32, (block, 1), 0)
        hot = token_codes(place, m, b, seqs, rows_seq) == code_ref[mb]
        out_ref[mb] = nn(jnp.where(hot, 1.0, 0.0).astype(BF), slots).astype(BF)
        return carry

    lax.fori_loop(0, MICRO * width, one, 0)


def stack_heads(block_of, part):
    low_lanes = lanes_of(ROWS) < HD
    pieces = []
    for b in range(2):
        block = block_of[b, part, :]
        pieces += [block, swap_halves(block)]
    return [jnp.where(low_lanes, piece, 0.0) for piece in pieces]


def masks_of(row_ref, part, m, kt, tile, seqs, rows_seq):
    place = lax.broadcasted_iota(jnp.int32, (1, tile), 1)
    code = token_codes(place, m, kt * SPREAD, seqs, rows_seq)
    allowed = code <= row_ref[part, 0:1]
    if seqs > 1:
        allowed = allowed & (code >= row_ref[part, 1:2])
    return allowed


def masked(scores, allowed):
    return jnp.concatenate(
        [
            jnp.where(allowed, scores[ROWS * h : ROWS * (h + 1), :], -1e30)
            for h in range(HEADS // 2)
        ],
        axis=0,
    )


def attend(q_scr, ctx_ref, log_ref, keys_ref, row_ref, scr, seqs, rows_seq):
    micros, tiles, tile, unused = keys_ref.shape
    low_lanes = lanes_of(ROWS) < HD
    high = ROWS * HEADS // 2

    def one(t, carry):
        m, c = lax.div(t, tiles), lax.rem(t, tiles)
        part = pl.ds(pl.multiple_of(t * ROWS, ROWS), ROWS)
        query = jnp.concatenate(stack_heads(q_scr, part), axis=0).astype(BF)

        def scores_at(kt, top):
            allowed = masks_of(row_ref, part, m, kt, tile, seqs, rows_seq)
            scores = masked(nt(query, keys_ref[m, kt]), allowed)
            scr[kt] = scores
            for piece in blocks_of(scores):
                top = jnp.maximum(top, piece)
            return top

        top = lax.fori_loop(0, c + 1, scores_at, jnp.full((high, LANES), -1e30, F4))
        top = jnp.max(top, axis=1, keepdims=True)

        def expo_at(kt, total):
            expo = jnp.exp(scr[kt] - top)
            scr[kt] = expo
            for piece in blocks_of(expo):
                total = total + piece
            return total

        total = lax.fori_loop(0, c + 1, expo_at, jnp.zeros((high, LANES), F4))
        total = jnp.sum(total, axis=1, keepdims=True)
        inverse = 1.0 / total

        def context_at(kt, so_far):
            return so_far + nn((scr[kt] * inverse).astype(BF), keys_ref[m, kt])

        context = lax.fori_loop(0, c + 1, context_at, jnp.zeros((high, LANES), F4))
        log_ref[t] = top + jnp.log(total)
        heads = [context[ROWS * h : ROWS * (h + 1), :] for h in range(HEADS // 2)]
        for b in range(2):
            ctx_ref[b, part, :] = jnp.where(
                low_lanes, swap_halves(heads[2 * b]), heads[2 * b + 1]
            )
        return carry

    lax.fori_loop(0, micros * tiles, one, 0)


def attend_pull(
    q_ref, ctx_ref, grad_scr, log_ref, keys_ref, row_ref, dq_ref, dkv_ref, seqs, rows_seq
):
    micros, tiles, tile, unused = keys_ref.shape
    low_lanes = lanes_of(ROWS) < HD
    high = ROWS * HEADS // 2

    def one(t, carry):
        m, c = lax.div(t, tiles), lax.rem(t, tiles)
        part = pl.ds(pl.multiple_of(t * ROWS, ROWS), ROWS)
        query = jnp.concatenate(stack_heads(q_ref, part), axis=0).astype(BF)
        grads = []
        inners = []
        for b in range(2):
            grad = grad_scr[b, part, :]
            product = grad * ctx_ref[b, part, :]
            for sub in range(2):
                moved = swap_halves(grad) if sub == 0 else grad
                grads.append(jnp.where(low_lanes, 0.0, moved))
                mine = low_lanes if sub == 0 else ~low_lanes
                inners.append(jnp.sum(jnp.where(mine, product, 0.0), axis=1, keepdims=True))
        grad = jnp.concatenate(grads, axis=0).astype(BF)
        inner = jnp.concatenate(inners, axis=0)
        log_total = log_ref[t]

        def pull_at(kt, so_far):
            both = keys_ref[m, kt]
            allowed = masks_of(row_ref, part, m, kt, tile, seqs, rows_seq)
            probs = jnp.exp(masked(nt(query, both), allowed) - log_total)
            grad_scores = (probs * (nt(grad, both) - inner)).astype(BF)
            dkv_ref[m, kt] += tn(grad_scores, query) + tn(probs.astype(BF), grad)
            return so_far + nn(grad_scores, both)

        total = lax.fori_loop(0, c + 1, pull_at, jnp.zeros((high, LANES), F4)) * 0.125
        heads = [total[ROWS * h : ROWS * (h + 1), :] for h in range(HEADS // 2)]
        for b in range(2):
            dq_ref[b, part, :] = jnp.where(
                low_lanes, heads[2 * b], swap_halves(heads[2 * b + 1])
            ).astype(BF)
        return carry

    lax.fori_loop(0, micros * tiles, one, 0)


def to_slots(dkv_ref, code_ref, own_out, near_out, seqs, rows_seq):
    micros, tiles, tile, unused = dkv_ref.shape
    block = seqs * rows_seq
    width = tiles * SPREAD
    cap = own_out.shape[0] // (micros * width)

    def one(mb, carry):
        m, b = lax.div(mb, width), lax.rem(mb, width)
        part = pl.ds(pl.multiple_of(mb * cap, cap), cap)
        inside = pl.ds(pl.multiple_of(lax.rem(b, SPREAD) * block, block), block)
        high, rest = split_two(dkv_ref[m, lax.div(b, SPREAD), inside, :])
        place = lax.broadcasted_iota(jnp.int32, (block, 1), 0)
        code = token_codes(place, m, b, seqs, rows_seq)
        hot = jnp.where(code == code_ref[mb], 1.0, 0.0).astype(BF)
        both = tn(hot, high) + tn(hot, rest)
        own_out[part, :] = both[:cap, :]
        near_out[part, :] = both[cap:, :]
        return carry

    lax.fori_loop(0, micros * width, one, 0)


def join_blocks(parity, own_ref, other_ref):
    return [
        jnp.where(parity == r // 2, own_ref[r % 2].astype(F4), other_ref[r % 2].astype(F4))
        for r in range(BLOCKS)
    ]


def branch_of(parity, k, own_ref, other_ref, att_ref):
    context = jnp.concatenate(join_blocks(parity, own_ref, other_ref), axis=1).astype(BF)
    at = k * 256 + LANES
    return jnp.concatenate(
        [nn(context, att_ref[r, :, at : at + LANES]) for r in range(BLOCKS)], axis=1
    )


def queries_of(k, stream, parity, vec_ref, att_ref, cos_ref, sin_ref, q_ref):
    normal, unused = normal_of(stream)
    normed = (normal * vec_ref[0:1, :D] + vec_ref[0:1, D : 2 * D]).astype(BF)
    cosine, sine = cos_ref[...], sin_ref[...]
    for i in range(2):
        weight = jnp.where(
            parity == 0,
            att_ref[i, :, k * 256 : k * 256 + LANES],
            att_ref[2 + i, :, k * 256 : k * 256 + LANES],
        )
        low = vec_ref[0:1, 4 * D + LANES * i : 4 * D + LANES * (i + 1)]
        high = vec_ref[0:1, 4 * D + LANES * (2 + i) : 4 * D + LANES * (3 + i)]
        query = nn(normed, weight) + jnp.where(parity == 0, low, high)
        query = spin(query, cosine, sine).astype(BF).astype(F4)
        q_ref[i] = query * 0.125


def first_kernel(
    seqs, rows_seq, sc_ref, low_ref, vec_ref, w0, w1, w2, w3, w4, w5, w6, w7, w8, w9, keys_ref, row_ref, cos_ref, sin_ref,
    stream_ref, q_ref, ctx_ref, log_ref, scr, att_ref, sem,
):
    copy = Fetch(sc_ref, (w0, w1, w2, w3, w4, w5, w6, w7, w8, w9), att_ref, sem, L * WIDE)
    stream_ref[...] = jnp.concatenate([low_ref[r] for r in range(BLOCKS)], axis=1)
    copy.wait()
    queries_of(0, stream_ref[...], sc_ref[1], vec_ref, att_ref, cos_ref, sin_ref, q_ref)
    attend(q_ref, ctx_ref, log_ref, keys_ref, row_ref, scr, seqs, rows_seq)


def second_kernel(
    seqs, rows_seq, sc_ref, partial_ref, own_ref, other_ref, vec_ref, w0, w1, w2, w3, w4, w5, w6, w7, w8, w9, keys_ref, row_ref,
    cos_ref, sin_ref, stream_ref, q_ref, ctx_ref, log_ref, scr, att_ref, sem,
):
    parity = sc_ref[1]
    Fetch(sc_ref, (w0, w1, w2, w3, w4, w5, w6, w7, w8, w9), att_ref, sem, L * WIDE).wait()
    stream_ref[...] = partial_ref[...] + branch_of(parity, 0, own_ref, other_ref, att_ref)
    queries_of(1, stream_ref[...], parity, vec_ref, att_ref, cos_ref, sin_ref, q_ref)
    attend(q_ref, ctx_ref, log_ref, keys_ref, row_ref, scr, seqs, rows_seq)


ROOT_HALF = 0.7071067811865476
ROOT_TAU = 0.3989422804014327


def feed_kernel(k, sc_ref, stream_ref, vec_ref, w0, w1, w2, w3, w4, w5, w6, w7, w8, w9, out_ref, ff_ref, sem):
    copy = Fetch(sc_ref, (w0, w1, w2, w3, w4, w5, w6, w7, w8, w9), ff_ref, sem, k * WIDE)
    stream = stream_ref[...]
    normal, unused = normal_of(stream)
    feed = (normal * vec_ref[0:1, 2 * D : 3 * D] + vec_ref[0:1, 3 * D : 4 * D]).astype(BF)
    total = stream + vec_ref[0:1, 5 * D : 6 * D] + vec_ref[0:1, 6 * D : 7 * D]
    cols = FF // BLOCKS
    copy.wait()
    for r in range(BLOCKS):
        at_r = 7 * D + cols * r
        hidden = nn(feed, ff_ref[r, :, :cols]) + vec_ref[0:1, at_r : at_r + cols]
        active = (0.5 * hidden * (1.0 + lax.erf(hidden * ROOT_HALF))).astype(BF)
        total = total + nt(active, ff_ref[r, :, cols:])
    out_ref[...] = total


def runs_of(tables_ref):
    vr = tables_ref.shape[1]
    step = RUN if vr % RUN == 0 else vr
    for start in range(0, vr, step):
        part = slice(start, start + step)
        yield start, step, jnp.concatenate([tables_ref[r, part, :] for r in range(BLOCKS)], axis=1)


def logits_kernel(
    sc_ref, partial_ref, own_ref, other_ref, w0, w1, w2, w3, w4, w5, w6, w7, w8, w9, final_ref, target_ref, tables_ref,
    logits_ref, stats_ref, stream_ref, picked_ref, att_ref, sem,
):
    parity, offset = sc_ref[1], sc_ref[3]
    Fetch(sc_ref, (w0, w1, w2, w3, w4, w5, w6, w7, w8, w9), att_ref, sem, L * WIDE).wait()
    stream = partial_ref[...] + branch_of(parity, 1, own_ref, other_ref, att_ref)
    stream_ref[...] = stream
    normal, unused = normal_of(stream)
    picked = (normal * final_ref[0:1, :] + final_ref[1:2, :]).astype(BF)
    picked_ref[...] = picked
    n_loss = picked.shape[0]
    top = jnp.full((1, n_loss), -1e30, F4)
    hit_total = jnp.zeros((1, n_loss), F4)
    target = target_ref[...] - offset
    for start, size, table in runs_of(tables_ref):
        logits = nt(table, picked)
        logits_ref[start : start + size, :] = logits
        top = jnp.maximum(top, jnp.max(logits, axis=0, keepdims=True))
        place = lax.broadcasted_iota(jnp.int32, (size, n_loss), 0) + start
        hit_total = hit_total + jnp.sum(
            jnp.where(place == target, logits, 0.0), axis=0, keepdims=True
        )
    total = jnp.zeros((1, n_loss), F4)
    step = tile_of(logits_ref.shape[0])
    for start in range(0, logits_ref.shape[0], step):
        total = total + jnp.sum(
            jnp.exp(logits_ref[start : start + step, :] - top), axis=0, keepdims=True
        )
    stats_ref[0:1, :] = top
    stats_ref[1:2, :] = total
    stats_ref[2:3, :] = hit_total
    stats_ref[3:8, :] = jnp.zeros((5, n_loss), F4)


def join_stats(one, two):
    top = jnp.maximum(one[0], two[0])
    total = one[1] * jnp.exp(one[0] - top) + two[1] * jnp.exp(two[0] - top)
    return top, total, one[2] + two[2]


def probs_kernel(
    sc_ref, stats_ref, weight_ref, target_ref, logits_ref, tables_ref, probs_ref, grad_ref,
    loss_ref,
):
    offset = sc_ref[3]
    vr, n_loss = logits_ref.shape
    parts = [tuple(stats_ref[k, i : i + 1, :] for i in range(3)) for k in range(stats_ref.shape[0])]
    while len(parts) > 1:
        parts = [join_stats(parts[i], parts[i + 1]) for i in range(0, len(parts), 2)]
    top, total, hit = parts[0]
    log_all = top + jnp.log(total)
    weight = weight_ref[...]
    loss_ref[0, 0] = jnp.sum(weight * (log_all - hit))
    share = weight / jnp.sum(weight)
    target = target_ref[...] - offset
    grads = jnp.zeros((n_loss, D), F4)
    for start, size, table in runs_of(tables_ref):
        place = lax.broadcasted_iota(jnp.int32, (size, n_loss), 0) + start
        probs = jnp.exp(logits_ref[start : start + size, :] - log_all)
        probs = (jnp.where(place == target, probs - 1.0, probs) * share).astype(BF)
        probs_ref[start : start + size, :] = probs
        grads = grads + tn(probs, table)
    for r in range(BLOCKS):
        grad_ref[r] = grads[:, LANES * r : LANES * (r + 1)]


def squares_kernel(probs_ref, picked_ref, out_ref):
    vr = probs_ref.shape[0]
    tile = tile_of(vr)
    total = jnp.zeros((), F4)
    for start in range(0, vr, tile):
        grads = nn(probs_ref[start : start + tile, :], picked_ref[...])
        total = total + jnp.sum(grads * grads)
    out_ref[0, 0] = total


def layer_pull(
    k, seqs, rows_seq, sc_ref, grad_stream, stream, vec_ref, att_ref, ff_ref, copy, own_ref, other_ref, q_ref,
    log_ref, keys_ref, row_ref, dq_ref, dkv_ref, wide_ref, out_ref, vec_out,
    feed_scr, low_scr, grad_scr, prod_scr, square,
):
    parity = sc_ref[1]
    block, place = sc_ref[4], sc_ref[5]
    rows = wide_ref.shape[1]
    cols = FF // BLOCKS
    normal, unused = normal_of(stream)
    feed = (normal * vec_ref[0:1, 2 * D : 3 * D] + vec_ref[0:1, 3 * D : 4 * D]).astype(BF)
    low = grad_stream.astype(BF)
    for r in range(BLOCKS):
        feed_scr[r] = feed[:, LANES * r : LANES * (r + 1)]
        low_scr[r] = low[:, LANES * r : LANES * (r + 1)]
    feed_own = feed_scr[block]
    low_own = low_scr[block]

    at = k * 256 + LANES
    half = D // 2
    start = pl.ds(pl.multiple_of(parity * half, half), half)
    grad_context = nt(low_scr[0], att_ref[0, start, at : at + LANES])
    for r in range(1, BLOCKS):
        grad_context = grad_context + nt(low_scr[r], att_ref[r, start, at : at + LANES])
    grad_context = grad_context.astype(BF).astype(F4)
    grad_scr[0] = grad_context[:, :LANES]
    grad_scr[1] = grad_context[:, LANES:]
    attend_pull(
        q_ref, own_ref, grad_scr, log_ref, keys_ref, row_ref, dq_ref, dkv_ref, seqs,
        rows_seq,
    )

    vec_out[0:1, 5 * D : 6 * D] = jnp.sum(low.astype(F4), axis=0, keepdims=True)
    vec_out[0:1, 6 * D : 7 * D] = jnp.sum(low.astype(F4), axis=0, keepdims=True)
    grad_feed = jnp.zeros_like(grad_stream)
    copy.wait()
    for r in range(BLOCKS):
        at_r = 7 * D + cols * r
        hidden = nn(feed, ff_ref[r, :, :cols]) + vec_ref[0:1, at_r : at_r + cols]
        grown = 1.0 + lax.erf(hidden * ROOT_HALF)
        active = (0.5 * hidden * grown).astype(BF)
        slope = 0.5 * grown + hidden * (ROOT_TAU * jnp.exp(-0.5 * hidden * hidden))
        grad_hidden = (nn(low, ff_ref[r, :, cols:]) * slope).astype(BF)
        grad_feed = grad_feed + nt(grad_hidden, ff_ref[r, :, :cols])
        vec_out[0:1, at_r : at_r + cols] = jnp.sum(
            grad_hidden.astype(F4), axis=0, keepdims=True
        )
        for which, product in enumerate((tn(feed_own, grad_hidden), tn(low_own, active))):
            prod_scr[...] = product
            piece = prod_scr[pl.ds(pl.multiple_of(place, 16), rows), :]
            wide_ref[which, :, cols * r : cols * (r + 1)] = piece
            square = square + jnp.sum(piece * piece)
    blocks = join_blocks(parity, own_ref, other_ref)
    context_own = blocks[0]
    for r in range(1, BLOCKS):
        context_own = jnp.where(block == r, blocks[r], context_own)
    prod_scr[...] = tn(context_own.astype(BF), low)
    piece = prod_scr[pl.ds(pl.multiple_of(place, 16), rows), :]
    out_ref[...] = piece
    square = square + jnp.sum(piece * piece)
    vec_out[0:1, 2 * D : 3 * D] = jnp.sum(grad_feed * normal, axis=0, keepdims=True)
    vec_out[0:1, 3 * D : 4 * D] = jnp.sum(grad_feed, axis=0, keepdims=True)
    return grad_feed, square


def query_pull(
    k, sc_ref, stream, grad_feed, own_ref, other_ref, vec_ref, att_ref, cos_ref, sin_ref, wq_ref,
    head_out, normed_scr, prod_scr, square,
):
    parity = sc_ref[1]
    block, place = sc_ref[4], sc_ref[5]
    rows = wq_ref.shape[0]
    normal, scale = normal_of(stream)
    normed = (normal * vec_ref[0:1, :D] + vec_ref[0:1, D : 2 * D]).astype(BF)
    for r in range(BLOCKS):
        normed_scr[r] = normed[:, LANES * r : LANES * (r + 1)]
    cosine, sine = cos_ref[...], sin_ref[...]
    grad_normed = jnp.zeros_like(stream)
    pieces = []
    for r, part in enumerate(join_blocks(parity, own_ref, other_ref)):
        piece = spin(part.astype(F4), cosine, -sine).astype(BF)
        head_out[0:1, 2 * D + LANES * r : 2 * D + LANES * (r + 1)] = jnp.sum(
            piece.astype(F4), axis=0, keepdims=True
        )
        grad_normed = grad_normed + nt(piece, att_ref[r, :, k * 256 : k * 256 + LANES])
        pieces.append(piece)
    prod_scr[...] = tn(normed_scr[block], jnp.concatenate(pieces, axis=1))
    piece = prod_scr[pl.ds(pl.multiple_of(place, 16), rows), :]
    wq_ref[...] = piece
    square = square + jnp.sum(piece * piece)
    head_out[0:1, :D] = jnp.sum(grad_normed * normal, axis=0, keepdims=True)
    head_out[0:1, D : 2 * D] = jnp.sum(grad_normed, axis=0, keepdims=True)
    shaped_all = grad_normed * vec_ref[0:1, :D] + grad_feed * vec_ref[0:1, 2 * D : 3 * D]
    return norm_pull(shaped_all, normal, scale), square


def last_pull_kernel(
    seqs, rows_seq, sc_ref, before_ref, grads_ref, final_ref, final_stream_ref, stream_ref, vec_ref, w0, w1, w2, w3, w4, w5, w6, w7, w8, w9,
    own_ref, other_ref, q_ref, log_ref, keys_ref, row_ref, dq_ref, dkv_ref,
    wide_ref, out_ref, vec_out, final_out, grad_out, feed_out, square_ref, feed_scr, low_scr,
    grad_scr, prod_scr, att_ref, ff_ref, sems,
):
    att_copy = Fetch(sc_ref, (w0, w1, w2, w3, w4, w5, w6, w7, w8, w9), att_ref, sems.at[0], L * WIDE)
    copy = Fetch(sc_ref, (w0, w1, w2, w3, w4, w5, w6, w7, w8, w9), ff_ref, sems.at[1], WIDE)
    grad_picked = jnp.concatenate([grads_ref[r] for r in range(BLOCKS)], axis=1)
    normal, scale = normal_of(final_stream_ref[...])
    final_out[0:1, :] = jnp.sum(grad_picked * normal, axis=0, keepdims=True)
    final_out[1:2, :] = jnp.sum(grad_picked, axis=0, keepdims=True)
    grad_stream = norm_pull(grad_picked * final_ref[0:1, :], normal, scale)
    grad_out[...] = grad_stream
    dkv_ref[...] = jnp.zeros_like(dkv_ref)
    att_copy.wait()
    grad_feed, square = layer_pull(
        1, seqs, rows_seq, sc_ref, grad_stream, stream_ref[...], vec_ref, att_ref, ff_ref, copy, own_ref,
        other_ref, q_ref, log_ref, keys_ref, row_ref, dq_ref, dkv_ref,
        wide_ref, out_ref, vec_out, feed_scr, low_scr, grad_scr, prod_scr, before_ref[0, 0],
    )
    feed_out[...] = grad_feed
    square_ref[0, 0] = square


def first_pull_kernel(
    seqs, rows_seq, sc_ref, grad_in_ref, feed_in_ref, dq_own_ref, dq_other_ref, stream1_ref, vec1_ref,
    stream_ref, vec_ref, w0, w1, w2, w3, w4, w5, w6, w7, w8, w9, own_ref, other_ref, q_ref, log_ref, keys_ref,
    row_ref, cos_ref, sin_ref, dkv_in_ref, chip_code_ref, dq_ref, own_slots,
    near_slots, wide_ref, out_ref, vec_out, wq_ref, head_out, grad_out, feed_out, square_ref, feed_scr,
    low_scr, grad_scr, prod_scr, dkv_ref, att_ref, ff_ref, sems, dkv_sem,
):
    dkv_copy = pltpu.make_async_copy(dkv_in_ref, dkv_ref, dkv_sem)
    dkv_copy.start()
    att_copy = Fetch(sc_ref, (w0, w1, w2, w3, w4, w5, w6, w7, w8, w9), att_ref, sems.at[0], L * WIDE)
    copy = Fetch(sc_ref, (w0, w1, w2, w3, w4, w5, w6, w7, w8, w9), ff_ref, sems.at[1], 0)
    att_copy.wait()
    grad_part, square = query_pull(
        1, sc_ref, stream1_ref[...], feed_in_ref[...], dq_own_ref, dq_other_ref, vec1_ref, att_ref,
        cos_ref, sin_ref, wq_ref, head_out, feed_scr, prod_scr, jnp.zeros((), F4),
    )
    grad_stream = grad_in_ref[...] + grad_part
    grad_out[...] = grad_stream
    dkv_copy.wait()
    grad_feed, square = layer_pull(
        0, seqs, rows_seq, sc_ref, grad_stream, stream_ref[...], vec_ref, att_ref, ff_ref, copy, own_ref,
        other_ref, q_ref, log_ref, keys_ref, row_ref, dq_ref, dkv_ref,
        wide_ref, out_ref, vec_out, feed_scr, low_scr, grad_scr, prod_scr, square,
    )
    to_slots(dkv_ref, chip_code_ref, own_slots, near_slots, seqs, rows_seq)
    feed_out[...] = grad_feed
    square_ref[0, 0] = square


def embed_pull_kernel(
    sc_ref, grad_in_ref, feed_in_ref, dq_own_ref, dq_other_ref, stream_ref, vec_ref, w0, w1, w2, w3, w4, w5, w6, w7, w8, w9, kv_ref,
    cos_ref, sin_ref, dkv_own_ref, dkv_other_ref, rows_ref, slot_cos_ref, slot_sin_ref,
    slot_ref, row_code_ref, id_row_ref, wq_ref, head_out, rows_out, ids_out,
    kv_out, gain_out, square_ref, count_ref, normed_scr, prod_scr, high_scr, low_scr, att_ref, sem,
):
    Fetch(sc_ref, (w0, w1, w2, w3, w4, w5, w6, w7, w8, w9), att_ref, sem, L * WIDE).wait()
    grad_part, square = query_pull(
        0, sc_ref, stream_ref[...], feed_in_ref[...], dq_own_ref, dq_other_ref, vec_ref, att_ref,
        cos_ref, sin_ref, wq_ref, head_out, normed_scr, prod_scr, jnp.zeros((), F4),
    )
    grad_high, grad_low = split_two(grad_in_ref[...] + grad_part)
    n_slots = rows_ref.shape[1]
    step = 256
    kv_total = jnp.zeros((D, LANES), F4)
    gain_total = jnp.zeros((1, D), F4)
    bias_total = jnp.zeros((1, D), F4)
    pair_total = jnp.zeros((1, LANES), F4)
    gain = vec_ref[0:1, :D]
    for start in range(0, n_slots, step):
        part = pl.ds(start, step)
        real = slot_ref[part, 0:1] < FAR
        grad_pair = dkv_own_ref[part, :] + dkv_other_ref[part, :]
        grad_pair = grad_pair.astype(BF).astype(F4)
        grad_pair = spin(grad_pair, slot_cos_ref[part, :], -slot_sin_ref[part, :])
        grad_pair = jnp.where(real, grad_pair, 0.0).astype(BF)
        rows = jnp.concatenate([rows_ref[r, part, :] for r in range(BLOCKS)], axis=1)
        normal, scale = normal_of(rows.astype(F4))
        normed = (normal * gain + vec_ref[0:1, D : 2 * D]).astype(BF)
        kv_total = kv_total + tn(normed, grad_pair)
        pair_total = pair_total + jnp.sum(grad_pair.astype(F4), axis=0, keepdims=True)
        grad_normed = nt(grad_pair, kv_ref[...])
        gain_total = gain_total + jnp.sum(grad_normed * normal, axis=0, keepdims=True)
        bias_total = bias_total + jnp.sum(grad_normed, axis=0, keepdims=True)
        pick = (slot_ref[part, 0:1] == row_code_ref[...]).astype(F4).astype(BF)
        grad_rows = norm_pull(grad_normed * gain, normal, scale)
        grad_rows = grad_rows + (nn(pick, grad_high) + nn(pick, grad_low))
        grad_rows = jnp.where(real, grad_rows, 0.0)
        high_scr[part, :], low_scr[part, :] = split_two(grad_rows)
    kv_out[...] = kv_total
    gain_out[0:1, :] = gain_total
    gain_out[1:2, :] = bias_total
    gain_out[2:3, :] = jnp.concatenate([pair_total, jnp.zeros((1, D - LANES), F4)], axis=1)
    gain_out[3:8, :] = jnp.zeros((5, D), F4)
    vr = sc_ref[6]
    ids = id_row_ref[...]
    spot = lax.broadcasted_iota(jnp.int32, (1, n_slots), 1)
    later = jnp.zeros((1, n_slots), F4)
    for start in range(0, n_slots, step):
        at = lax.broadcasted_iota(jnp.int32, (step, 1), 0) + start
        same = (slot_ref[pl.ds(start, step), 1:2] == ids) & (at < spot)
        later = jnp.maximum(later, jnp.max(jnp.where(same, 1.0, 0.0), axis=0, keepdims=True))
    lead = jnp.where(ids < vr, 1.0 - later, 0.0)
    rank = jnp.zeros((8, n_slots), F4)
    many = jnp.broadcast_to(lead, (8, n_slots)).astype(BF)
    for start in range(0, n_slots, step):
        before = jnp.where(slot_ref[pl.ds(start, step), 1:2] < ids, 1.0, 0.0).astype(BF)
        rank = rank + nn(many[:, start : start + step], before)
    rank = jnp.where(lead > 0.0, rank[0:1, :].astype(jnp.int32), -1)
    count_ref[0, 0] = jnp.sum(lead).astype(jnp.int32)
    for start in range(0, n_slots, step):
        part = pl.ds(start, step)
        at = lax.broadcasted_iota(jnp.int32, (step, 1), 0) + start
        packed = jnp.max(jnp.where(rank == at, ids, -1), axis=1, keepdims=True)
        ids_out[part, :] = packed
        hot = jnp.where(packed == ids, 1.0, 0.0).astype(BF)
        total = nn(hot, high_scr[...]) + nn(hot, low_scr[...])
        rows_out[part, :] = total.astype(BF)
        square = square + jnp.sum(total * total)
    square_ref[0, 0] = square


TILE = 528
SETTLE = 1056


def params():
    return pltpu.CompilerParams(vmem_limit_bytes=63 * 1024 * 1024)


def base_kernel(first_ref, second_ref, after_ref, step_ref):
    one = BETA_ONE * first_ref[0, 0]
    two = BETA_TWO * second_ref[0, 0]
    step = step_of(one, two)
    for r in range(BLOCKS):
        step_ref[r] = step[:, LANES * r : LANES * (r + 1)].astype(BF)


def base_pass(first, second, after):
    vr = first.shape[2]
    whole = pl.BlockSpec((1, 1, SETTLE, D), lambda i: (0, 0, i, 0))
    return pl.pallas_call(
        base_kernel,
        grid=(pl.cdiv(vr, SETTLE),),
        in_specs=[whole, whole, pl.BlockSpec((16, LANES), lambda i: (0, 0))],
        out_specs=pl.BlockSpec((BLOCKS, SETTLE, LANES), lambda i: (0, i, 0)),
        out_shape=shaped(BLOCKS, vr, LANES, kind=BF),
        compiler_params=params(),
        name="embedding_base",
        cost_estimate=takes(14),
    )(first, second, after)


def unembed_kernel(clip_ref, probs_ref, picked_ref, first_ref, second_ref, *refs):
    one_ref, two_ref, step_ref = refs[-3:]
    gradient = nn(probs_ref[...], picked_ref[...]) * clip_ref[0]
    one, two, step = moments_fast(gradient, first_ref[0, 0], second_ref[0, 0])
    one_ref[0, 0] = one
    two_ref[0, 0] = two
    for r in range(BLOCKS):
        step_ref[r] = step[:, LANES * r : LANES * (r + 1)].astype(BF)


def unembed_pass(clip, probs, picked, first, second, held, start, count):
    vr, n_loss = probs.shape
    rows = min(vr, (start + count) * TILE) - start * TILE
    whole = pl.BlockSpec((1, 1, TILE, D), lambda i: (0, 1, i + start, 0))
    return pl.pallas_call(
        unembed_kernel,
        grid=(count,),
        in_specs=[
            SM,
            pl.BlockSpec((TILE, n_loss), lambda i: (i + start, 0)),
            pl.BlockSpec((n_loss, D), lambda i: (0, 0)),
            whole,
            whole,
        ]
        + [ANY] * len(held),
        out_specs=[whole, whole, pl.BlockSpec((BLOCKS, TILE, LANES), lambda i: (0, i, 0))],
        out_shape=[shaped(*first.shape)] * 2 + [shaped(BLOCKS, rows, LANES, kind=BF)],
        input_output_aliases={5 + i: i for i in range(len(held))},
        compiler_params=params(),
        name="unembedding_adam",
        cost_estimate=takes(16),
    )(clip, probs, picked, first, second, *held)


GROUP = 128


def overlapping(id_at, count, first, tile, step):
    def one(i, carry):
        least = id_at(i * GROUP)
        most = id_at(jnp.minimum(i * GROUP + GROUP, count) - 1)

        @pl.when((least < first + tile) & (most >= first))
        def _():
            step(i, pl.ds(pl.multiple_of(i * GROUP, GROUP), GROUP))

        return carry

    lax.fori_loop(0, lax.div(count + GROUP - 1, GROUP), one, 0)


def embed_kernel(
    start, last, clip_ref, count_ref, at_ref, id_ref, col_ref, rows_ref, first_ref, second_ref, base_ref,
    *refs,
):
    one_ref, two_ref, extra_out, scr, extra_scr, extra_ref = refs[-6:]
    tile = one_ref.shape[2]
    first = (pl.program_id(0) + start) * tile
    place = lax.broadcasted_iota(jnp.int32, (tile, 1), 0) + first
    row = lax.broadcasted_iota(jnp.int32, (1, tile), 1) + first

    @pl.when(pl.program_id(0) == 0)
    def _():
        extra_ref[...] = jnp.zeros_like(extra_ref)

    scr[...] = jnp.zeros_like(scr)

    def gather(i, part):
        hot = jnp.where(place == id_ref[i], 1.0, 0.0).astype(BF)
        scr[...] += nn(hot, rows_ref[part, :])

    overlapping(lambda k: at_ref[k], count_ref[0], first, tile, gather)
    one, two, step = moments_fast(scr[...] * clip_ref[0], first_ref[0, 0], second_ref[0, 0])
    one_ref[0, 0] = one
    two_ref[0, 0] = two
    base = jnp.concatenate([base_ref[r] for r in range(BLOCKS)], axis=1).astype(F4)
    extra_scr[...] = jnp.where(place < last, step - base, 0.0).astype(BF)

    def scatter(i, part):
        hot = jnp.where(row == col_ref[part, :], 1.0, 0.0).astype(BF)
        picked = nn(hot, extra_scr[...])
        for r in range(BLOCKS):
            extra_ref[r, part, :] += picked[:, LANES * r : LANES * (r + 1)]

    overlapping(lambda k: at_ref[k], count_ref[0], first, tile, scatter)

    @pl.when(pl.program_id(0) == pl.num_programs(0) - 1)
    def _():
        extra_out[...] = extra_ref[...].astype(BF)


def embed_pass(clip, count, ids, rows, first, second, base, held, after, start, tiles):
    n_slots = rows.shape[0]
    vr = first.shape[2]
    whole = pl.BlockSpec((1, 1, TILE, D), lambda i: (0, 0, i + start, 0))
    blocks = pl.BlockSpec((BLOCKS, n_slots, LANES), lambda i: (0, 0, 0))
    groups = n_slots // GROUP
    return pl.pallas_call(
        partial(embed_kernel, start, vr),
        grid=(tiles,),
        in_specs=[
            SM,
            SM,
            SM,
            pl.BlockSpec((groups, 1, GROUP), lambda i: (0, 0, 0)),
            pl.BlockSpec((n_slots, 1), lambda i: (0, 0)),
            pl.BlockSpec((n_slots, D), lambda i: (0, 0)),
            whole,
            whole,
            pl.BlockSpec((BLOCKS, TILE, LANES), lambda i: (0, i + start, 0)),
        ]
        + [ANY] * 3,
        out_specs=[whole, whole, blocks],
        out_shape=[shaped(*first.shape)] * 2 + [shaped(BLOCKS, n_slots, LANES, kind=BF)],
        input_output_aliases={9: 0, 10: 1},
        scratch_shapes=[
            pltpu.VMEM((TILE, D), F4),
            pltpu.VMEM((TILE, D), BF),
            pltpu.VMEM((BLOCKS, n_slots, LANES), F4),
        ],
        compiler_params=params(),
        name="embedding_adam",
        cost_estimate=takes(17),
    )(clip, count, ids.reshape(-1), ids.reshape(groups, 1, GROUP), ids, rows, first, second, base, *held, after)


def layers_kernel(
    clip_ref, after_ref, wq0, out0, wq1, out1, wide0, wide1, kv_ref, a1, a2, f1, f2, k1, k2, oa1, oa2, of1, of2,
    ok1, ok2, step_ref,
):
    clip = clip_ref[0]
    rows = wq0.shape[0]
    for k, grads in enumerate(((wq0, out0), (wq1, out1))):
        for i in range(2):
            one, two, step = moments_fast(grads[i][...] * clip, a1[0, k, i], a2[0, k, i])
            oa1[0, k, i] = one
            oa2[0, k, i] = two
            at = (2 * k + i) * rows
            for r in range(BLOCKS):
                step_ref[r, at : at + rows, :] = step[:, LANES * r : LANES * (r + 1)].astype(BF)
    cols = FF // BLOCKS // LANES
    for k, grads in enumerate((wide0, wide1)):
        for i in range(2):
            one, two, step = moments_fast(grads[i] * clip, f1[0, k, i], f2[0, k, i])
            of1[0, k, i] = one
            of2[0, k, i] = two
            for r in range(BLOCKS):
                for q in range(cols):
                    at = (2 * L + (2 * k + i) * cols + q) * rows
                    lane = LANES * (r * cols + q)
                    step_ref[r, at : at + rows, :] = step[:, lane : lane + LANES].astype(BF)
    one, two, step = moments_fast(kv_ref[...] * clip, k1[0], k2[0])
    ok1[0] = one
    ok2[0] = two
    at = (2 * L + 2 * L * cols) * rows
    for r in range(BLOCKS):
        moved = step if r == 0 else pltpu.roll(step, LANES - r * (LANES // BLOCKS), 1)
        step_ref[r, at : at + rows, :] = moved.astype(BF)


def settle(total, master, outer, rate, reps):
    mean_diff = rate * (total * (1.0 / reps) + DECAY * master)
    momentum = OUTER_MOMENTUM * outer + mean_diff
    return master - OUTER_RATE * (mean_diff + OUTER_MOMENTUM * momentum), momentum


def embed_settle_kernel(
    reps, rate, count_ref, at_ref, id_ref, extra_ref, base_ref, master_ref, outer_ref, *refs
):
    new_ref, mom_ref, scr = refs[-3:]
    tile = base_ref.shape[0]
    first = pl.program_id(0) * tile
    place = lax.broadcasted_iota(jnp.int32, (tile, 1), 0) + first
    scr[...] = base_ref[...].astype(F4)
    for g in range(reps):

        def add(i, part, g=g):
            hot = jnp.where(place == id_ref[g, i], 1.0, 0.0).astype(BF)
            scr[...] += nn(hot, extra_ref[g, part, :])

        overlapping(lambda k, g=g: at_ref[g, k], count_ref[g], first, tile, add)
    new_ref[0], mom_ref[0] = settle(scr[...], master_ref[0], outer_ref[0], rate, reps)


def embed_settle(reps, counts, ids, extra, base, master, outer, held):
    vr = base.shape[0]
    slots = extra.shape[1]
    whole = pl.BlockSpec((1, SETTLE, LANES), lambda i: (0, i, 0))
    return pl.pallas_call(
        partial(embed_settle_kernel, reps, LEARN_RATES[0]),
        grid=(pl.cdiv(vr, SETTLE),),
        in_specs=[
            SM,
            SM,
            pl.BlockSpec((reps, slots // GROUP, 1, GROUP), lambda i: (0, 0, 0, 0)),
            pl.BlockSpec((reps, slots, LANES), lambda i: (0, 0, 0)),
            pl.BlockSpec((SETTLE, LANES), lambda i: (i, 0)),
            whole,
            whole,
        ]
        + [ANY] * len(held),
        out_specs=[whole, whole],
        out_shape=[shaped(*master.shape)] * 2,
        input_output_aliases={7 + i: i for i in range(len(held))},
        scratch_shapes=[pltpu.VMEM((SETTLE, LANES), F4)],
        compiler_params=params(),
        name="embedding_settle",
        cost_estimate=takes(13),
    )(counts, ids.reshape(reps, -1), ids, extra, base, master, outer, *held)


def unembed_settle_kernel(reps, rate, sum_ref, master_ref, outer_ref, held_one, held_two, *refs):
    new_ref, mom_ref = refs
    new_ref[0], mom_ref[0] = settle(
        sum_ref[...].astype(F4), master_ref[0], outer_ref[0], rate, reps
    )


def unembed_settle(reps, total, master, outer, held):
    whole = pl.BlockSpec((1, SETTLE, LANES), lambda i: (1, i, 0))
    return pl.pallas_call(
        partial(unembed_settle_kernel, reps, LEARN_RATES[0]),
        grid=(pl.cdiv(total.shape[0], SETTLE),),
        in_specs=[pl.BlockSpec((SETTLE, LANES), lambda i: (i, 0)), whole, whole, ANY, ANY],
        out_specs=[whole, whole],
        out_shape=[shaped(*master.shape)] * 2,
        input_output_aliases={3: 0, 4: 1},
        compiler_params=params(),
        name="unembedding_settle",
        cost_estimate=takes(5),
    )(total, master, outer, *held)


def body(
    token_ids,
    prompt_mask,
    loss_pos,
    tables,
    attention,
    feedforward,
    key_value,
    gains_biases,
    first_tables,
    first_attention,
    first_feedforward,
    first_key_value,
    first_gains,
    second_tables,
    second_attention,
    second_feedforward,
    second_key_value,
    second_gains,
    outer_tables,
    outer_attention,
    outer_feedforward,
    outer_key_value,
    outer_gains,
):
    width = lax.axis_size(WIDE_AXES)
    reps = lax.axis_size("rep")
    w = lax.axis_index(WIDE_AXES)
    rep = lax.axis_index("rep")
    seqs = token_ids.shape[3]
    rows_seq = LEN // width
    block = seqs * rows_seq
    cap = 2 * block // width
    vr = tables.shape[1]
    lrows = loss_pos.shape[4]
    n_micro = width * lrows
    n_loss = MICRO * n_micro
    span = width * cap
    n_slots = MICRO * span
    own_rows = D // width
    parity = w % 2

    def over_wide(value, k):
        return lax.ppermute(value, WIDE_AXES, [(i, i ^ k) for i in range(width)])

    def over_rep(value, k):
        return lax.ppermute(value, "rep", [(i, i ^ k) for i in range(reps)])

    def sum_wide(value, kind, beside=()):
        half = value.shape[0] // 2
        keep = lax.dynamic_slice_in_dim(value, parity * half, half)
        give = lax.dynamic_slice_in_dim(value, (1 - parity) * half, half)
        mine = (keep + over_wide(give, 1)).astype(kind)
        parts = [mine] + [over_wide(mine, k) for k in range(2, width, 2)]
        parts, *beside = lax.optimization_barrier((parts, *beside))
        parts = [part.astype(F4) for part in parts]
        while len(parts) > 1:
            parts = [parts[i] + parts[i + 1] for i in range(0, len(parts), 2)]
        total = parts[0].astype(value.dtype)
        other = over_wide(total, 1)
        joined = jnp.concatenate(
            [jnp.where(parity == 0, total, other), jnp.where(parity == 0, other, total)]
        )
        return (joined, *beside) if beside else joined

    scalars = jnp.stack(
        [
            w,
            parity,
            rep,
            w * vr,
            w * own_rows // LANES,
            w * own_rows % LANES,
            jnp.asarray(vr, jnp.int32),
            jnp.zeros((), jnp.int32),
        ]
    ).astype(jnp.int32)

    pack = jnp.concatenate(
        [feedforward[k, i] for k in range(L) for i in range(2)]
        + [attention[k, i] for k in range(L) for i in range(2)],
        axis=1,
    ).astype(BF)

    own_table = tables[1].astype(BF)

    n_mb = MICRO * width

    def by_block(array):
        array = array.reshape(MICRO, seqs, width, rows_seq).transpose(0, 2, 1, 3)
        return array.reshape(n_mb, block).astype(F4)

    tokens = by_block(token_ids)
    flat = jnp.concatenate([gains_biases, key_value.reshape(-1)])
    n_flat = flat.shape[0]
    n_small = gains_biases.shape[0]
    flat = jnp.pad(flat, (0, -n_flat % (8 * block))).reshape(-1, block)
    message = jnp.concatenate([tokens, flat])
    message, pack = lax.optimization_barrier((message, pack))
    pack_near = [over_wide(pack, k) for k in range(2, width, 2)]
    everyone = [message] + [over_rep(message, k) for k in range(1, reps)]
    lines = n_slots // LANES
    slot_ids, slot_codes, slot_rows, rest = call(
        partial(slots_kernel, seqs, rows_seq, vr, cap),
        [shaped(reps, lines, LANES, kind=jnp.int32)]
        + [shaped(lines, LANES, kind=jnp.int32)] * 2
        + [shaped(reps, *flat.shape)],
        (scalars, *everyone),
        scratch=[pltpu.VMEM((reps, *message.shape), F4)],
        smem=1,
        cost=7, name="slots",
    )
    (mine_w,) = call(
        stack_kernel,
        [shaped(width // 2, *pack.shape, kind=BF)],
        (pack, *pack_near),
        cost=2, name="stack_weights",
    )
    half_w = mine_w.shape[0] // 2
    x_w, y_w = over_rep(mine_w, 1), over_rep(mine_w, 2)
    slot_ids, mine_w = lax.optimization_barrier((slot_ids, mine_w))
    asked = [None] * reps
    for k in range(reps - 1, -1, -1):
        asked[k] = tables[0].at[slot_ids[k].reshape(-1)].get(mode="promise_in_bounds").astype(BF)
    rows = [asked[0]] + [over_rep(asked[k], k) for k in range(1, reps)]
    own_codes, own_ids = slot_codes.reshape(-1), slot_rows.reshape(-1)

    rest = rest.reshape(reps, -1)
    vectors, pair_bias, final_gain, final_bias = unpack_small(rest[:, :n_small].reshape(-1))
    final_rows = jnp.stack([final_gain, final_bias])
    vec = [vectors[k][None, :] for k in range(L)]
    kv_near = rest[:, n_small:n_flat].reshape(reps, own_rows, -1).transpose(1, 0, 2)
    kv_near = kv_near.reshape(own_rows, LANES).astype(BF)
    kv_near = [kv_near] + [over_wide(kv_near, k) for k in range(2, width, 2)]
    kv_near = [part for piece in kv_near for part in (piece, over_wide(piece, 1))]

    codes = loss_pos.reshape(n_mb, lrows)
    blocks = jnp.arange(n_mb, dtype=jnp.int32)[:, None]
    row_code = (
        blocks // width * (seqs * LEN)
        + codes // (rows_seq - 1) * LEN
        + blocks % width * rows_seq
        + codes % (rows_seq - 1)
    ).reshape(1, n_loss)
    frequency = 10000.0 ** (-2.0 * jnp.arange(ROT // 2, dtype=F4) / ROT)
    angles = jnp.concatenate([own_codes, row_code[0]]) % LEN
    angles = angles.astype(F4)[None, :] * frequency[:, None]
    turns = jnp.concatenate([jnp.cos(angles), jnp.sin(angles)])
    int_of = partial(shaped, kind=jnp.int32)
    (
        key_codes, chip_codes, slot_cols, row_cols, target_row, weight, slot_cos, slot_sin, row_cos,
        row_sin,
    ) = call(
        partial(places_kernel, seqs, rows_seq, vr, cap),
        [
            int_of(n_mb, 1, span), int_of(n_mb, 1, 2 * cap), int_of(n_slots, 2), int_of(n_loss, 2),
            int_of(1, n_loss), shaped(1, n_loss), shaped(n_slots, LANES), shaped(n_slots, LANES),
            shaped(n_loss, LANES), shaped(n_loss, LANES),
        ],
        (
            scalars, tokens, by_block(prompt_mask), loss_pos.reshape(-1, LANES), slot_codes, slot_rows,
            row_code, turns,
        ),
        smem=1,
        cost=4, name="places",
    )
    count = jnp.sum(weight)

    rows, x_w, y_w, kv_near, own_table = lax.optimization_barrier(
        (rows, x_w, y_w, kv_near, own_table)
    )

    unembed = lax.all_gather(own_table, "rep")
    d_w = [over_rep(x_w[:half_w], 2), over_rep(y_w[half_w:], 1)]
    pairs, stream, kv_low, rows = call(
        kv_kernel,
        [shaped(n_slots, LANES, kind=BF), shaped(BLOCKS, n_loss, LANES, kind=BF), shaped(D, LANES, kind=BF), shaped(reps, n_slots, LANES, kind=BF)],
        (
            scalars, *rows, slot_cos, slot_sin, vec[0], pair_bias[None, :], own_codes[None, :],
            row_cols, *kv_near,
        ),
        smem=1,
        cost=2, name="keys_values",
    )
    keep = lax.dynamic_slice_in_dim(stream, 2 * parity, 2)
    give = lax.dynamic_slice_in_dim(stream, 2 * (1 - parity), 2)
    keep = (keep + over_wide(give, 1)).reshape(2 * n_loss, LANES)
    near = jnp.concatenate([pairs, keep])
    near = [near] + [over_wide(near, k) for k in range(2, width, 2)]
    base_step = base_pass(first_tables, second_tables, pairs)
    near, base_step, d_w = lax.optimization_barrier((near, base_step, d_w))
    pieces = []
    for piece in near:
        pieces += [piece, over_wide(piece, 1)]
    weights = [mine_w, x_w, y_w, *d_w]
    weights = weights + [over_wide(part, 1) for part in weights]


    keys, stream = call(
        partial(order_kernel, seqs, rows_seq, width, cap),
        [shaped(MICRO * width, block, LANES, kind=BF), shaped(BLOCKS, n_loss, LANES)],
        (scalars, base_step, key_codes, *pieces),
        smem=1,
        far=(1,),
        cost=5, name="token_order",
    )
    weights = [mine_w, x_w, y_w, *d_w]
    weights = weights + [over_wide(part, 1) for part in weights]

    tiles = width // SPREAD
    keys = keys.reshape(MICRO, tiles, SPREAD * block, LANES)

    codes = (row_cols,)
    halves = shaped(2, n_loss, LANES)
    att_room = [pltpu.VMEM((reps, D, ATT), BF), pltpu.SemaphoreType.DMA((2, 4, width // 2))]
    ff_room = [pltpu.VMEM((reps, D, WIDE), BF), pltpu.SemaphoreType.DMA((2, 4, width // 2))]
    both_room = [att_room[0], ff_room[0], pltpu.SemaphoreType.DMA((2, 2, 4, width // 2))]
    stacked = ROWS * HEADS // 2
    logs = shaped(n_loss // ROWS, stacked, 1)
    scores = pltpu.VMEM((tiles, stacked, SPREAD * block), F4)
    whole = shaped(n_loss, D)

    def other_half(value):
        return over_wide(value.astype(BF), 1)

    stream0, q0, ctx0, log0 = call(
        partial(first_kernel, seqs, rows_seq),
        [whole, halves, halves, logs],
        (scalars, stream, vec[0], *weights, keys, *codes, row_cos, row_sin),
        smem=1,
        scratch=[scores] + att_room,
        far=range(3, 13),
        cost=9, name="first_attention",
    )
    far0 = other_half(ctx0)
    (partial0,) = call(partial(feed_kernel, 0), [whole], (scalars, stream0, vec[0], *weights), smem=1, scratch=ff_room, far=range(3, 13), name="first_feed")
    partial0, unembed = lax.optimization_barrier((partial0, unembed))
    stream1, q1, ctx1, log1 = call(
        partial(second_kernel, seqs, rows_seq),
        [whole, halves, halves, logs],
        (scalars, partial0, ctx0, far0, vec[1], *weights, keys, *codes, row_cos, row_sin),
        smem=1,
        scratch=[scores] + att_room,
        far=range(5, 15),
        cost=9, name="second_attention",
    )
    far1 = other_half(ctx1)

    (partial1,) = call(partial(feed_kernel, 1), [whole], (scalars, stream1, vec[1], *weights), smem=1, scratch=ff_room, far=range(3, 13), name="second_feed")
    logits, stats, stream2, picked = call(
        logits_kernel,
        [shaped(vr, n_loss), shaped(8, n_loss), whole, shaped(n_loss, D, kind=BF)],
        (scalars, partial1, ctx1, far1, *weights, final_rows, target_row, unembed),
        smem=1,
        scratch=att_room,
        far=range(4, 14),
        cost=10, name="logits",
    )
    near = [stats] + [over_wide(stats, k) for k in range(2, width, 2)]
    stats = jnp.stack([part for piece in near for part in (piece, over_wide(piece, 1))])
    probs, grad_picked, loss_sum = call(
        probs_kernel,
        [shaped(vr, n_loss, kind=BF), shaped(BLOCKS, n_loss, LANES), shaped(1, 1)],
        (scalars, stats, weight, target_row, logits, unembed),
        smem=1,
        out_specs=[VM, VM, SM],
        cost=9, name="loss_gradient",
    )
    base_step, grad_picked = lax.optimization_barrier((base_step, grad_picked))
    base_sum = lax.psum_scatter(base_step, "rep", scatter_dimension=0, tiled=True)[0]

    (unembed_square,) = call(
        squares_kernel, [shaped(1, 1)], (probs, picked), out_specs=[SM], cost=3, name="squares"
    )
    grad_picked, unembed_square = sum_wide(grad_picked, BF, (unembed_square,))

    wide_shape = shaped(2, own_rows, FF)
    out_shape = shaped(own_rows, D)
    vec_shape = shaped(1, 7 * D + FF)
    head_shape = shaped(1, 3 * D)
    dq_shape = shaped(2, n_loss, LANES, kind=BF)
    dkv_shape = shaped(MICRO, tiles, SPREAD * block, LANES)
    slots_shape = shaped(n_slots, LANES)
    pull_scratch = [
        pltpu.VMEM((BLOCKS, n_loss, LANES), BF),
        pltpu.VMEM((BLOCKS, n_loss, LANES), BF),
        pltpu.VMEM((2, n_loss, LANES), F4),
        pltpu.VMEM((LANES, D), F4),
    ]
    dq1, dkv, wide1, out1, vec1, final_grad, grad_stream, grad_feed, square1 = call(
        partial(last_pull_kernel, seqs, rows_seq),
        [
            dq_shape, dkv_shape, wide_shape, out_shape, vec_shape, shaped(2, D), whole, whole,
            shaped(1, 1),
        ],
        (
            scalars, unembed_square, grad_picked, final_rows, stream2, stream1, vec[1], *weights, ctx1,
            far1, q1, log1, keys, *codes,
        ),
        smem=2,
        out_specs=[VM] * 8 + [SM],
        scratch=pull_scratch + both_room,
        far=range(7, 17),
        cost=16, name="second_pull",
    )
    far_dq1 = over_wide(dq1, 1)
    dq0, own_dkv, near_dkv, wide0, out0, vec0, wq1, head1, grad_stream, grad_feed, square0 = call(
        partial(first_pull_kernel, seqs, rows_seq),
        [
            dq_shape, slots_shape, slots_shape, wide_shape, out_shape, vec_shape, out_shape,
            head_shape, whole, whole, shaped(1, 1),
        ],
        (
            scalars, grad_stream, grad_feed, dq1, far_dq1, stream1, vec[1], stream0, vec[0],
            *weights, ctx0, far0, q0, log0, keys, *codes, row_cos, row_sin, dkv,
            chip_codes,
        ),
        smem=1,
        out_specs=[VM] * 10 + [SM],
        scratch=pull_scratch
        + [pltpu.VMEM(dkv_shape.shape, F4)]
        + both_room
        + [pltpu.SemaphoreType.DMA],
        far=[*range(9, 19), 27],
        cost=23, name="first_pull",
    )
    far_dq0 = over_wide(dq0, 1)
    far_dkv = over_wide(near_dkv, 1)
    wq0, head0, grad_rows, row_ids, kv_part, gain_part, square_rows, row_count = call(
        embed_pull_kernel,
        [
            out_shape, head_shape, shaped(n_slots, D, kind=BF), shaped(n_slots, 1, kind=jnp.int32),
            shaped(D, LANES), shaped(8, D), shaped(1, 1), shaped(1, 1, kind=jnp.int32),
        ],
        (
            scalars, grad_stream, grad_feed, dq0, far_dq0, stream0, vec[0], *weights, kv_low, row_cos,
            row_sin, own_dkv, far_dkv, rows, slot_cos, slot_sin,
            slot_cols, row_code, own_ids[None, :],
        ),
        smem=1,
        out_specs=[VM] * 6 + [SM, SM],
        scratch=[
            pltpu.VMEM((BLOCKS, n_loss, LANES), BF),
            pltpu.VMEM((LANES, D), F4),
            pltpu.VMEM((n_slots, D), BF),
            pltpu.VMEM((n_slots, D), BF),
        ]
        + att_room,
        far=range(7, 17),
        cost=12, name="embedding_pull",
    )

    square = (square0 + square1 + square_rows)[0, 0]
    message = jnp.concatenate(
        [kv_part, gain_part.reshape(-1, LANES), jnp.full((16, LANES), square, F4)]
    )
    message, base_sum = sum_wide(message, F4, (base_sum,))
    kv_total = message[:D]
    gain_total = message[D : D + 8 * BLOCKS].reshape(8, D)
    square = message[D + 8 * BLOCKS, 0]

    def vector_grad(head, vec_part):
        return [head[0, : 2 * D], vec_part[0, 2 * D : 4 * D], head[0, 2 * D :], vec_part[0, 5 * D :]]

    grad_small = jnp.concatenate(
        [head0[0, : 2 * D] + gain_total[:2].reshape(-1)]
        + vector_grad(head0, vec0)[1:]
        + vector_grad(head1, vec1)
        + [gain_total[2, :LANES], final_grad.reshape(-1)]
    )
    square = square + jnp.sum(kv_total * kv_total) + jnp.sum(grad_small * grad_small)
    clip_factor = jnp.minimum(1.0, CLIP / (jnp.sqrt(square) + 1e-06))

    clip = clip_factor.reshape(1)

    n_tiles = pl.cdiv(vr, TILE)
    size = n_tiles
    pieces = pl.cdiv(n_tiles, size)
    bounds = [min(size * i, n_tiles) for i in range(pieces + 1)]
    held = []
    terms = []

    for i in range(pieces):
        *held, step = unembed_pass(
            clip, probs, picked, first_tables, second_tables, held, bounds[i],
            bounds[i + 1] - bounds[i],
        )
        terms.append(lax.psum_scatter(step, "rep", scatter_dimension=0, tiled=True)[0])

    kv_grad = lax.dynamic_slice_in_dim(kv_total, w * own_rows, own_rows, axis=0)
    sm_one, sm_two, sm_step = moments_step(
        grad_small * clip_factor, first_gains[0], second_gains[0]
    )
    pack_rows = own_rows * (2 * L + 2 * L * (FF // BLOCKS // LANES) + 1)
    att_one, att_two, ff_one, ff_two, kv_one, kv_two, packed = call(
        layers_kernel,
        [shaped(*first_attention.shape)] * 2
        + [shaped(*first_feedforward.shape)] * 2
        + [shaped(*first_key_value.shape)] * 2
        + [shaped(BLOCKS, pack_rows, LANES, kind=BF)],
        (
            clip, step, wq0, out0, wq1, out1, wide0, wide1, kv_grad, first_attention, second_attention,
            first_feedforward, second_feedforward, first_key_value, second_key_value,
        ),
        smem=1,
        far=(1,),
        cost=8, name="layers_adam",
    )
    n_small = sm_step.shape[0] // reps
    sm_step = jnp.pad(sm_step.astype(BF).reshape(reps, n_small), ((0, 0), (0, -n_small % 2048)))
    packed = jnp.concatenate([packed, sm_step.reshape(reps, -1, LANES)], axis=1)
    steps = packed
    packed = lax.all_to_all(packed, "rep", 0, 0, tiled=True)
    packed = jnp.sum(packed.astype(F4), axis=0)

    e_tiles = pl.cdiv(vr, TILE)
    e_pieces = 1
    e_bounds = [e_tiles * i // e_pieces for i in range(e_pieces + 1)]
    for i in range(e_pieces):
        *held, extra = embed_pass(
            clip, row_count.reshape(1), row_ids, grad_rows, first_tables, second_tables, base_step, held,
            steps, e_bounds[i], e_bounds[i + 1] - e_bounds[i],
        )
    one_tables, two_tables = held
    coded = jnp.concatenate([(row_ids + LANES) // LANES, (row_ids + LANES) % LANES])
    coded = jnp.broadcast_to(coded.astype(BF).reshape(1, -1, LANES), (reps, n_slots // 64, LANES))
    extra = jnp.concatenate([extra.astype(BF), coded], axis=1)
    extra = lax.all_to_all(extra, "rep", 0, 0, tiled=True)
    coded = extra[:, n_slots:].reshape(reps, 2, n_slots).astype(jnp.int32)
    coded = coded[:, 0] * LANES + coded[:, 1] - LANES
    counts = jnp.sum((coded >= 0).astype(jnp.int32), axis=1)

    new_tables = embed_settle(
        reps, counts, coded.reshape(reps, n_slots // GROUP, 1, GROUP), extra, base_sum, tables,
        outer_tables, (),
    )
    new_tables = unembed_settle(reps, terms[0], tables, outer_tables, new_tables)

    cols = FF // BLOCKS // LANES
    at_ff = 2 * L * own_rows
    at_kv = at_ff + 2 * L * cols * own_rows
    masters = (attention, feedforward, key_value, gains_biases)
    outers = (outer_attention, outer_feedforward, outer_key_value, outer_gains)
    sums = (
        packed[:at_ff].reshape(L, 2, own_rows, LANES),
        packed[at_ff:at_kv]
        .reshape(L, 2, cols, own_rows, LANES)
        .transpose(0, 1, 3, 2, 4)
        .reshape(feedforward.shape),
        packed[at_kv : at_kv + own_rows, : LANES // BLOCKS],
        packed[pack_rows:].reshape(-1)[:n_small],
    )
    stepped = [new_tables] + [
        settle(sums[i], masters[i], outers[i], LEARN_RATES[i + 1], reps) for i in range(4)
    ]
    return (
        loss_sum.reshape(1),
        count.reshape(1),
        *[pair[0] for pair in stepped],
        one_tables,
        att_one,
        ff_one,
        kv_one,
        sm_one[None],
        two_tables,
        att_two,
        ff_two,
        kv_two,
        sm_two[None],
        *[pair[1] for pair in stepped],
    )


def solution(mesh):
    split = (
        P(None, WIDE_AXES, "rep"),
        P(None, None, WIDE_AXES, "rep"),
        P(None, None, WIDE_AXES, "rep"),
        P(WIDE_AXES, "rep"),
        P("rep"),
    )
    moments = (
        P("rep", None, WIDE_AXES, None),
        P("rep", None, None, WIDE_AXES, None),
        P("rep", None, None, WIDE_AXES, None),
        P("rep", WIDE_AXES, None),
        P("rep", None),
    )
    tokens = P("rep", None, None, None, None)
    parted = mesh.devices.reshape(mesh.shape["rep"], mesh.shape["wide"] // 2, 2)
    return jax.shard_map(
        body,
        mesh=Mesh(parted, ("rep",) + WIDE_AXES),
        in_specs=(tokens,) * 3 + split + moments + moments + split,
        out_specs=(P("rep"), P("rep")) + split + moments + moments + split,
        check_vma=False,
    )
```
